32 devices in a mesh: fsdp: 8 (over z, x), seq: 4 (over y, core).
Axes of the slice: x: 2, y: 2, z: 4, core: 2. Of those that a mesh axis runs over, the one named last changes fastest.
Arguments:
- tokens: bfloat16 [8, 1024, 1024], P('fsdp', 'seq'), may hold values from -6 to 6, as said below
- lengths: int32 [8], P('fsdp'), may hold values from 769 to 1024, as said below
- cotangent: bfloat16 [8, 1024, 1024], P('fsdp', 'seq'), may hold values from -6 to 6
- ln1_gain: bfloat16 [2, 1024], P(None, 'fsdp'), may hold values from 0.099609375 to 1.8984375
- ln1_bias: bfloat16 [2, 1024], P(None, 'fsdp'), may hold values from -1.75 to 1.75
- qkv_weight: bfloat16 [2, 1024, 3072], P(None, 'fsdp'), may hold values from -0.1875 to 0.1875
- query_bias: bfloat16 [2, 1024], P(None, 'fsdp'), may hold values from -3 to 3
- value_bias: bfloat16 [2, 1024], P(None, 'fsdp'), may hold values from -3 to 3
- out_weight: bfloat16 [2, 1024, 1024], P(None, 'fsdp'), may hold values from -0.375 to 0.375
- out_bias: bfloat16 [2, 1024], P(None, 'fsdp'), may hold values from -1.75 to 1.75
- ln2_gain: bfloat16 [2, 1024], P(None, 'fsdp'), may hold values from 0.099609375 to 1.8984375
- ln2_bias: bfloat16 [2, 1024], P(None, 'fsdp'), may hold values from -1.75 to 1.75
- up_weight: bfloat16 [2, 1024, 4096], P(None, 'fsdp'), may hold values from -0.1875 to 0.1875
- up_bias: bfloat16 [2, 4096], P(None, 'fsdp'), may hold values from -3 to 3
- down_weight: bfloat16 [2, 4096, 1024], P(None, 'fsdp'), may hold values from -0.09375 to 0.09375
- down_bias: bfloat16 [2, 1024], P(None, 'fsdp'), may hold values from -1.75 to 1.75
Outputs:
- output: bfloat16 [8, 1024, 1024], P('fsdp', 'seq')
- input_grad: float32 [8, 1024, 1024], P('fsdp', 'seq')
- ln1_gain_grad: float32 [2, 1024], P(None, 'fsdp')
- ln1_bias_grad: float32 [2, 1024], P(None, 'fsdp')
- qkv_weight_grad: float32 [2, 1024, 3072], P(None, 'fsdp')
- query_bias_grad: float32 [2, 1024], P(None, 'fsdp')
- value_bias_grad: float32 [2, 1024], P(None, 'fsdp')
- out_weight_grad: float32 [2, 1024, 1024], P(None, 'fsdp')
- out_bias_grad: float32 [2, 1024], P(None, 'fsdp')
- ln2_gain_grad: float32 [2, 1024], P(None, 'fsdp')
- ln2_bias_grad: float32 [2, 1024], P(None, 'fsdp')
- up_weight_grad: float32 [2, 1024, 4096], P(None, 'fsdp')
- up_bias_grad: float32 [2, 4096], P(None, 'fsdp')
- down_weight_grad: float32 [2, 4096, 1024], P(None, 'fsdp')
- down_bias_grad: float32 [2, 1024], P(None, 'fsdp')
The draws below stay inside these ranges and needn't reach their ends.
Inputs may be any that keep to these rules, and one draw needn't show every extreme that they name: `lengths`: keys at or after a sequence's length are hidden from every query. Every length exceeds three quarters of 1024; in every draw some sequence has exactly 1024. `tokens`: input activations of order one.
All inputs are finite; a program needn't handle non-finite values.
Results may differ from the reference program's by a relative error of at most 0.03.
Values may be sent and summed in bfloat16 or wider, within the bound.
No kernel may reach another device: no remote copies, remote signals or barrier semaphores. Data moves between devices by JAX's collectives and lax.ppermute only.
A program may use at most 320 MiB of HBM per device.

```python
import math
import jax
import jax.numpy as jnp
from jax import lax

HEADS = 16
HEAD_DIM = 64
FF = 4096
D = 1024
LAYERS = 2
BLOCK = 256
LEN = 1024
SEQS = 8


def draw_lengths(key, part):
    key = jax.random.fold_in(key, 7)
    first_key, second_key = jax.random.split(key)
    drawn = jax.random.randint(first_key, (SEQS,), LEN - LEN // 4 + 1, LEN + 1)
    chosen = jax.random.randint(second_key, (), 0, SEQS)
    return jnp.where(jnp.arange(SEQS) == chosen, LEN, drawn).astype(jnp.int32)


def draw_tokens(key, part):
    key = jax.random.fold_in(key, 11)
    noise_key, direction_key, sign_key = jax.random.split(key, 3)
    noise = jax.random.normal(noise_key, (SEQS, LEN, D), jnp.float32)
    direction = jax.random.uniform(direction_key, (D,), jnp.float32, -1.6, 1.6)
    block_signs = (jax.random.randint(sign_key, (SEQS, LEN // BLOCK), 0, 2) * 2 - 1).astype(jnp.float32)
    sign_rows = jnp.repeat(block_signs, BLOCK, axis=1)
    values = noise + 1.5 * sign_rows[:, :, None] * direction[None, None, :]
    return jnp.clip(values, -6.0, 6.0).astype(jnp.bfloat16)


def levels(key, extent, cuts, least, largest):
    gain = 1.0
    for position, blocks in cuts:
        heights = jax.random.uniform(jax.random.fold_in(jax.random.fold_in(key, 6), position), (blocks,), jnp.float32, least / len(cuts), largest / len(cuts))
        gain = gain * jnp.repeat(jnp.exp(heights), extent[position] // blocks).reshape((-1,) + (1,) * (len(extent) - 1 - position))
    return gain


def scatter_about(stream_key, shape, deviation, reach, cuts=(), kind=jnp.bfloat16):
    array = jax.random.normal(stream_key, shape, jnp.float32) * deviation
    if len(cuts) > 0:
        array = levels(stream_key, shape, cuts, -0.22, 0.18) * array
    return jnp.clip(array, min=-reach, max=reach).astype(kind)


def setup_inputs(seed: int = 0) -> dict:
    key_of = jax.random.split(jax.random.key(seed), 17)
    tokens = draw_tokens(jax.random.fold_in(key_of[16], 71), 0)
    lengths = draw_lengths(jax.random.fold_in(key_of[16], 71), 0)
    cotangent = scatter_about(key_of[2], (SEQS, LEN, D), 1.0, 6.0, ((0, 8), (1, 4)))
    ln1_gain = jnp.clip(1.0 + 0.18 * jax.random.normal(key_of[3], (LAYERS, D), jnp.float32), 0.099609375, 1.8984375).astype(jnp.bfloat16)
    ln1_bias = scatter_about(key_of[4], (LAYERS, D), 0.3, 1.75, ((1, 8),))
    qkv_weight = scatter_about(key_of[5], (LAYERS, D, 3 * D), D ** -0.5, 0.1875, ((1, 8),))
    query_bias = scatter_about(key_of[6], (LAYERS, D), 0.5, 3.0, ((1, 8),))
    value_bias = scatter_about(key_of[7], (LAYERS, D), 0.5, 3.0, ((1, 8),))
    out_weight = scatter_about(key_of[8], (LAYERS, D, D), (D // 4) ** -0.5, 0.375, ((1, 8),))
    out_bias = scatter_about(key_of[9], (LAYERS, D), 0.3, 1.75, ((1, 8),))
    ln2_gain = jnp.clip(1.0 + 0.18 * jax.random.normal(key_of[10], (LAYERS, D), jnp.float32), 0.099609375, 1.8984375).astype(jnp.bfloat16)
    ln2_bias = scatter_about(key_of[11], (LAYERS, D), 0.3, 1.75, ((1, 8),))
    up_weight = scatter_about(key_of[12], (LAYERS, D, FF), D ** -0.5, 0.1875, ((1, 8),))
    up_bias = scatter_about(key_of[13], (LAYERS, FF), 0.5, 3.0, ((1, 8),))
    down_weight = scatter_about(key_of[14], (LAYERS, FF, D), FF ** -0.5, 0.09375, ((1, 8),))
    down_bias = scatter_about(key_of[15], (LAYERS, D), 0.3, 1.75, ((1, 8),))
    return dict(tokens=tokens, lengths=lengths, cotangent=cotangent, ln1_gain=ln1_gain, ln1_bias=ln1_bias, qkv_weight=qkv_weight, query_bias=query_bias, value_bias=value_bias, out_weight=out_weight, out_bias=out_bias, ln2_gain=ln2_gain, ln2_bias=ln2_bias, up_weight=up_weight, up_bias=up_bias, down_weight=down_weight, down_bias=down_bias)


@jax.custom_vjp
def low(v):
    return lax.optimization_barrier(v.astype(jnp.bfloat16)).astype(jnp.float32)

@jax.custom_vjp
def low_back(v):
    return v

def low_keep(v):
    return (low(v), None)

def low_pass(kept, grad):
    return (grad,)

def back_keep(v):
    return (v, None)

def back_low(kept, grad):
    return (low(grad),)
low.defvjp(low_keep, low_pass)
low_back.defvjp(back_keep, back_low)
EPS = 1e-05
NEG = -1e+30

def normalize(inputs, scale_vec, shift_vec):
    center = inputs - lax.optimization_barrier(jnp.mean(inputs, axis=-1, keepdims=True))
    spread = lax.optimization_barrier(jnp.mean(center * center, axis=-1, keepdims=True))
    return center * lax.rsqrt(spread + EPS) * scale_vec + shift_vec

def smooth_gelu(values_in):
    inner = 0.7978845608028654 * (values_in + 0.044715 * values_in * values_in * values_in)
    return 0.5 * values_in * (1.0 + jnp.tanh(inner))

def head_slopes():
    return jnp.exp2(-8.0 * (jnp.arange(HEADS, dtype=jnp.float32) + 1.0) / HEADS)

def product(left_side, right_side):
    return jnp.matmul(left_side, right_side, precision=lax.Precision.HIGHEST)

def attend_sequence(members):
    queries, keys, values, seq_length = members
    query_span = min(512, LEN)
    query_blocks = queries.reshape(LEN // query_span, query_span, HEADS, HEAD_DIM)
    key_heads = keys.reshape(LEN, HEADS, HEAD_DIM)
    value_heads = values.reshape(LEN, HEADS, HEAD_DIM)
    key_pos = jnp.arange(LEN, dtype=jnp.int32)
    slopes = head_slopes()

    def one_block(block_members):
        query_block, first_row = block_members
        query_pos = first_row + jnp.arange(query_span, dtype=jnp.int32)
        raw_scores = jnp.einsum('qhd,khd->hqk', query_block, key_heads, precision=lax.Precision.HIGHEST) * HEAD_DIM ** (-0.5)
        distance = jnp.abs(query_pos[:, None] - key_pos[None, :]).astype(jnp.float32)
        raw_scores = low_back(raw_scores - slopes[:, None, None] * distance[None])
        visible = (key_pos[None, :] // BLOCK <= query_pos[:, None] // BLOCK) & (key_pos[None, :] < seq_length)
        masked = jnp.where(visible[None], raw_scores, NEG)
        row_max = lax.optimization_barrier(jnp.max(masked, axis=-1, keepdims=True))
        exponent = jnp.exp(masked - row_max)
        probabilities = low(exponent / lax.optimization_barrier(jnp.sum(exponent, axis=-1, keepdims=True)))
        return jnp.einsum('hqk,khd->qhd', probabilities, value_heads, precision=lax.Precision.HIGHEST)
    starts = jnp.arange(LEN // query_span, dtype=jnp.int32) * query_span
    attended = lax.map(jax.checkpoint(one_block), (query_blocks, starts))
    return attended.reshape(LEN, HEADS * HEAD_DIM)

def layer(stream, weight_set, seq_lengths):
    gain_one, shift_one, w_qkv, bias_query, bias_value, w_out, bias_out, gain_two, shift_two, w_up, bias_up, w_down, bias_down = weight_set
    model_width = HEADS * HEAD_DIM
    normed_one = low(normalize(stream, gain_one, shift_one))
    packed = product(normed_one, w_qkv) + jnp.concatenate([bias_query, jnp.zeros_like(bias_query), bias_value])
    packed = low(low_back(packed))
    attended = lax.map(jax.checkpoint(attend_sequence), (packed[..., :model_width], packed[..., model_width:2 * model_width], packed[..., 2 * model_width:], seq_lengths))
    attended = low(low_back(attended))
    middle = stream + low_back(product(attended, w_out) + bias_out)
    normed_two = low(normalize(middle, gain_two, shift_two))
    hidden_pre = low_back(product(normed_two, w_up) + bias_up)
    hidden_act = low(smooth_gelu(hidden_pre))
    return middle + low_back(product(hidden_act, w_down) + bias_down)

def forward(stream, weight_set, seq_lengths):
    for layer_index in range(LAYERS):
        stream = layer(stream, tuple((item[layer_index] for item in weight_set)), seq_lengths)
    return stream

def reference(tokens, lengths, cotangent, ln1_gain, ln1_bias, qkv_weight, query_bias, value_bias, out_weight, out_bias, ln2_gain, ln2_bias, up_weight, up_bias, down_weight, down_bias):
    params = tuple((item.astype(jnp.float32) for item in (ln1_gain, ln1_bias, qkv_weight, query_bias, value_bias, out_weight, out_bias, ln2_gain, ln2_bias, up_weight, up_bias, down_weight, down_bias)))
    model_width = HEADS * HEAD_DIM
    group_size = math.gcd(SEQS, max(1, 4096 // LEN))
    group_count = SEQS // group_size
    inputs = tokens.astype(jnp.float32).reshape(group_count, group_size, LEN, model_width)
    cot_rows = cotangent.astype(jnp.float32).reshape(group_count, group_size, LEN, model_width)
    seq_lengths = lengths.reshape(group_count, group_size)

    def one_group(totals, members):
        stream_in, cot_group, length_group = members
        result, pullback = jax.vjp(lambda stream_arg, weight_arg: forward(stream_arg, weight_arg, length_group), stream_in, params)
        grad_in, grad_weights = pullback(cot_group)
        totals = tuple((first_item + second_item for first_item, second_item in zip(totals, grad_weights)))
        return (totals, (result, grad_in))
    start_totals = tuple((jnp.zeros_like(item) for item in params))
    grads, (results, grad_inputs) = lax.scan(one_group, start_totals, (inputs, cot_rows, seq_lengths))
    return (results.reshape(SEQS, LEN, model_width).astype(jnp.bfloat16), grad_inputs.reshape(SEQS, LEN, model_width), grads[0], grads[1], grads[2], grads[3], grads[4], grads[5], grads[6], grads[7], grads[8], grads[9], grads[10], grads[11], grads[12])
```

```python
import jax
import jax.numpy as jnp
from jax import lax
from jax.sharding import PartitionSpec as P

HEADS = 16
HEAD_DIM = 64
LAYERS = 2
BLOCK = 256
EPS = 1e-05
NEG = -1e30
BF = jnp.bfloat16
F32 = jnp.float32


def normalize(inputs, scale_vec, shift_vec):
    center = inputs - jnp.mean(inputs, axis=-1, keepdims=True)
    spread = jnp.mean(center * center, axis=-1, keepdims=True)
    return center * lax.rsqrt(spread + EPS) * scale_vec + shift_vec


def smooth_gelu(values_in):
    inner = 0.7978845608028654 * (values_in + 0.044715 * values_in * values_in * values_in)
    return 0.5 * values_in * (1.0 + jnp.tanh(inner))


def head_slopes():
    return jnp.exp2(-8.0 * (jnp.arange(HEADS, dtype=F32) + 1.0) / HEADS)


def cube_masks(size):
    if size == 8:
        return (1, 2, 6)
    if size == 32:
        return (1, 3, 4, 12, 16)
    return tuple(1 << bit for bit in range(size.bit_length() - 1))


def rotated(masks, by):
    by = by % len(masks)
    return masks[by:] + masks[:by]


def hop(value, axis, mask):
    size = lax.axis_size(axis)
    return lax.ppermute(value, axis, [(i, i ^ mask) for i in range(size)])


def core_swap(value):
    return hop(value, "seq", 1)


def y_swap(value):
    return hop(value, "seq", 2)


def slot_table(order):
    rel = [0]
    for mask in order:
        rel = rel + [item ^ mask for item in rel]
    return rel


def take_slot(stacked, index):
    return lax.dynamic_index_in_dim(stacked, index, 0, keepdims=False)


def gather_shards(shard, order):
    current = shard[None]
    for mask in order:
        current = jnp.concatenate([current, hop(current, "fsdp", mask)])
    rel = slot_table(order)
    slot_of = [0] * len(rel)
    for slot, item in enumerate(rel):
        slot_of[item] = slot
    slot_of = jnp.array(slot_of, jnp.int32)
    me = lax.axis_index("fsdp")
    return jnp.concatenate(
        [take_slot(current, slot_of[me ^ owner])[None] for owner in range(len(rel))]
    )


def scatter_shards(full, order, kind=BF):
    me = lax.axis_index("fsdp")
    rel = slot_table(order[::-1])
    current = jnp.concatenate([take_slot(full, me ^ item)[None] for item in rel])
    for mask in order:
        half = current.shape[0] // 2
        other = hop(current[half:], "fsdp", mask)
        current = (current[:half].astype(F32) + other.astype(F32)).astype(kind)
    return current[0]


def attention_scores(queries, keys, q_pos, k_pos, slopes, seq_length):
    raw = jnp.einsum("qhd,khd->hqk", queries, keys, preferred_element_type=F32) * HEAD_DIM**-0.5
    distance = jnp.abs(q_pos[:, None] - k_pos[None, :]).astype(F32)
    raw = raw - slopes[:, None, None] * distance[None]
    visible = (k_pos[None, :] // BLOCK <= q_pos[:, None] // BLOCK) & (k_pos[None, :] < seq_length)
    return raw, visible[None]


def attend(queries, keys, values, q_pos, k_pos, slopes, seq_length):
    raw, visible = attention_scores(queries, keys, q_pos, k_pos, slopes, seq_length)
    top = jnp.max(jnp.where(visible, raw, NEG), axis=-1)
    weights = jnp.where(visible, jnp.exp(raw - top[..., None]), 0.0)
    total = jnp.sum(weights, axis=-1)
    summed = jnp.einsum("hqk,khd->hqd", weights.astype(BF), values, preferred_element_type=F32)
    attended = jnp.transpose(summed / total[..., None], (1, 0, 2)).reshape(queries.shape[0], -1)
    return attended, top + jnp.log(total)


def attend_back(queries, keys, values, grad_att, attended, lse, q_pos, k_pos, slopes, seq_length):
    rows, heads, _ = queries.shape
    grad_heads = grad_att.reshape(rows, heads, HEAD_DIM)
    delta = jnp.sum(
        grad_heads.astype(F32) * attended.reshape(rows, heads, HEAD_DIM), axis=-1
    ).T
    raw, visible = attention_scores(queries, keys, q_pos, k_pos, slopes, seq_length)
    probs = jnp.where(visible, jnp.exp(raw - lse[..., None]), 0.0)
    grad_probs = jnp.einsum("qhd,khd->hqk", grad_heads, values, preferred_element_type=F32)
    grad_scores = (probs * (grad_probs - delta[..., None])).astype(BF)
    scale = HEAD_DIM**-0.5
    grad_q = jnp.einsum("hqk,khd->qhd", grad_scores, keys, preferred_element_type=F32) * scale
    grad_k = jnp.einsum("hqk,qhd->khd", grad_scores, queries, preferred_element_type=F32) * scale
    grad_v = jnp.einsum("hqk,qhd->khd", probs.astype(BF), grad_heads, preferred_element_type=F32)
    return (
        grad_q.reshape(rows, -1),
        grad_k.reshape(keys.shape[0], -1),
        grad_v.reshape(keys.shape[0], -1),
    )


def dot(left, right):
    return jnp.dot(left, right, preferred_element_type=F32)


def dot_t(left, right):
    return jnp.einsum("tf,df->td", left, right, preferred_element_type=F32)


def t_dot(left, right):
    return jnp.einsum("td,tf->df", left, right, preferred_element_type=F32)


def pair(own):
    return jnp.concatenate([own, core_swap(own)])


def pair_sum(partial, rows):
    return partial[:rows] + core_swap(partial[rows:].astype(BF)).astype(F32)


def shards(
    tokens,
    lengths,
    cotangent,
    ln1_gain,
    ln1_bias,
    qkv_weight,
    query_bias,
    value_bias,
    out_weight,
    out_bias,
    ln2_gain,
    ln2_bias,
    up_weight,
    up_bias,
    down_weight,
    down_bias,
):
    fsdp = lax.axis_size("fsdp")
    masks = cube_masks(fsdp)
    run = lax.axis_index("seq")
    core = run % 2
    stream = tokens[0].astype(F32)
    rows, width = stream.shape
    half = width // 2
    seq_length = lengths[0]
    hidden = up_weight.shape[2]
    piece = hidden // fsdp // 2
    heads = HEADS // 2

    own_pos = jnp.arange(rows, dtype=jnp.int32)
    blocks = [(run ^ j) * rows + own_pos for j in range(4)]
    q_pos = jnp.concatenate(blocks[:2])
    k_pos = jnp.concatenate(blocks)
    slopes = lax.dynamic_slice_in_dim(head_slopes(), core * heads, heads)

    def core_part(value, axis):
        size = value.shape[axis] // 2
        return lax.dynamic_slice_in_dim(value, core * size, size, axis)

    vectors = (ln1_gain, ln1_bias, query_bias, value_bias, out_bias, ln2_gain, ln2_bias, down_bias)
    small = jnp.concatenate([jnp.stack(vectors, 1).reshape(LAYERS, -1), up_bias], axis=1)
    small = gather_shards(small, rotated(masks, 0)).astype(F32)
    part = width // fsdp

    def small_of(layer, member):
        return small[:, layer, member * part : (member + 1) * part].reshape(-1)

    def gathered(layer):
        qkv = qkv_weight[layer].reshape(-1, 3, width)
        qkv = core_part(qkv, 2).reshape(-1, 3 * half)
        w_qkv = gather_shards(qkv, rotated(masks, 0)).reshape(width, 3 * half)
        out_half = gather_shards(core_part(out_weight[layer], 1), rotated(masks, 0))
        out_half = out_half.reshape(width, half)
        out_other = core_swap(out_half)
        w_out = jnp.where(
            core == 0,
            jnp.concatenate([out_half, out_other], axis=1),
            jnp.concatenate([out_other, out_half], axis=1),
        )
        up = up_weight[layer].reshape(part, fsdp, 2, piece)
        up = lax.dynamic_index_in_dim(up, core, 2, keepdims=False).reshape(part, -1)
        w_up = gather_shards(up, rotated(masks, 1)).reshape(width, hidden // 2)
        w_down = gather_shards(core_part(down_weight[layer], 0), rotated(masks, 2))
        w_down = w_down.reshape(hidden // 2, width)
        bias_up = small[:, layer, 8 * part :].reshape(fsdp, 2, piece)
        bias_up = lax.dynamic_index_in_dim(bias_up, core, 1, keepdims=False).reshape(-1)
        bias_qkv = jnp.concatenate(
            [
                core_part(small_of(layer, 2), 0),
                jnp.zeros((half,), F32),
                core_part(small_of(layer, 3), 0),
            ]
        )
        return w_qkv, bias_qkv, w_out, w_up, bias_up, w_down

    weights = [gathered(layer) for layer in range(LAYERS)]
    saved = []
    for layer in range(LAYERS):
        w_qkv, bias_qkv, w_out, w_up, bias_up, w_down = weights[layer]
        normed = normalize(stream, small_of(layer, 0), small_of(layer, 1))
        h1 = pair(normed.astype(BF))
        packed = (dot(h1, w_qkv) + bias_qkv).astype(BF)
        kv = packed[:, half:]
        kv = jnp.concatenate([kv, y_swap(kv)])
        queries = packed[:, :half].reshape(-1, heads, HEAD_DIM)
        keys = kv[:, :half].reshape(-1, heads, HEAD_DIM)
        values = kv[:, half:].reshape(-1, heads, HEAD_DIM)
        attended, lse = attend(queries, keys, values, q_pos, k_pos, slopes, seq_length)
        att_low = attended.astype(BF)
        att_other = core_swap(att_low[rows:])
        att_own = jnp.where(
            core == 0,
            jnp.concatenate([att_low[:rows], att_other], axis=1),
            jnp.concatenate([att_other, att_low[:rows]], axis=1),
        )
        middle = stream + (dot(att_own, w_out) + small_of(layer, 4))
        normed = normalize(middle, small_of(layer, 5), small_of(layer, 6))
        h2 = pair(normed.astype(BF))
        pre = dot(h2, w_up) + bias_up
        act = smooth_gelu(pre).astype(BF)
        saved.append(
            (stream, h1, queries, keys, values, attended, lse, att_own, middle, h2, pre, act)
        )
        stream = middle + (pair_sum(dot(act, w_down), rows) + small_of(layer, 7))
    result = stream.astype(BF)[None]

    grad = cotangent[0].astype(F32)
    layer_grads = [None] * LAYERS
    for layer in reversed(range(LAYERS)):
        w_qkv, bias_qkv, w_out, w_up, bias_up, w_down = weights[layer]
        stream, h1, queries, keys, values, attended, lse, att_own, middle, h2, pre, act = saved[
            layer
        ]

        def owner_sum(full, by):
            shard = scatter_shards(full, rotated(masks, by)[::-1]).astype(F32)
            shard = shard + y_swap(shard.astype(BF)).astype(F32)
            return shard

        g_own = grad.astype(BF)
        g_down = pair(g_own)
        grad_down_w = owner_sum(t_dot(act, g_down).astype(BF).reshape(fsdp, piece, width), 2)
        grad_act = dot_t(g_down, w_down)
        _, gelu_pull = jax.vjp(smooth_gelu, pre)
        g_pre = gelu_pull(grad_act)[0].astype(BF)
        grad_up_w = owner_sum(t_dot(h2, g_pre).astype(BF).reshape(fsdp, part, -1), 1)
        grad_h2 = pair_sum(dot_t(g_pre, w_up), rows)
        _, norm_pull = jax.vjp(normalize, middle, small_of(layer, 5), small_of(layer, 6))
        grad_middle, grad_gain_two, grad_shift_two = norm_pull(grad_h2)
        grad_middle = grad + grad_middle
        g_branch = grad_middle.astype(BF)
        grad_out = t_dot(att_own, g_branch).astype(BF)
        kept = core_part(grad_out, 1)
        sent = lax.dynamic_slice_in_dim(grad_out, (1 - core) * half, half, 1)
        grad_out = (kept.astype(F32) + core_swap(sent).astype(F32)).astype(BF)
        grad_out_w = owner_sum(grad_out.reshape(fsdp, part, half), 0)
        g_att = dot_t(g_branch, w_out).astype(BF)
        g_att_kept = core_part(g_att, 1)
        g_att_sent = lax.dynamic_slice_in_dim(g_att, (1 - core) * half, half, 1)
        g_att = jnp.concatenate([g_att_kept, core_swap(g_att_sent)])
        grad_q, grad_k, grad_v = attend_back(
            queries, keys, values, g_att, attended, lse, q_pos, k_pos, slopes, seq_length
        )
        grad_kv = jnp.concatenate([grad_k, grad_v], axis=1)
        local = 2 * rows
        grad_kv = grad_kv[:local].astype(BF).astype(F32) + y_swap(grad_kv[local:].astype(BF)).astype(F32)
        g_packed = jnp.concatenate([grad_q, grad_kv], axis=1).astype(BF)
        grad_qkv_w = owner_sum(t_dot(h1, g_packed).astype(BF).reshape(fsdp, part, -1), 0)
        grad_h1 = pair_sum(dot_t(g_packed, w_qkv), rows)
        _, norm_pull = jax.vjp(normalize, stream, small_of(layer, 0), small_of(layer, 1))
        grad_stream, grad_gain_one, grad_shift_one = norm_pull(grad_h1)
        grad = grad_middle + grad_stream

        def spread(value):
            return lax.dynamic_update_slice_in_dim(
                jnp.zeros((2 * value.shape[0],), F32), value, core * value.shape[0], 0
            )

        packed_sum = jnp.sum(g_packed, axis=0, dtype=F32)
        up_sum = jnp.sum(g_pre, axis=0, dtype=F32).reshape(fsdp, 1, piece)
        up_sum = lax.dynamic_update_slice_in_dim(
            jnp.zeros((fsdp, 2, piece), F32), up_sum, core, 1
        ).reshape(fsdp, 2 * piece)
        members = [
            grad_gain_one,
            grad_shift_one,
            spread(packed_sum[:half]),
            spread(packed_sum[2 * half :]),
            jnp.sum(g_branch, axis=0, dtype=F32),
            grad_gain_two,
            grad_shift_two,
            jnp.sum(g_own, axis=0, dtype=F32),
        ]
        vector = jnp.concatenate([item.reshape(fsdp, part) for item in members] + [up_sum], axis=1)
        vector = scatter_shards(vector, rotated(masks, 0), F32)
        vector = vector + y_swap(vector)
        vector = vector + core_swap(vector)
        small_grads = [vector[i * part : (i + 1) * part] for i in range(8)] + [vector[8 * part :]]

        def both(own, axis):
            other = core_swap(own)
            return jnp.where(
                core == 0,
                jnp.concatenate([own, other], axis=axis),
                jnp.concatenate([other, own], axis=axis),
            )

        grad_qkv_w = both(grad_qkv_w.reshape(part, 3, half), 2).reshape(part, 3 * width)
        grad_out_w = both(grad_out_w, 1)
        grad_up_w = both(grad_up_w.reshape(part, fsdp, 1, piece), 2).reshape(part, hidden)
        grad_down_w = both(grad_down_w, 0)
        layer_grads[layer] = (
            small_grads[0],
            small_grads[1],
            grad_qkv_w,
            small_grads[2],
            small_grads[3],
            grad_out_w,
            small_grads[4],
            small_grads[5],
            small_grads[6],
            grad_up_w,
            small_grads[8],
            grad_down_w,
            small_grads[7],
        )
    stacked = tuple(
        jnp.stack([layer_grads[layer][member] for layer in range(LAYERS)]) for member in range(13)
    )
    return (result, grad[None]) + stacked


def solution(mesh):
    vector = P(None, "fsdp")
    matrix = P(None, "fsdp", None)
    data = P("fsdp", "seq", None)
    weight_specs = (
        vector,
        vector,
        matrix,
        vector,
        vector,
        matrix,
        vector,
        vector,
        vector,
        matrix,
        vector,
        matrix,
        vector,
    )
    in_specs = (data, P("fsdp"), data) + weight_specs
    out_specs = (data, data) + weight_specs
    return jax.shard_map(shards, mesh=mesh, in_specs=in_specs, out_specs=out_specs, check_vma=False)
```

```python
import functools

import jax
import jax.numpy as jnp
from jax import lax
from jax.experimental import pallas as pl
from jax.experimental.pallas import tpu as pltpu
from jax.sharding import PartitionSpec as P

HEADS = 16
HEAD_DIM = 64
LAYERS = 2
BLOCK = 256
EPS = 1e-05
NEG = -1e30
BF = jnp.bfloat16
F32 = jnp.float32


def normalize(inputs, scale_vec, shift_vec):
    center = inputs - jnp.mean(inputs, axis=-1, keepdims=True)
    spread = jnp.mean(center * center, axis=-1, keepdims=True)
    return center * lax.rsqrt(spread + EPS) * scale_vec + shift_vec


def smooth_gelu(values_in):
    inner = 0.7978845608028654 * (values_in + 0.044715 * values_in * values_in * values_in)
    return 0.5 * values_in * (1.0 + jnp.tanh(inner))


def head_slopes():
    return jnp.exp2(-8.0 * (jnp.arange(HEADS, dtype=F32) + 1.0) / HEADS)


def cube_masks(size):
    return tuple(1 << bit for bit in range(size.bit_length() - 1))


def hop(value, axis, mask):
    size = lax.axis_size(axis)
    return lax.ppermute(value, axis, [(i, i ^ mask) for i in range(size)])


def core_swap(value):
    return hop(value, "seq", 1)


def y_swap(value):
    return hop(value, "seq", 2)


def natural(parts):
    run = lax.axis_index("seq")
    stacked = jnp.stack(parts)
    return [lax.dynamic_index_in_dim(stacked, run ^ j, 0, keepdims=False) for j in range(4)]


def relative(value, axis):
    run = lax.axis_index("seq")
    size = value.shape[axis] // 4
    return [lax.dynamic_slice_in_dim(value, (run ^ j) * size, size, axis) for j in range(4)]


def seq_gather(own):
    across = y_swap(own)
    return jnp.concatenate([own, core_swap(own), across, core_swap(across)])


def seq_scatter(parts):
    far = parts[2] + core_swap(parts[3].astype(BF)).astype(F32)
    near = parts[0] + core_swap(parts[1].astype(BF)).astype(F32)
    return near + y_swap(far.astype(BF)).astype(F32)


def heads_to_rows(parts):
    across = y_swap(jnp.stack(parts[2:]))
    beside = core_swap(jnp.stack([parts[1], across[1]]))
    return jnp.concatenate(natural([parts[0], beside[0], across[0], beside[1]]), axis=1)


def rows_to_heads(value):
    parts = relative(value, 1)
    beside = core_swap(jnp.stack([parts[1], parts[3]]))
    across = y_swap(jnp.stack([parts[2], beside[1]]))
    return jnp.concatenate([parts[0], beside[0], across[0], across[1]])


def gather_small(shard):
    size = lax.axis_size("fsdp")
    current = shard[None]
    for mask in cube_masks(size):
        current = jnp.concatenate([current, hop(current, "fsdp", mask)])
    me = lax.axis_index("fsdp")
    return jnp.take(current, me ^ jnp.arange(size), axis=0)


def sum_small(full):
    size = lax.axis_size("fsdp")
    me = lax.axis_index("fsdp")
    current = jnp.take(full, me ^ jnp.arange(size), axis=0)
    for mask in cube_masks(size)[::-1]:
        half = current.shape[0] // 2
        current = current[:half] + hop(current[half:], "fsdp", mask)
    current = current[0]
    current = current + y_swap(current)
    return current + core_swap(current)


def assemble_kernel(widths, me_ref, *refs):
    count = len(widths)
    slots, outs, sems = refs[: -count - 1], refs[-count - 1 : -1], refs[-1]
    me = me_ref[0]
    rows = slots[0].shape[0]
    copies = []
    for r, slot in enumerate(slots):
        start = pl.multiple_of((me ^ r) * rows, rows)
        offset = 0
        for i, (out, size) in enumerate(zip(outs, widths)):
            source = slot.at[:, pl.ds(offset, size)]
            copies.append(
                pltpu.make_async_copy(source, out.at[pl.ds(start, rows), :], sems.at[r, i])
            )
            offset += size
    for copy in copies:
        copy.start()
    for copy in copies:
        copy.wait()


def assemble(slots, widths):
    rows = slots[0].shape[0]
    me = lax.axis_index("fsdp").astype(jnp.int32).reshape(1)
    hbm = pl.BlockSpec(memory_space=pl.ANY)
    return pl.pallas_call(
        functools.partial(assemble_kernel, widths),
        grid_spec=pltpu.PrefetchScalarGridSpec(
            num_scalar_prefetch=1,
            grid=(),
            in_specs=[hbm] * len(slots),
            out_specs=[hbm] * len(widths),
            scratch_shapes=[pltpu.SemaphoreType.DMA((len(slots), len(widths)))],
        ),
        out_shape=[jax.ShapeDtypeStruct((len(slots) * rows, size), BF) for size in widths],
        name="assemble",
    )(me, *slots)


def disperse_kernel(widths, slots, me_ref, *refs):
    count = len(widths)
    mats, even, odd, sems = refs[:count], refs[count], refs[count + 1], refs[-1]
    me = me_ref[0]
    rows = even.shape[1]
    copies = []
    for r in range(slots):
        start = pl.multiple_of((me ^ r) * rows, rows)
        target = (odd if r % 2 else even).at[r // 2]
        offset = 0
        for i, (mat, size) in enumerate(zip(mats, widths)):
            copies.append(
                pltpu.make_async_copy(
                    mat.at[pl.ds(start, rows), :],
                    target.at[:, pl.ds(offset, size)],
                    sems.at[r, i],
                )
            )
            offset += size
    for copy in copies:
        copy.start()
    for copy in copies:
        copy.wait()


def disperse(mats, slots):
    widths = [mat.shape[1] for mat in mats]
    rows = mats[0].shape[0] // slots
    me = lax.axis_index("fsdp").astype(jnp.int32).reshape(1)
    hbm = pl.BlockSpec(memory_space=pl.ANY)
    shape = jax.ShapeDtypeStruct((slots // 2, rows, sum(widths)), BF)
    return pl.pallas_call(
        functools.partial(disperse_kernel, widths, slots),
        grid_spec=pltpu.PrefetchScalarGridSpec(
            num_scalar_prefetch=1,
            grid=(),
            in_specs=[hbm] * len(mats),
            out_specs=[hbm] * 2,
            scratch_shapes=[pltpu.SemaphoreType.DMA((slots, len(widths)))],
        ),
        out_shape=[shape, shape],
        name="disperse",
    )(me, *mats)


def tied(value, after):
    return lax.optimization_barrier((value, after))[0]


def gather_bundle(own):
    size = lax.axis_size("fsdp")
    slots = [None] * size
    slots[0] = own
    for r in range(2, size, 2):
        slots[r] = hop(own, "fsdp", r)
    for r in range(0, size, 2):
        slots[r + 1] = hop(slots[r], "fsdp", 1)
    return slots


def scatter_bundle(mats, split=False):
    size = lax.axis_size("fsdp")
    even, odd = disperse(mats, size)
    if split:
        places = list(range(1, size // 2)) + [0]
        summed = [None] * (size // 2)
        for k in places:
            summed[k] = even[k].astype(F32) + hop(odd[k], "fsdp", 1).astype(F32)
    else:
        summed = even.astype(F32) + hop(odd, "fsdp", 1).astype(F32)
    total = summed[0]
    for k in range(1, size // 2):
        total = total + hop(summed[k].astype(BF), "fsdp", 2 * k).astype(F32)
    return total.astype(BF)


def attention_scores(queries, keys, q_pos, k_pos, slopes, seq_length):
    raw = jnp.einsum("qhd,khd->hqk", queries, keys, preferred_element_type=F32) * HEAD_DIM**-0.5
    distance = jnp.abs(q_pos[:, None] - k_pos[None, :]).astype(F32)
    raw = raw - slopes[:, None, None] * distance[None]
    visible = (k_pos[None, :] // BLOCK <= q_pos[:, None] // BLOCK) & (k_pos[None, :] < seq_length)
    return raw, visible[None]


def attend(queries, keys, values, q_pos, k_pos, slopes, seq_length):
    raw, visible = attention_scores(queries, keys, q_pos, k_pos, slopes, seq_length)
    top = jnp.max(jnp.where(visible, raw, NEG), axis=-1)
    weights = jnp.where(visible, jnp.exp(raw - top[..., None]), 0.0)
    total = jnp.sum(weights, axis=-1)
    summed = jnp.einsum("hqk,khd->hqd", weights.astype(BF), values, preferred_element_type=F32)
    attended = jnp.transpose(summed / total[..., None], (1, 0, 2)).reshape(queries.shape[0], -1)
    return attended, top + jnp.log(total)


def attend_back(queries, keys, values, grad_att, attended, lse, q_pos, k_pos, slopes, seq_length):
    rows, heads, _ = queries.shape
    grad_heads = grad_att.reshape(rows, heads, HEAD_DIM)
    delta = jnp.sum(
        grad_heads.astype(F32) * attended.reshape(rows, heads, HEAD_DIM), axis=-1
    ).T
    raw, visible = attention_scores(queries, keys, q_pos, k_pos, slopes, seq_length)
    probs = jnp.where(visible, jnp.exp(raw - lse[..., None]), 0.0)
    grad_probs = jnp.einsum("qhd,khd->hqk", grad_heads, values, preferred_element_type=F32)
    grad_scores = (probs * (grad_probs - delta[..., None])).astype(BF)
    scale = HEAD_DIM**-0.5
    grad_q = jnp.einsum("hqk,khd->qhd", grad_scores, keys, preferred_element_type=F32) * scale
    grad_k = jnp.einsum("hqk,qhd->khd", grad_scores, queries, preferred_element_type=F32) * scale
    grad_v = jnp.einsum("hqk,qhd->khd", probs.astype(BF), grad_heads, preferred_element_type=F32)
    return (
        grad_q.reshape(rows, -1),
        grad_k.reshape(keys.shape[0], -1),
        grad_v.reshape(keys.shape[0], -1),
    )


def dot(left, right):
    return jnp.dot(left, right, preferred_element_type=F32)


def dot_t(left, right):
    return jnp.einsum("tf,df->td", left, right, preferred_element_type=F32)


def t_dot(left, right):
    return jnp.einsum("td,tf->df", left, right, preferred_element_type=F32)


def shards(
    tokens,
    lengths,
    cotangent,
    ln1_gain,
    ln1_bias,
    qkv_weight,
    query_bias,
    value_bias,
    out_weight,
    out_bias,
    ln2_gain,
    ln2_bias,
    up_weight,
    up_bias,
    down_weight,
    down_bias,
):
    fsdp = lax.axis_size("fsdp")
    run = lax.axis_index("seq")
    stream = tokens[0].astype(F32)
    rows, width = stream.shape
    seq_length = lengths[0]
    hidden = up_weight.shape[2]
    heads = HEADS // 4
    mine = width // 4
    part = width // fsdp
    piece = hidden // fsdp // 4

    positions = jnp.concatenate(
        [(run ^ j) * rows + jnp.arange(rows, dtype=jnp.int32) for j in range(4)]
    )
    slopes = lax.dynamic_slice_in_dim(head_slopes(), run * heads, heads)

    def quarter(value, axis):
        size = value.shape[axis] // 4
        return lax.dynamic_slice_in_dim(value, run * size, size, axis)

    vectors = (ln1_gain, ln1_bias, query_bias, value_bias, out_bias, ln2_gain, ln2_bias, down_bias)
    small = jnp.concatenate([jnp.stack(vectors, 1).reshape(LAYERS, -1), up_bias], axis=1)
    small = gather_small(small).astype(F32)

    def small_of(layer, member):
        return small[:, layer, member * part : (member + 1) * part].reshape(-1)

    half = width // 2

    def core_half(value, axis):
        return lax.dynamic_slice_in_dim(value, (run % 2) * half, half, axis)

    def bundle(layer, members):
        parts = {
            "qkv": lambda: quarter(qkv_weight[layer].reshape(part, 3, width), 2),
            "out": lambda: core_half(out_weight[layer], 1),
            "up": lambda: quarter(up_weight[layer].reshape(part, fsdp, -1), 2),
            "down": lambda: quarter(down_weight[layer], 0),
        }
        return jnp.concatenate([parts[name]().reshape(part, -1) for name in members], axis=1)

    def both(own):
        other = core_swap(own)
        return jnp.where(
            run % 2 == 0,
            jnp.concatenate([own, other], axis=1),
            jnp.concatenate([other, own], axis=1),
        )

    first = gather_bundle(bundle(0, ["qkv"]))
    second = gather_bundle(tied(bundle(0, ["out", "up", "down"]), first[2::2]))
    third = gather_bundle(tied(bundle(1, ["qkv", "out", "up", "down"]), second[2::2]))
    sizes = [3 * mine, half, hidden // 4, width]
    weights = [assemble(first, sizes[:1]) + assemble(second, sizes[1:]), assemble(third, sizes)]
    weights = [(w_qkv, both(w_out), w_up, w_down) for w_qkv, w_out, w_up, w_down in weights]

    def biases(layer):
        bias_up = quarter(small[:, layer, 8 * part :], 1).reshape(-1)
        bias_qkv = jnp.concatenate(
            [quarter(small_of(layer, 2), 0), jnp.zeros((mine,), F32), quarter(small_of(layer, 3), 0)]
        )
        return bias_qkv, bias_up

    saved = []
    for layer in range(LAYERS):
        w_qkv, w_out, w_up, w_down = weights[layer]
        bias_qkv, bias_up = biases(layer)
        normed = normalize(stream, small_of(layer, 0), small_of(layer, 1))
        h1 = seq_gather(normed.astype(BF))
        packed = (dot(h1, w_qkv) + bias_qkv).astype(BF)
        queries, keys, values = (
            packed[:, i * mine : (i + 1) * mine].reshape(-1, heads, HEAD_DIM) for i in range(3)
        )
        attended, lse = attend(queries, keys, values, positions, positions, slopes, seq_length)
        att_low = attended.astype(BF)
        att_own = heads_to_rows([att_low[j * rows : (j + 1) * rows] for j in range(4)])
        middle = stream + (dot(att_own, w_out) + small_of(layer, 4))
        normed = normalize(middle, small_of(layer, 5), small_of(layer, 6))
        h2 = seq_gather(normed.astype(BF))
        pre = dot(h2, w_up) + bias_up
        act = smooth_gelu(pre).astype(BF)
        saved.append(
            (stream, h1, queries, keys, values, attended, lse, att_own, middle, h2, pre, act)
        )
        partial = dot(act, w_down)
        total = seq_scatter([partial[j * rows : (j + 1) * rows] for j in range(4)])
        stream = middle + (total + small_of(layer, 7))
    result = stream.astype(BF)[None]

    grad = cotangent[0].astype(F32)
    layer_grads = [None] * LAYERS
    for layer in reversed(range(LAYERS)):
        w_qkv, w_out, w_up, w_down = weights[layer]
        stream, h1, queries, keys, values, attended, lse, att_own, middle, h2, pre, act = saved[
            layer
        ]
        g_own = grad.astype(BF)
        g_down = seq_gather(g_own)
        grad_down_w = t_dot(act, g_down).astype(BF)
        _, gelu_pull = jax.vjp(smooth_gelu, pre)
        g_pre = gelu_pull(dot_t(g_down, w_down))[0].astype(BF)
        grad_up_w = t_dot(h2, g_pre).astype(BF)
        partial = dot_t(g_pre, w_up)
        grad_h2 = seq_scatter([partial[j * rows : (j + 1) * rows] for j in range(4)])
        _, norm_pull = jax.vjp(normalize, middle, small_of(layer, 5), small_of(layer, 6))
        grad_middle, grad_gain_two, grad_shift_two = norm_pull(grad_h2)
        grad_middle = grad + grad_middle
        g_branch = grad_middle.astype(BF)
        grad_out_w = t_dot(att_own, g_branch).astype(BF)
        grad_out_w = (
            core_half(grad_out_w, 1).astype(F32)
            + core_swap(
                lax.dynamic_slice_in_dim(grad_out_w, (1 - run % 2) * half, half, 1)
            ).astype(F32)
        ).astype(BF)
        g_att = rows_to_heads(dot_t(g_branch, w_out).astype(BF))
        grads = attend_back(
            queries, keys, values, g_att, attended, lse, positions, positions, slopes, seq_length
        )
        g_packed = jnp.concatenate(grads, axis=1).astype(BF)
        grad_qkv_w = t_dot(h1, g_packed).astype(BF)
        partial = dot_t(g_packed, w_qkv)
        grad_h1 = seq_scatter([partial[j * rows : (j + 1) * rows] for j in range(4)])
        _, norm_pull = jax.vjp(normalize, stream, small_of(layer, 0), small_of(layer, 1))
        grad_stream, grad_gain_one, grad_shift_one = norm_pull(grad_h1)
        grad = grad_middle + grad_stream

        def spread(value, axis=0):
            shape = list(value.shape)
            size = shape[axis]
            shape[axis] = 4 * size
            return lax.dynamic_update_slice_in_dim(jnp.zeros(shape, F32), value, run * size, axis)

        packed_sum = jnp.sum(g_packed, axis=0, dtype=F32)
        members = [
            grad_gain_one,
            grad_shift_one,
            spread(packed_sum[:mine]),
            spread(packed_sum[2 * mine :]),
            jnp.sum(g_branch, axis=0, dtype=F32),
            grad_gain_two,
            grad_shift_two,
            jnp.sum(g_own, axis=0, dtype=F32),
        ]
        up_sum = spread(jnp.sum(g_pre, axis=0, dtype=F32).reshape(fsdp, piece), 1)
        vector = jnp.concatenate([item.reshape(fsdp, part) for item in members] + [up_sum], axis=1)
        vector = sum_small(vector)
        small_grads = [vector[i * part : (i + 1) * part] for i in range(8)] + [vector[8 * part :]]

        if layer:
            total = scatter_bundle([grad_qkv_w, grad_out_w, grad_up_w, grad_down_w])
            totals = [total]
        else:
            totals = [
                scatter_bundle([grad_qkv_w], True),
                scatter_bundle([grad_out_w, grad_up_w, grad_down_w]),
            ]
        quarters = []
        for total in totals:
            across = y_swap(total)
            beside = core_swap(jnp.stack([total, across]))
            quarters.append([total, beside[0], across, beside[1]])
        quarters = [jnp.concatenate(pieces, axis=1) for pieces in zip(*quarters)]
        edges = [3 * mine, 3 * mine + half, 3 * mine + half + hidden // 4]
        quarters = [jnp.split(item, edges, axis=1) for item in quarters]
        by_name = list(zip(*quarters))

        def whole(parts, axis):
            return jnp.concatenate(natural(parts), axis=axis).astype(F32)

        outs = by_name[1]
        halves = [
            outs[0].astype(F32) + outs[2].astype(F32),
            outs[1].astype(F32) + outs[3].astype(F32),
        ]
        grad_out_w = jnp.where(
            run % 2 == 0,
            jnp.concatenate(halves, axis=1),
            jnp.concatenate(halves[::-1], axis=1),
        )
        layer_grads[layer] = (
            small_grads[0],
            small_grads[1],
            whole([item.reshape(part, 3, mine) for item in by_name[0]], 2).reshape(part, 3 * width),
            small_grads[2],
            small_grads[3],
            grad_out_w,
            small_grads[4],
            small_grads[5],
            small_grads[6],
            whole([item.reshape(part, fsdp, piece) for item in by_name[2]], 2).reshape(
                part, hidden
            ),
            small_grads[8],
            whole([item.reshape(piece, width) for item in by_name[3]], 0),
            small_grads[7],
        )
    stacked = tuple(
        jnp.stack([layer_grads[layer][member] for layer in range(LAYERS)]) for member in range(13)
    )
    return (result, grad[None]) + stacked


def solution(mesh):
    vector = P(None, "fsdp")
    matrix = P(None, "fsdp", None)
    data = P("fsdp", "seq", None)
    weight_specs = (
        vector,
        vector,
        matrix,
        vector,
        vector,
        matrix,
        vector,
        vector,
        vector,
        matrix,
        vector,
        matrix,
        vector,
    )
    in_specs = (data, P("fsdp"), data) + weight_specs
    out_specs = (data, data) + weight_specs
    return jax.shard_map(shards, mesh=mesh, in_specs=in_specs, out_specs=out_specs, check_vma=False)
```

```python
import functools

import jax
import jax.numpy as jnp
from jax import lax
from jax.experimental import pallas as pl
from jax.experimental.pallas import tpu as pltpu
from jax.sharding import PartitionSpec as P

HEADS = 16
HEAD_DIM = 64
LAYERS = 2
BLOCK = 256
EPS = 1e-05
NEG = -1e30
BF = jnp.bfloat16
F32 = jnp.float32
GELU = 0.7978845608028654
CUBIC = 0.044715
VMEM = pl.BlockSpec(memory_space=pltpu.VMEM)
SMEM = pl.BlockSpec(memory_space=pltpu.SMEM)


def head_slopes():
    return jnp.exp2(-8.0 * (jnp.arange(HEADS, dtype=F32) + 1.0) / HEADS)


def hop(value, axis, mask):
    size = lax.axis_size(axis)
    return lax.ppermute(value, axis, [(i, i ^ mask) for i in range(size)])


def core_swap(value):
    return hop(value, "seq", 1)


def y_swap(value):
    return hop(value, "seq", 2)


def sum_small(full):
    size = lax.axis_size("fsdp")
    me = lax.axis_index("fsdp")
    full = full + y_swap(full)
    full = full + core_swap(full)
    slots = jnp.take(full, me ^ jnp.arange(size), axis=0)
    slots = slots.reshape((size // 2, 2) + full.shape[1:])
    slots = slots[:, 0] + hop(slots[:, 1], "fsdp", 1)
    total = slots[0]
    for k in range(1, size // 2):
        total = total + hop(slots[k], "fsdp", 2 * k)
    return total


def assemble_kernel(column, stride, key_ref, same, other, out, held, sems):
    key = key_ref[0]
    pairs, rows, width = held.shape[0] // 2, held.shape[1], held.shape[2]
    loads, stores = [], []
    for r in range(2 * pairs):
        place = pl.ds(r // 2 * stride, rows)
        source = (other if r % 2 else same).at[place, pl.ds(column, width)]
        loads.append(pltpu.make_async_copy(source, held.at[r], sems.at[r, 0]))
        start = pl.multiple_of((r ^ key) * rows, rows)
        target = out.at[pl.ds(start, rows), :]
        stores.append(pltpu.make_async_copy(held.at[r], target, sems.at[r, 1]))
    for load in loads:
        load.start()
    for load, store in zip(loads, stores):
        load.wait()
        store.start()
    for store in stores:
        store.wait()


def assemble(halves, column, width, rows, key):
    slots = lax.axis_size("fsdp")
    stride = 2 * halves[0].shape[0] // slots
    key = key.astype(jnp.int32).reshape(1)
    hbm = pl.BlockSpec(memory_space=pl.ANY)
    return pl.pallas_call(
        functools.partial(assemble_kernel, column, stride),
        grid_spec=pltpu.PrefetchScalarGridSpec(
            num_scalar_prefetch=1,
            grid=(),
            in_specs=[hbm] * 2,
            out_specs=hbm,
            scratch_shapes=[
                pltpu.VMEM((slots, rows, width), BF),
                pltpu.SemaphoreType.DMA((slots, 2)),
            ],
        ),
        out_shape=jax.ShapeDtypeStruct((slots * rows, width), BF),
        compiler_params=pltpu.CompilerParams(vmem_limit_bytes=32 << 20),
        cost_estimate=pl.CostEstimate(flops=0, bytes_accessed=0, transcendentals=0),
        name="assemble",
    )(key, *halves)


def tied(value, after):
    return lax.optimization_barrier((value, after))[0]


def meet(*values):
    return lax.optimization_barrier(values)


def pack_kernel(names, layer, place, *refs):
    sources, (out, sems) = dict(zip(names, refs)), refs[len(names) :]
    run = place[0]
    copies = []
    column = 0

    def add(source, size, rows=None):
        rows = source.shape[0] if rows is None else rows
        target = out.at[pl.ds(0, rows), pl.ds(column, size)]
        copies.append(pltpu.make_async_copy(source, target, sems.at[len(copies)]))
        return column + size

    for name in names:
        source = sources[name]
        if name == "small":
            rows = source.shape[0]
            target = out.at[pl.ds(out.shape[0] - rows, rows), :]
            copies.append(pltpu.make_async_copy(source, target, sems.at[len(copies)]))
            continue
        source = source.at[layer]
        part, width = source.shape
        if name == "qkv":
            for third in range(3):
                start = pl.multiple_of((4 * third + run) * (width // 12), width // 12)
                column = add(source.at[:, pl.ds(start, width // 12)], width // 12)
        elif name == "out":
            start = pl.multiple_of(run % 2 * (width // 2), width // 2)
            column = add(source.at[:, pl.ds(start, width // 2)], width // 2)
        elif name == "up":
            piece = part
            for slot in range(width // (4 * piece)):
                start = pl.multiple_of((4 * slot + run) * piece, piece)
                column = add(source.at[:, pl.ds(start, piece)], piece)
        else:
            start = pl.multiple_of(run * (part // 4), part // 4)
            column = add(source.at[pl.ds(start, part // 4), :], width)
    for copy in copies:
        copy.start()
    for copy in copies:
        copy.wait()


def pack(names, arrays, layer, place, rows, columns):
    count = sum({"qkv": 3, "up": arrays[0].shape[-1]}.get(name, 1) for name in names)
    hbm = pl.BlockSpec(memory_space=pl.ANY)
    return pl.pallas_call(
        functools.partial(pack_kernel, names, layer),
        in_specs=[SMEM] + [hbm] * len(arrays),
        out_specs=VMEM,
        out_shape=jax.ShapeDtypeStruct((rows, columns), BF),
        scratch_shapes=[pltpu.SemaphoreType.DMA((min(count, 64),))],
        compiler_params=pltpu.CompilerParams(vmem_limit_bytes=32 << 20),
        cost_estimate=pl.CostEstimate(flops=0, bytes_accessed=0, transcendentals=0),
        name="pack",
    )(place, *arrays)


def z_groups():
    size = lax.axis_size("fsdp")
    return [[x + 2 * k for k in range(size // 2)] for x in range(2)]


def gather_z(own):
    return lax.all_gather(own, "fsdp", axis=0, tiled=True, axis_index_groups=z_groups())


def x_swap(value):
    return hop(value, "fsdp", 1)


def added(same, received):
    return (same.astype(F32) + received.astype(F32)).astype(BF)


def scatter_z(same):
    return lax.psum_scatter(
        same, "fsdp", scatter_dimension=0, tiled=True, axis_index_groups=z_groups()
    )


def four(total):
    across = y_swap(total)
    return total, core_swap(total), across, core_swap(across)


def staged(body, held, refs):
    count = len(held)
    inputs, rest = refs[:count], refs[count:]
    places = [i for i in range(count) if held[i]]
    sems, buffers, rest = rest[-1], rest[-1 - len(places) : -1], rest[: -1 - len(places)]
    copies = [
        pltpu.make_async_copy(inputs[i], buffer, sems.at[number])
        for number, (i, buffer) in enumerate(zip(places, buffers))
    ]
    for copy in copies:
        copy.start()
    for copy in copies:
        copy.wait()
    inputs = list(inputs)
    for i, buffer in zip(places, buffers):
        inputs[i] = buffer
    body(*inputs, *rest)


def kernel_call(body, name, inputs, outputs, scratch=(), in_specs=None):
    held = [spec is VMEM for spec in in_specs or [VMEM] * len(inputs)]
    buffers = [pltpu.VMEM(item.shape, item.dtype) for item, one in zip(inputs, held) if one]
    return pl.pallas_call(
        lambda *refs: staged(body, held, refs),
        in_specs=[pl.BlockSpec(memory_space=pl.ANY) if one else SMEM for one in held],
        out_specs=[VMEM] * len(outputs),
        out_shape=[jax.ShapeDtypeStruct(shape, kind) for shape, kind in outputs],
        scratch_shapes=[*scratch, *buffers, pltpu.SemaphoreType.DMA((max(len(buffers), 1),))],
        compiler_params=pltpu.CompilerParams(vmem_limit_bytes=48 << 20),
        cost_estimate=pl.CostEstimate(flops=0, bytes_accessed=0, transcendentals=0),
        name=name,
    )(*inputs)


def nn(left, right):
    return jnp.dot(left, right, preferred_element_type=F32)


def nt(left, right):
    return lax.dot_general(left, right, (((1,), (1,)), ((), ())), preferred_element_type=F32)


def tn(left, right):
    return lax.dot_general(left, right, (((0,), (0,)), ((), ())), preferred_element_type=F32)


def normalized(value):
    center = value - jnp.mean(value, axis=-1, keepdims=True)
    scale = lax.rsqrt(jnp.mean(center * center, axis=-1, keepdims=True) + EPS)
    return center * scale, scale


def norm_back(value, gain, grad):
    hat, scale = normalized(value)
    inner = grad * gain
    mean = jnp.mean(inner, axis=-1, keepdims=True)
    along = jnp.mean(inner * hat, axis=-1, keepdims=True)
    grad_gain = jnp.sum(grad * hat, axis=0, keepdims=True)
    return scale * (inner - mean - hat * along), grad_gain, jnp.sum(grad, axis=0, keepdims=True)


GAIN_ONE, SHIFT_ONE, BIAS_Q, BIAS_V, BIAS_OUT, GAIN_TWO, SHIFT_TWO, BIAS_DOWN = range(8)


def row(table, index):
    return table[index : index + 1, :]


def first_norm_kernel(a, b, c, d, table, *outs):
    for value, out in zip((a, b, c, d), outs):
        hat, _ = normalized(value[...].astype(F32))
        out[...] = (hat * row(table, GAIN_ONE) + row(table, SHIFT_ONE)).astype(BF)


def first_norm(blocks, table):
    outs = [(item.shape, BF) for item in blocks]
    return kernel_call(first_norm_kernel, "first_norm", (*blocks, table), outs)


def layer_end_kernel(middle, keep, beside, across, table, after, stream, normed):
    total = keep[...] + beside[...].astype(F32) + across[...].astype(F32)
    value = middle[...] + (total + row(table, BIAS_DOWN))
    stream[...] = value
    if after is None:
        normed[...] = value.astype(BF)
    else:
        hat, _ = normalized(value)
        normed[...] = (hat * row(after, GAIN_ONE) + row(after, SHIFT_ONE)).astype(BF)


def last_end_kernel(middle, keep, beside, across, table, stream, low):
    layer_end_kernel(middle, keep, beside, across, table, None, stream, low)


def layer_end(middle, sums, table, after):
    outs = [(middle.shape, F32), (middle.shape, BF)]
    if after is None:
        return kernel_call(last_end_kernel, "last_end", (middle, *sums, table), outs)
    return kernel_call(layer_end_kernel, "layer_end", (middle, *sums, table, after), outs)


def out_kernel(
    scalars, own, beside, across, w_own, w_other, stream, table, middle, normed, attended
):
    run = scalars[0]
    core = run % 2
    parts = [own[...], beside[0], across[0], beside[1]]
    size = parts[0].shape[1]
    starts = [pl.multiple_of((run ^ j) * size, size) for j in range(4)]
    for part, start in zip(parts, starts):
        attended[:, pl.ds(start, size)] = part
    half = w_own.shape[1]
    for weight, place in ((w_own, core), (w_other, 1 - core)):
        total = None
        for part, start in zip(parts, starts):
            term = nn(part, weight[pl.ds(start, size), :])
            total = term if total is None else total + term
        lanes = pl.ds(pl.multiple_of(place * half, half), half)
        bias = table[BIAS_OUT : BIAS_OUT + 1, lanes]
        middle[:, lanes] = stream[:, lanes] + (total + bias)
    hat, _ = normalized(middle[...])
    normed[...] = (hat * row(table, GAIN_TWO) + row(table, SHIFT_TWO)).astype(BF)


def out_step(scalars, own, beside, across, w_outs, stream, table):
    outs = [(stream.shape, F32), (stream.shape, BF), (stream.shape, BF)]
    inputs = (scalars, own, beside, across, *w_outs, stream, table)
    return kernel_call(out_kernel, "out_step", inputs, outs, in_specs=[SMEM] + [VMEM] * 7)


def ffn_kernel(a, b, w_up, bias, w_down, act, slope, keep, send, source):
    rows = a.shape[0]
    source[:rows, :] = a[...]
    source[rows:, :] = b[...]
    pre = nn(source[...], w_up[...]) + bias[...]
    square = pre * pre
    bent = jnp.tanh(GELU * pre * (1.0 + CUBIC * square))
    half = 0.5 + 0.5 * bent
    value = (pre * half).astype(BF)
    act[...] = value
    rise = half + (0.5 * GELU) * pre * (1.0 - bent * bent) * (1.0 + 3.0 * CUBIC * square)
    slope[...] = rise.astype(BF)
    total = nn(value, w_down[...])
    keep[...] = total[:rows, :]
    send[...] = total[rows:, :].astype(BF)


def ffn(a, b, w_up, bias, w_down):
    rows, width = a.shape
    hidden = w_up.shape[1]
    outs = [
        ((2 * rows, hidden), BF),
        ((2 * rows, hidden), BF),
        ((rows, width), F32),
        ((rows, width), BF),
    ]
    scratch = [pltpu.VMEM((2 * rows, width), BF)]
    return kernel_call(ffn_kernel, "ffn", (a, b, w_up, bias, w_down), outs, scratch)


def ffn_back_kernel(a, b, slope, w_up, w_down, grad_pre, keep, send, sums, source):
    rows = a.shape[0]
    source[:rows, :] = a[...]
    source[rows:, :] = b[...]
    grad_act = nt(source[...], w_down[...])
    value = (grad_act * slope[...].astype(F32)).astype(BF)
    grad_pre[...] = value
    sums[...] = jnp.sum(value.astype(F32), axis=0, keepdims=True)
    total = nt(value, w_up[...])
    keep[...] = total[:rows, :]
    send[...] = total[rows:, :].astype(BF)


def ffn_back(a, b, slope, w_up, w_down):
    rows, width = a.shape
    hidden = w_up.shape[1]
    outs = [
        ((2 * rows, hidden), BF),
        ((rows, width), F32),
        ((rows, width), BF),
        ((1, hidden), F32),
    ]
    scratch = [pltpu.VMEM((2 * rows, width), BF)]
    return kernel_call(ffn_back_kernel, "ffn_back", (a, b, slope, w_up, w_down), outs, scratch)


def weight_grad_kernel(count, parts, scalars, *refs):
    x = scalars[1]
    lefts, rights = refs[: parts[0]], refs[parts[0] : parts[0] + parts[1]]
    same, other, left, right, total = refs[parts[0] + parts[1] :]
    for sources, target in ((lefts, left), (rights, right)):
        start = 0
        for source in sources:
            target[start : start + source.shape[0], :] = source[...]
            start += source.shape[0]
    total[...] = tn(left[...], right[...]).astype(BF)
    rows = total.shape[0] // count
    for r in range(count):
        start = pl.multiple_of((r ^ x) * rows, rows)
        target = other if r % 2 else same
        target[r // 2 * rows : (r // 2 + 1) * rows, :] = total[pl.ds(start, rows), :]


def weight_grad(lefts, rights, place):
    count = lax.axis_size("fsdp")
    total = sum(item.shape[0] for item in lefts)
    tall, wide = lefts[0].shape[1], rights[0].shape[1]
    outs = [((tall // 2, wide), BF)] * 2
    scratch = [
        pltpu.VMEM((total, tall), BF),
        pltpu.VMEM((total, wide), BF),
        pltpu.VMEM((tall, wide), BF),
    ]
    inputs = (place, *lefts, *rights)
    body = functools.partial(weight_grad_kernel, count, (len(lefts), len(rights)))
    specs = [SMEM] + [VMEM] * (len(inputs) - 1)
    return kernel_call(body, "weight_grad", inputs, outs, scratch, specs)


def out_grad_kernel(count, place, left, right, keep, send, total):
    core, x = place[0] % 2, place[1]
    half = keep.shape[2]
    rows = total.shape[0] // count
    for target, number in ((keep, core), (send, 1 - core)):
        lanes = pl.ds(pl.multiple_of(number * half, half), half)
        total[...] = tn(left[...], right[:, lanes]).astype(BF)
        for r in range(count):
            start = pl.multiple_of((r ^ x) * rows, rows)
            target[r % 2, r // 2 * rows : (r // 2 + 1) * rows, :] = total[pl.ds(start, rows), :]


def out_grad(left, right, place):
    count = lax.axis_size("fsdp")
    tall, wide = left.shape[1], right.shape[1]
    outs = [((2, tall // 2, wide // 2), BF)] * 2
    scratch = [pltpu.VMEM((tall, wide // 2), BF)]
    body = functools.partial(out_grad_kernel, count)
    return kernel_call(
        body, "out_grad", (place, left, right), outs, scratch, [SMEM, VMEM, VMEM]
    )


def finish_kernel(layout, slots, aliased, place, *refs):
    run = place[0]
    groups = []
    for number in range(layout[-1]):
        groups.append(refs[4 * number : 4 * number + 4])
    refs = refs[4 * layout[-1] + aliased :]
    qkv, out, up, down = refs
    part, width = out.shape[1], out.shape[2]
    mine, half, size = width // 4, width // 2, up.shape[2] // 4
    piece = size // slots
    (q_group, q_start), (o_group, o_start), (u_group, u_start), (d_group, d_start) = layout[0]
    for j in range(4):
        owner = run ^ j
        for third in range(3):
            lanes = pl.ds(pl.multiple_of(third * width + owner * mine, mine), mine)
            start = q_start + third * mine
            qkv[0, :, lanes] = groups[q_group][j][:, start : start + mine].astype(F32)
        if piece % 128:
            lanes = pl.ds(pl.multiple_of(owner * size, size), size)
            up[0, :, lanes] = groups[u_group][j][:, u_start : u_start + size].astype(F32)
        else:
            for slot in range(slots):
                lanes = pl.ds(pl.multiple_of((4 * slot + owner) * piece, piece), piece)
                start = u_start + slot * piece
                up[0, :, lanes] = groups[u_group][j][:, start : start + piece].astype(F32)
        rows = pl.ds(pl.multiple_of(owner * part, part), part)
        down[0, rows, :] = groups[d_group][j][:, d_start : d_start + width].astype(F32)
    for j in range(2):
        lanes = pl.ds(pl.multiple_of((run ^ j) % 2 * half, half), half)
        columns = slice(o_start, o_start + half)
        first, second = groups[o_group][j][:, columns], groups[o_group][j + 2][:, columns]
        out[0, :, lanes] = first.astype(F32) + second.astype(F32)


def finish(layer, layers, groups, starts, place, before):
    slots = lax.axis_size("fsdp")
    part = groups[0][0].shape[0]
    width = part * slots
    shapes = [(part, 3 * width), (part, width), (part, 4 * width), (4 * part, width)]
    inputs = [place] + [item for group in groups for item in group]
    count = len(inputs)
    specs = [SMEM] + [VMEM] * (count - 1)
    aliases = {}
    if before is not None:
        inputs += before
        specs += [pl.BlockSpec(memory_space=pl.ANY)] * 4
        aliases = {count + i: i for i in range(4)}
    layout = (starts, len(groups))
    return pl.pallas_call(
        functools.partial(finish_kernel, layout, slots, len(aliases)),
        grid=(1,),
        in_specs=specs,
        out_specs=[pl.BlockSpec((1,) + shape, lambda i: (layer, 0, 0)) for shape in shapes],
        out_shape=[jax.ShapeDtypeStruct((layers,) + shape, F32) for shape in shapes],
        input_output_aliases=aliases,
        compiler_params=pltpu.CompilerParams(vmem_limit_bytes=48 << 20),
        cost_estimate=pl.CostEstimate(flops=0, bytes_accessed=0, transcendentals=0),
        name="finish",
    )(*inputs)


def out_back_kernel(
    scalars,
    keep,
    beside,
    across,
    middle,
    grad,
    table,
    w_own,
    w_other,
    grad_middle,
    branch,
    own,
    near,
    far,
    sums,
):
    run = scalars[0]
    core = run % 2
    total = keep[...] + beside[...].astype(F32) + across[...].astype(F32)
    value, grad_gain, grad_shift = norm_back(middle[...], row(table, GAIN_TWO), total)
    value = grad[...] + value
    grad_middle[...] = value
    low = value.astype(BF)
    branch[...] = low
    sums[...] = jnp.zeros_like(sums)
    sums[0:1, :] = grad_gain
    sums[1:2, :] = grad_shift
    sums[2:3, :] = jnp.sum(low.astype(F32), axis=0, keepdims=True)
    sums[3:4, :] = jnp.sum(grad[...].astype(BF).astype(F32), axis=0, keepdims=True)
    size = own.shape[1]
    half = w_own.shape[1]
    for j in range(4):
        rows = pl.ds(pl.multiple_of((run ^ j) * size, size), size)
        result = None
        for weight, place in ((w_own, core), (w_other, 1 - core)):
            lanes = pl.ds(pl.multiple_of(place * half, half), half)
            term = nt(branch[:, lanes], weight[rows, :])
            result = term if result is None else result + term
        result = result.astype(BF)
        if j == 0:
            own[...] = result
        elif j == 2:
            far[...] = result
        else:
            near[j // 2] = result


def out_back(scalars, sums, middle, grad, table, w_outs):
    rows, width = middle.shape
    mine = width // 4
    outs = [
        ((rows, width), F32),
        ((rows, width), BF),
        ((rows, mine), BF),
        ((2, rows, mine), BF),
        ((rows, mine), BF),
        ((8, width), F32),
    ]
    inputs = (scalars, *sums, middle, grad, table, *w_outs)
    return kernel_call(out_back_kernel, "out_back", inputs, outs, in_specs=[SMEM] + [VMEM] * 8)


def layer_begin_kernel(
    keep, beside, across, stream, grad_middle, table, grad, low, sums
):
    total = keep[...] + beside[...].astype(F32) + across[...].astype(F32)
    value, grad_gain, grad_shift = norm_back(stream[...], row(table, GAIN_ONE), total)
    value = grad_middle[...] + value
    grad[...] = value
    low[...] = value.astype(BF)
    sums[...] = jnp.zeros_like(sums)
    sums[0:1, :] = grad_gain
    sums[1:2, :] = grad_shift


def layer_begin(sums, stream, grad_middle, table):
    shape = stream.shape
    outs = [(shape, F32), (shape, BF), ((8, shape[1]), F32)]
    return kernel_call(
        layer_begin_kernel, "layer_begin", (*sums, stream, grad_middle, table), outs
    )


def halves(value, head):
    lane = lax.broadcasted_iota(jnp.int32, value.shape, 1)
    return jnp.where((lane >= HEAD_DIM) == (head == 1), value, jnp.zeros_like(value))


def masked_scores(keys, query, i, j, slope, offsets, length):
    scores = nt(keys, query)
    if i == j:
        scores = scores - slope * jnp.abs(offsets)
    else:
        scores = scores - (slope * offsets + slope * float((i - j) * BLOCK))
    if j == 0:
        return scores, None
    return scores, j * BLOCK + lax.broadcasted_iota(jnp.int32, scores.shape, 0) < length


def block(i):
    return slice(i * BLOCK, (i + 1) * BLOCK)


def distances(ref):
    shape = (BLOCK, BLOCK)
    offsets = lax.broadcasted_iota(jnp.int32, shape, 1) - lax.broadcasted_iota(jnp.int32, shape, 0)
    ref[...] = offsets.astype(F32)


def attend_kernel(
    scalars, slopes, a, b, c, d, w_qkv, bias, nat, att, own, near, far, lse, low, scores, offsets
):
    run, length = scalars[0], scalars[1]
    blocks = nat.shape[0] // BLOCK
    mine = nat.shape[1] // 3
    for j, rows in enumerate((a, b, c, d)):
        place = pl.ds(pl.multiple_of((run ^ j) * BLOCK, BLOCK), BLOCK)
        nat[place, :] = (nn(rows[...], w_qkv[...]) + bias[...]).astype(BF)
    distances(offsets)
    for i in range(blocks):
        for pair in range(mine // 128):
            lanes = slice(pair * 128, (pair + 1) * 128)
            out = jnp.zeros((128, BLOCK), F32)
            for head in range(2):
                slope = slopes[pair * 2 + head]
                query = halves(nat[block(i), lanes], head) * jnp.asarray(HEAD_DIM**-0.5, BF)
                top = None
                for j in range(i + 1):
                    keys = nat[block(j), mine + pair * 128 : mine + (pair + 1) * 128]
                    tile, seen = masked_scores(keys, query, i, j, slope, offsets[...], length)
                    if seen is not None:
                        tile = jnp.where(seen, tile, NEG)
                    scores[block(j), :] = tile
                    tile_top = jnp.max(tile, axis=0, keepdims=True)
                    top = tile_top if top is None else jnp.maximum(top, tile_top)
                total = jnp.zeros((1, BLOCK), F32)
                summed = jnp.zeros((128, BLOCK), F32)
                for j in range(i + 1):
                    weights = jnp.exp(scores[block(j), :] - top)
                    total = total + jnp.sum(weights, axis=0, keepdims=True)
                    values = nat[block(j), 2 * mine + pair * 128 : 2 * mine + (pair + 1) * 128]
                    summed = summed + tn(halves(values, head), weights.astype(BF))
                out = out + summed / total
                lse[pair * 2 + head : pair * 2 + head + 1, block(i)] = top + jnp.log(total)
            rows = jnp.transpose(out)
            att[block(i), lanes] = rows
            low[run ^ i, :, lanes] = rows.astype(BF)
    own[...] = low[0]
    near[...] = low[1]
    far[...] = low[2:4]


def attend_back_kernel(
    scalars,
    slopes,
    nat,
    own,
    beside,
    across,
    att,
    lse,
    w_qkv,
    out,
    near_keep,
    near_send,
    far_keep,
    far_send,
    sums,
    nat_grad,
    grad_q,
    grad_k,
    grad_v,
    offsets,
):
    run, length = scalars[0], scalars[1]
    blocks = nat.shape[0] // BLOCK
    mine = nat.shape[1] // 3
    for j, rows in enumerate((own[...], beside[0], across[0], across[1])):
        place = pl.ds(pl.multiple_of((run ^ j) * BLOCK, BLOCK), BLOCK)
        nat_grad[place, :] = rows
    distances(offsets)
    grad_k[...] = jnp.zeros_like(grad_k)
    grad_v[...] = jnp.zeros_like(grad_v)
    scale = jnp.asarray(HEAD_DIM**-0.5, BF)
    for pair in range(mine // 128):
        lanes = slice(pair * 128, (pair + 1) * 128)
        k_lanes = slice(mine + pair * 128, mine + (pair + 1) * 128)
        v_lanes = slice(2 * mine + pair * 128, 2 * mine + (pair + 1) * 128)
        for i in range(blocks):
            grad_rows = nat_grad[block(i), lanes]
            product = grad_rows.astype(F32) * att[block(i), lanes]
            ones = lax.broadcasted_iota(jnp.int32, (8, 128), 1) // HEAD_DIM
            ones = (ones == lax.broadcasted_iota(jnp.int32, (8, 128), 0)).astype(F32)
            delta = lax.dot_general(
                ones,
                product,
                (((1,), (1,)), ((), ())),
                precision=lax.Precision.HIGHEST,
                preferred_element_type=F32,
            )
            sum_q = jnp.zeros((128, BLOCK), F32)
            for head in range(2):
                number = pair * 2 + head
                slope = slopes[number]
                query = halves(nat[block(i), lanes], head) * scale
                grad_head = halves(grad_rows, head)
                row_lse = lse[number : number + 1, block(i)]
                row_delta = delta[head : head + 1, :]
                for j in range(i + 1):
                    keys = nat[block(j), k_lanes]
                    tile, seen = masked_scores(keys, query, i, j, slope, offsets[...], length)
                    probs = jnp.exp(tile - row_lse)
                    if seen is not None:
                        probs = jnp.where(seen, probs, 0.0)
                    grad_probs = nt(nat[block(j), v_lanes], grad_head)
                    grad_scores = (probs * (grad_probs - row_delta)).astype(BF)
                    grad_v[block(j), lanes] += nn(probs.astype(BF), grad_head)
                    grad_k[block(j), lanes] += nn(grad_scores, query)
                    sum_q = sum_q + tn(halves(keys, head), grad_scores)
            grad_q[block(i), lanes] = (jnp.transpose(sum_q) * HEAD_DIM**-0.5).astype(BF)
    sums[...] = jnp.zeros_like(sums)
    for j in range(4):
        place = pl.ds(pl.multiple_of((run ^ j) * BLOCK, BLOCK), BLOCK)
        out[block(j), :mine] = grad_q[place, :]
        out[block(j), mine : 2 * mine] = grad_k[place, :].astype(BF)
        out[block(j), 2 * mine :] = grad_v[place, :].astype(BF)
        rows = out[block(j), :]
        sums[0:1, :] += jnp.sum(rows.astype(F32), axis=0, keepdims=True)
        partial = nt(rows, w_qkv[...])
        if j == 0:
            near_keep[...] = partial
        elif j == 1:
            near_send[...] = partial.astype(BF)
        elif j == 2:
            far_keep[...] = partial
        else:
            far_send[...] = partial.astype(BF)


def attend(blocks, w_qkv, bias, scalars, slopes):
    rows, width = blocks[0].shape
    columns = w_qkv.shape[1]
    mine = columns // 3
    outs = [
        ((4 * rows, columns), BF),
        ((4 * rows, mine), F32),
        ((rows, mine), BF),
        ((rows, mine), BF),
        ((2, rows, mine), BF),
        ((8, 4 * rows), F32),
    ]
    scratch = [
        pltpu.VMEM((4, rows, mine), BF),
        pltpu.VMEM((4 * rows, BLOCK), F32),
        pltpu.VMEM((BLOCK, BLOCK), F32),
    ]
    inputs = (scalars, slopes, *blocks, w_qkv, bias)
    specs = [SMEM, SMEM] + [VMEM] * 6
    return kernel_call(attend_kernel, "attend", inputs, outs, scratch, specs)


def attend_back(nat, own, beside, across, att, lse, w_qkv, scalars, slopes):
    total, columns = nat.shape
    rows, mine = total // 4, columns // 3
    width = w_qkv.shape[0]
    outs = [
        ((total, columns), BF),
        ((rows, width), F32),
        ((rows, width), BF),
        ((rows, width), F32),
        ((rows, width), BF),
        ((8, columns), F32),
    ]
    scratch = [
        pltpu.VMEM((total, mine), BF),
        pltpu.VMEM((total, mine), BF),
        pltpu.VMEM((total, mine), F32),
        pltpu.VMEM((total, mine), F32),
        pltpu.VMEM((BLOCK, BLOCK), F32),
    ]
    inputs = (scalars, slopes, nat, own, beside, across, att, lse, w_qkv)
    specs = [SMEM, SMEM] + [VMEM] * 7
    return kernel_call(attend_back_kernel, "attend_back", inputs, outs, scratch, specs)


def shards(
    tokens,
    lengths,
    cotangent,
    ln1_gain,
    ln1_bias,
    qkv_weight,
    query_bias,
    value_bias,
    out_weight,
    out_bias,
    ln2_gain,
    ln2_bias,
    up_weight,
    up_bias,
    down_weight,
    down_bias,
):
    fsdp = lax.axis_size("fsdp")
    run = lax.axis_index("seq")
    rows, width = tokens.shape[1:]
    hidden = up_weight.shape[2]
    heads = HEADS // 4
    mine = width // 4
    half = width // 2
    ffn_size = hidden // 4
    part = width // fsdp
    piece = hidden // fsdp // 4
    me = lax.axis_index("fsdp")
    scalars = jnp.stack([run.astype(jnp.int32), lengths[0]])
    place = jnp.stack([run, me % 2]).astype(jnp.int32)
    slopes = lax.dynamic_slice_in_dim(head_slopes(), run * heads, heads)

    def quarter(value, axis):
        size = value.shape[axis] // 4
        return lax.dynamic_slice_in_dim(value, run * size, size, axis)

    def core_half(value, axis):
        return lax.dynamic_slice_in_dim(value, (run % 2) * half, half, axis)

    def qkv_of(layer):
        return quarter(qkv_weight[layer].reshape(part, 3, width), 2).reshape(part, 3 * mine)

    def out_of(layer):
        return core_half(out_weight[layer], 1)

    def up_of(layer):
        return quarter(up_weight[layer].reshape(part, fsdp, -1), 2).reshape(part, ffn_size)

    def down_of(layer):
        return quarter(down_weight[layer], 0)

    def seq_blocks(own):
        across = y_swap(own)
        return [own, core_swap(own), across, core_swap(across)]

    def summed(near, far):
        far = far_sum(far)
        return near[0], core_swap(near[1]), y_swap(far)

    def far_sum(far):
        return (far[0] + core_swap(far[1]).astype(F32)).astype(BF)

    vectors = (ln1_gain, ln1_bias, query_bias, value_bias, out_bias, ln2_gain, ln2_bias, down_bias)
    small = jnp.concatenate([jnp.stack(vectors, 1).reshape(LAYERS, -1), up_bias], axis=1)
    columns = 3 * mine
    extra = small.size // columns
    small = jnp.pad(small.reshape(extra, columns), ((0, -extra % 16), (0, 0)))
    stride = part + small.shape[0]
    own = pack(["qkv", "small"], [qkv_weight, small], 0, place, stride, columns)
    token_blocks = seq_blocks(tokens[0])
    even = [own] + [hop(own, "fsdp", 2 * k) for k in range(1, fsdp // 2)]
    first = jnp.concatenate(even)
    first = (first, x_swap(first))
    cot_blocks = seq_blocks(tied(cotangent[0], token_blocks[2]))
    token_blocks, cot_blocks, first = meet(token_blocks, cot_blocks, first)
    arrays = dict(qkv=qkv_weight, out=out_weight, up=up_weight, down=down_weight)
    sizes = dict(qkv=columns, out=half, up=ffn_size, down=width)

    def bundle(layer, names):
        if part % 128:
            parts = dict(qkv=qkv_of, out=out_of, up=up_of, down=down_of)
            return jnp.concatenate([parts[name](layer) for name in names], axis=1)
        total = sum(sizes[name] for name in names)
        return pack(names, [arrays[name] for name in names], layer, place, part, total)

    packs = [
        bundle(0, ["out", "up"]),
        bundle(0, ["down"]),
        bundle(1, ["qkv", "out"]),
        bundle(1, ["up", "down"]),
    ]
    token_blocks = tied(token_blocks, packs)
    early_one, late_one, early_two, late_two = (gather_z(item) for item in packs)

    def matrix(halves, column, size, key=me % 2):
        return assemble(halves, column, size, part, key)

    small = [item.reshape(fsdp // 2, stride, columns)[:, part : part + extra] for item in first]
    small = jnp.stack(small, 1).reshape(fsdp, LAYERS, -1)
    small = jnp.take(small, me ^ jnp.arange(fsdp), axis=0).astype(F32)
    tables, biases = [], []
    for layer in range(LAYERS):
        table = small[:, layer, : 8 * part].reshape(fsdp, 8, part)
        table = jnp.transpose(table, (1, 0, 2)).reshape(8, width)
        bias_q, bias_v = quarter(table[BIAS_Q], 0), quarter(table[BIAS_V], 0)
        bias_qkv = jnp.concatenate([bias_q, jnp.zeros_like(bias_q), bias_v])
        bias_up = quarter(small[:, layer, 8 * part :], 1)
        tables.append(table)
        biases.append((bias_qkv.reshape(1, -1), bias_up.reshape(1, -1)))

    stream = tokens[0].astype(F32)
    h1 = first_norm(token_blocks, tables[0])
    w_qkv = assemble(first, 0, columns, part, me)
    moved = x_swap(tied(early_one, first))
    saved, weights = [], []
    for layer in range(LAYERS):
        top = layer + 1 == LAYERS
        bias_qkv, bias_up = biases[layer]
        packed, attended, own, near, far, lse = attend(h1, w_qkv, bias_qkv, scalars, slopes)
        across = y_swap(far)
        if top:
            across, moved = meet(across, moved)
            late_two = (late_two, moved)
            w_out = matrix(early_two, columns, half)
            w_up, w_down = matrix(late_two, 0, ffn_size), matrix(late_two, ffn_size, width)
        else:
            across, moved, late_one = meet(across, moved, late_one)
            early_one = (early_one, moved)
            w_out, w_up = matrix(early_one, 0, half), matrix(early_one, half, ffn_size)
            moved = x_swap(late_one)
        beside = core_swap(jnp.stack([near, across[1]]))
        w_outs = (w_out, core_swap(w_out))
        middle, normed, att_own = out_step(
            scalars, own, beside, across, w_outs, stream, tables[layer]
        )
        h2 = seq_blocks(normed)
        if not top:
            h2[2], moved, early_two = meet(h2[2], moved, early_two)
            w_down = matrix((late_one, moved), 0, width)
            moved = x_swap(early_two)
            h2[3] = core_swap(h2[2])
        near = ffn(h2[0], h2[1], w_up, bias_up, w_down)
        if top:
            h2[2], near = meet(h2[2], near)
            h2[3] = core_swap(h2[2])
        far = ffn(h2[2], h2[3], w_up, bias_up, w_down)
        saved.append((stream, h1, packed, attended, lse, att_own, middle, h2, near[:2], far[:2]))
        weights.append((w_qkv, w_outs, w_up, w_down))
        if top:
            last_sums = near[2:], far[2:]
        else:
            sums, moved, late_two = meet(summed(near[2:], far[2:]), moved, late_two)
            early_two = (early_two, moved)
            w_qkv = matrix(early_two, 0, columns)
            moved = x_swap(late_two)
            stream, normed = layer_end(middle, sums, tables[layer], tables[layer + 1])
            h1 = seq_blocks(normed)

    grad = cotangent[0].astype(F32)
    g_down = cot_blocks
    vectors = [None] * LAYERS
    upper, lower = [], []
    waiting = None
    for layer in reversed(range(LAYERS)):
        top = layer + 1 == LAYERS
        totals = upper if top else lower
        w_qkv, w_outs, w_up, w_down = weights[layer]
        stream, h1, packed, attended, lse, att_own, middle, h2, act_near, act_far = saved[layer]
        near = ffn_back(g_down[0], g_down[1], act_near[1], w_up, w_down)
        if not top:
            g_down[2], near, waiting, reduced, upper[1] = meet(
                g_down[2], near, waiting, reduced, upper[1]
            )
            g_down[3] = core_swap(g_down[2])
            reduced = added(*waiting)
            upper.append(scatter_z(reduced))
        far = ffn_back(g_down[2], g_down[3], act_far[1], w_up, w_down)
        far_low = far_sum(far[1:3])
        acts, h2_late = tied(([act_near[0], act_far[0]], h2), far_low if not top else near)
        sent_down = weight_grad(acts, g_down, place)
        moved_down = x_swap(sent_down[1])
        sent_up = weight_grad(h2_late, [near[0], far[0]], place)
        sums = near[1], core_swap(near[2]), y_swap(far_low)
        if not top:
            sums = tied(sums, (reduced, upper[2]))
        sums, sent_up = meet(sums, sent_up)
        moved_up = x_swap(sent_up[1])
        grad_middle, g_branch, own, near_att, far_att, lines_two = out_back(
            scalars, sums, middle, grad, tables[layer], w_outs
        )
        beside = core_swap(near_att)
        across = jnp.stack([far_att, beside[1]])
        att_late, branch_late = tied((att_own, g_branch), across)
        across = y_swap(across)
        keep, send = out_grad(att_late, branch_late, place)
        sent_out = added(keep, core_swap(send))
        across, moved, sent_out = meet(across, moved_down, sent_out)
        reduced = added(sent_down[0], moved)
        totals.append(scatter_z(reduced))
        moved_out = x_swap(sent_out[1])
        if not top:
            across = tied(across, upper[3])
        g_packed, *parts, packed_sum = attend_back(
            packed, own, beside, across, attended, lse, w_qkv, scalars, slopes
        )
        if top:
            one, two = tied(last_sums, across)
            last_sums = summed(one, two)
            parts, moved, last_sums, reduced = meet(parts, moved_up, last_sums, reduced)
            result = layer_end(saved[layer][6], last_sums, tables[layer], None)[1]
        else:
            parts, moved, reduced = meet(parts, moved_up, reduced)
        reduced = added(sent_up[0], moved)
        totals.append(scatter_z(reduced))
        far_low = far_sum(parts[2:])
        sent_qkv = weight_grad(tied(h1, far_low), [g_packed], place)
        sums = parts[0], core_swap(parts[1]), y_swap(far_low)
        sums = tied(sums, (sent_qkv, reduced, totals[0]))
        sums, moved = meet(sums, moved_out)
        reduced = added(sent_out[0], moved)
        totals.append(scatter_z(reduced))
        waiting = sent_qkv[0], x_swap(sent_qkv[1])
        if not top:
            totals.append(scatter_z(added(*waiting)))
        up_sum = near[3] + far[3]
        grad, normed, lines_one = layer_begin(sums, stream, grad_middle, tables[layer])
        if layer:
            g_down = seq_blocks(normed)

        vectors[layer] = (lines_two, lines_two, packed_sum, lines_one, up_sum)

    def spread(value, axis=0):
        shape = list(value.shape)
        size = shape[axis]
        shape[axis] = 4 * size
        return lax.dynamic_update_slice_in_dim(jnp.zeros(shape, F32), value, run * size, axis)

    small_sums = []
    for _, lines_two, packed_sum, lines_one, up_sum in tied(vectors, grad):
        members = [
            lines_one[0],
            lines_one[1],
            spread(packed_sum[0, :mine]),
            spread(packed_sum[0, 2 * mine :]),
            lines_two[2],
            lines_two[0],
            lines_two[1],
            lines_two[3],
        ]
        small_sums.append(
            jnp.concatenate(
                [item.reshape(fsdp, part) for item in members]
                + [spread(up_sum.reshape(fsdp, piece), 1)],
                axis=1,
            )
        )

    upper = [four(item) for item in tied(upper, grad)]
    starts = ((3, 0), (2, 0), (1, 0), (0, 0))
    matrices = finish(1, LAYERS, upper, starts, place, None)
    lower[3] = tied(lower[3], matrices)
    lower = [four(item) for item in lower]
    matrices = finish(0, LAYERS, lower, starts, place, matrices)
    grad_qkv_w, grad_out_w, grad_up_w, grad_down_w = matrices
    if piece % 128:
        grad_up_w = grad_up_w.reshape(LAYERS, part, 4, fsdp, piece)
        grad_up_w = jnp.swapaxes(grad_up_w, 2, 3).reshape(LAYERS, part, hidden)
    vector = sum_small(jnp.stack(small_sums, axis=1))
    lines = [vector[:, i * part : (i + 1) * part] for i in range(8)]
    gain_one, shift_one, bias_q, bias_v, bias_o, gain_two, shift_two, bias_down = lines
    return (
        result[None],
        grad[None],
        gain_one,
        shift_one,
        grad_qkv_w,
        bias_q,
        bias_v,
        grad_out_w,
        bias_o,
        gain_two,
        shift_two,
        grad_up_w,
        vector[:, 8 * part :],
        grad_down_w,
        bias_down,
    )


def solution(mesh):
    vector = P(None, "fsdp")
    matrix = P(None, "fsdp", None)
    data = P("fsdp", "seq", None)
    weight_specs = (
        vector,
        vector,
        matrix,
        vector,
        vector,
        matrix,
        vector,
        vector,
        vector,
        matrix,
        vector,
        matrix,
        vector,
    )
    in_specs = (data, P("fsdp"), data) + weight_specs
    out_specs = (data, data) + weight_specs
    return jax.shard_map(shards, mesh=mesh, in_specs=in_specs, out_specs=out_specs, check_vma=False)
```

```python
import functools

import jax
import jax.numpy as jnp
from jax import lax
from jax.experimental import pallas as pl
from jax.experimental.pallas import tpu as pltpu
from jax.sharding import PartitionSpec as P

HEADS = 16
HEAD_DIM = 64
LAYERS = 2
BLOCK = 256
EPS = 1e-05
NEG = -1e30
BF = jnp.bfloat16
F32 = jnp.float32
GELU = 0.7978845608028654
CUBIC = 0.044715
VMEM = pl.BlockSpec(memory_space=pltpu.VMEM)
SMEM = pl.BlockSpec(memory_space=pltpu.SMEM)


def head_slopes():
    return jnp.exp2(-8.0 * (jnp.arange(HEADS, dtype=F32) + 1.0) / HEADS)


def hop(value, axis, mask):
    size = lax.axis_size(axis)
    return lax.ppermute(value, axis, [(i, i ^ mask) for i in range(size)])


def core_swap(value):
    return hop(value, "seq", 1)


def y_swap(value):
    return hop(value, "seq", 2)


def sum_small(full):
    size = lax.axis_size("fsdp")
    me = lax.axis_index("fsdp")
    full = full + y_swap(full)
    full = full + core_swap(full)
    slots = jnp.take(full, me ^ jnp.arange(size), axis=0)
    slots = slots.reshape((size // 2, 2) + full.shape[1:])
    slots = slots[:, 0] + hop(slots[:, 1], "fsdp", 1)
    total = slots[0]
    for k in range(1, size // 2):
        total = total + hop(slots[k], "fsdp", 2 * k)
    return total


def assemble_kernel(column, stride, key_ref, same, other, out, held, sems):
    key = key_ref[0]
    pairs, rows, width = held.shape[0] // 2, held.shape[1], held.shape[2]
    loads, stores = [], []
    for r in range(2 * pairs):
        place = pl.ds(r // 2 * stride, rows)
        source = (other if r % 2 else same).at[place, pl.ds(column, width)]
        loads.append(pltpu.make_async_copy(source, held.at[r], sems.at[r, 0]))
        start = pl.multiple_of((r ^ key) * rows, rows)
        target = out.at[pl.ds(start, rows), :]
        stores.append(pltpu.make_async_copy(held.at[r], target, sems.at[r, 1]))
    for load in loads:
        load.start()
    for load, store in zip(loads, stores):
        load.wait()
        store.start()
    for store in stores:
        store.wait()


def assemble(halves, column, width, rows, key):
    slots = lax.axis_size("fsdp")
    stride = 2 * halves[0].shape[0] // slots
    key = key.astype(jnp.int32).reshape(1)
    hbm = pl.BlockSpec(memory_space=pl.ANY)
    return pl.pallas_call(
        functools.partial(assemble_kernel, column, stride),
        grid_spec=pltpu.PrefetchScalarGridSpec(
            num_scalar_prefetch=1,
            grid=(),
            in_specs=[hbm] * 2,
            out_specs=hbm,
            scratch_shapes=[
                pltpu.VMEM((slots, rows, width), BF),
                pltpu.SemaphoreType.DMA((slots, 2)),
            ],
        ),
        out_shape=jax.ShapeDtypeStruct((slots * rows, width), BF),
        compiler_params=pltpu.CompilerParams(vmem_limit_bytes=32 << 20),
        cost_estimate=pl.CostEstimate(flops=0, bytes_accessed=0, transcendentals=0),
        name="assemble",
    )(key, *halves)


def tied(value, after):
    return lax.optimization_barrier((value, after))[0]


def meet(*values):
    return lax.optimization_barrier(values)


def pack_kernel(names, layer, place, *refs):
    sources, (out, sems) = dict(zip(names, refs)), refs[len(names) :]
    run = place[0]
    copies = []
    column = 0

    def add(source, size, rows=None):
        rows = source.shape[0] if rows is None else rows
        target = out.at[pl.ds(0, rows), pl.ds(column, size)]
        copies.append(pltpu.make_async_copy(source, target, sems.at[len(copies)]))
        return column + size

    for name in names:
        source = sources[name]
        if name == "small":
            rows = source.shape[0]
            target = out.at[pl.ds(out.shape[0] - rows, rows), :]
            copies.append(pltpu.make_async_copy(source, target, sems.at[len(copies)]))
            continue
        source = source.at[layer]
        part, width = source.shape
        if name == "qkv":
            for third in range(3):
                start = pl.multiple_of((4 * third + run) * (width // 12), width // 12)
                column = add(source.at[:, pl.ds(start, width // 12)], width // 12)
        elif name == "out":
            start = pl.multiple_of(run % 2 * (width // 2), width // 2)
            column = add(source.at[:, pl.ds(start, width // 2)], width // 2)
        elif name == "up":
            piece = part
            for slot in range(width // (4 * piece)):
                start = pl.multiple_of((4 * slot + run) * piece, piece)
                column = add(source.at[:, pl.ds(start, piece)], piece)
        else:
            start = pl.multiple_of(run * (part // 4), part // 4)
            column = add(source.at[pl.ds(start, part // 4), :], width)
    for copy in copies:
        copy.start()
    for copy in copies:
        copy.wait()


def pack(names, arrays, layer, place, rows, columns):
    count = sum({"qkv": 3, "up": arrays[0].shape[-1]}.get(name, 1) for name in names)
    hbm = pl.BlockSpec(memory_space=pl.ANY)
    return pl.pallas_call(
        functools.partial(pack_kernel, names, layer),
        in_specs=[SMEM] + [hbm] * len(arrays),
        out_specs=VMEM,
        out_shape=jax.ShapeDtypeStruct((rows, columns), BF),
        scratch_shapes=[pltpu.SemaphoreType.DMA((min(count, 64),))],
        compiler_params=pltpu.CompilerParams(vmem_limit_bytes=32 << 20),
        cost_estimate=pl.CostEstimate(flops=0, bytes_accessed=0, transcendentals=0),
        name="pack",
    )(place, *arrays)


def z_groups():
    size = lax.axis_size("fsdp")
    return [[x + 2 * k for k in range(size // 2)] for x in range(2)]


def gather_z(own):
    return lax.all_gather(own, "fsdp", axis=0, tiled=True, axis_index_groups=z_groups())


def x_swap(value):
    return hop(value, "fsdp", 1)


def scatter_z(same):
    return lax.psum_scatter(
        same, "fsdp", scatter_dimension=0, tiled=True, axis_index_groups=z_groups()
    )


def four(total):
    across = y_swap(total)
    return total, core_swap(total), across, core_swap(across)


class Slots:
    def __init__(self, halves, column, width, rows, keys, key):
        self.halves, self.column, self.width, self.rows = halves, column, width, rows
        self.keys, self.key = keys, key

    def copies(self, keys, same, other, buffer):
        count = buffer.shape[0] // self.rows
        stride = 2 * same.shape[0] // count
        for r in range(count):
            source = other if r % 2 else same
            source = source.at[pl.ds(r // 2 * stride, self.rows), pl.ds(self.column, self.width)]
            start = pl.multiple_of((r ^ keys[self.key]) * self.rows, self.rows)
            yield source, buffer.at[pl.ds(start, self.rows), :]


def staged(body, plan, refs):
    refs = list(refs)
    keys = refs.pop(0) if any(isinstance(item, Slots) for item in plan) else None
    taken = [refs.pop(0) for item in plan for _ in range(1 + isinstance(item, Slots))]
    sems = refs.pop()
    places = [i for i, item in enumerate(plan) if item is not None]
    buffers = refs[len(refs) - len(places) :]
    refs = refs[: len(refs) - len(places)]
    inputs, copies = [], []
    for item in plan:
        if item is None:
            inputs.append(taken.pop(0))
            continue
        buffer = buffers.pop(0)
        inputs.append(buffer)
        if item is VMEM:
            moves = [(taken.pop(0), buffer)]
        else:
            moves = item.copies(keys, taken.pop(0), taken.pop(0), buffer)
        for source, target in moves:
            copies.append(pltpu.make_async_copy(source, target, sems.at[len(copies)]))
    for copy in copies:
        copy.start()
    for copy in copies:
        copy.wait()
    body(*inputs, *refs)


def kernel_call(body, name, inputs, outputs, scratch=(), in_specs=None, cost=0):
    plan, arrays, specs, buffers, keys = [], [], [], [], None
    count = 1
    hbm = pl.BlockSpec(memory_space=pl.ANY)
    for item, spec in zip(inputs, in_specs or [VMEM] * len(inputs)):
        if isinstance(item, Slots):
            shape = (lax.axis_size("fsdp") * item.rows, item.width)
            plan.append(item)
            arrays += item.halves
            specs += [hbm, hbm]
            buffers.append(pltpu.VMEM(shape, BF))
            keys = item.keys
            count += lax.axis_size("fsdp")
            continue
        arrays.append(item)
        plan.append(VMEM if spec is VMEM else None)
        specs.append(hbm if spec is VMEM else SMEM)
        if spec is VMEM:
            buffers.append(pltpu.VMEM(item.shape, item.dtype))
            count += 1
    if keys is not None:
        arrays, specs = [keys] + arrays, [SMEM] + specs
    return pl.pallas_call(
        lambda *refs: staged(body, plan, refs),
        in_specs=specs,
        out_specs=[VMEM] * len(outputs),
        out_shape=[jax.ShapeDtypeStruct(shape, kind) for shape, kind in outputs],
        scratch_shapes=[*scratch, *buffers, pltpu.SemaphoreType.DMA((count,))],
        compiler_params=pltpu.CompilerParams(vmem_limit_bytes=48 << 20),
        cost_estimate=pl.CostEstimate(flops=0, bytes_accessed=cost, transcendentals=0),
        name=name,
    )(*arrays)


def pair_kernel(keep, received, same, other):
    for i, target in enumerate((same, other)):
        target[...] = (keep[i].astype(F32) + received[i].astype(F32)).astype(BF)


def added_pair(keep, received):
    outs = [(keep.shape[1:], BF)] * 2
    return kernel_call(pair_kernel, "added_pair", (keep, received), outs)


def add_kernel(same, *refs):
    out = refs[-1]
    start = 0
    for item in refs[:-1]:
        rows = slice(start, start + item.shape[0])
        out[rows, :] = (same[rows, :].astype(F32) + item[...].astype(F32)).astype(BF)
        start += item.shape[0]


def added(same, *received):
    return kernel_call(add_kernel, "added", (same, *received), [(same.shape, BF)])[0]


def nn(left, right):
    return jnp.dot(left, right, preferred_element_type=F32)


def nt(left, right):
    return lax.dot_general(left, right, (((1,), (1,)), ((), ())), preferred_element_type=F32)


def tn(left, right):
    return lax.dot_general(left, right, (((0,), (0,)), ((), ())), preferred_element_type=F32)


def normalized(value):
    center = value - jnp.mean(value, axis=-1, keepdims=True)
    scale = lax.rsqrt(jnp.mean(center * center, axis=-1, keepdims=True) + EPS)
    return center * scale, scale


def norm_back(value, gain, grad):
    hat, scale = normalized(value)
    inner = grad * gain
    mean = jnp.mean(inner, axis=-1, keepdims=True)
    along = jnp.mean(inner * hat, axis=-1, keepdims=True)
    grad_gain = jnp.sum(grad * hat, axis=0, keepdims=True)
    return scale * (inner - mean - hat * along), grad_gain, jnp.sum(grad, axis=0, keepdims=True)


GAIN_ONE, SHIFT_ONE, BIAS_Q, BIAS_V, BIAS_OUT, GAIN_TWO, SHIFT_TWO, BIAS_DOWN = range(8)


def row(table, index):
    return table[index : index + 1, :]


def first_norm_kernel(a, b, c, d, table, *outs):
    for value, out in zip((a, b, c, d), outs):
        hat, _ = normalized(value[...].astype(F32))
        out[...] = (hat * row(table, GAIN_ONE) + row(table, SHIFT_ONE)).astype(BF)


def first_norm(blocks, table):
    outs = [(item.shape, BF) for item in blocks]
    return kernel_call(first_norm_kernel, "first_norm", (*blocks, table), outs)


def layer_end_kernel(middle, keep, beside, across, table, after, stream, normed):
    total = keep[...] + beside[...].astype(F32) + across[...].astype(F32)
    value = middle[...] + (total + row(table, BIAS_DOWN))
    stream[...] = value
    if after is None:
        normed[...] = value.astype(BF)
    else:
        hat, _ = normalized(value)
        normed[...] = (hat * row(after, GAIN_ONE) + row(after, SHIFT_ONE)).astype(BF)


def last_end_kernel(middle, keep, beside, across, table, stream, low):
    layer_end_kernel(middle, keep, beside, across, table, None, stream, low)


def layer_end(middle, sums, table, after):
    outs = [(middle.shape, F32), (middle.shape, BF)]
    if after is None:
        return kernel_call(last_end_kernel, "last_end", (middle, *sums, table), outs)
    return kernel_call(layer_end_kernel, "layer_end", (middle, *sums, table, after), outs)


def out_kernel(
    scalars, own, beside, across, far, w_own, w_other, stream, table, middle, normed, attended
):
    run = scalars[0]
    core = run % 2
    parts = [own[...], beside[...], across[...], far[...]]
    size = parts[0].shape[1]
    starts = [pl.multiple_of((run ^ j) * size, size) for j in range(4)]
    for part, start in zip(parts, starts):
        attended[:, pl.ds(start, size)] = part
    half = w_own.shape[1]
    for weight, place in ((w_own, core), (w_other, 1 - core)):
        total = None
        for part, start in zip(parts, starts):
            term = nn(part, weight[pl.ds(start, size), :])
            total = term if total is None else total + term
        lanes = pl.ds(pl.multiple_of(place * half, half), half)
        bias = table[BIAS_OUT : BIAS_OUT + 1, lanes]
        middle[:, lanes] = stream[:, lanes] + (total + bias)
    hat, _ = normalized(middle[...])
    normed[...] = (hat * row(table, GAIN_TWO) + row(table, SHIFT_TWO)).astype(BF)


def out_step(scalars, parts, w_outs, stream, table):
    outs = [(stream.shape, F32), (stream.shape, BF), (stream.shape, BF)]
    inputs = (scalars, *parts, *w_outs, stream, table)
    return kernel_call(out_kernel, "out_step", inputs, outs, in_specs=[SMEM] + [VMEM] * 8)


def ffn_kernel(a, b, w_up, bias, w_down, act, slope, keep, send, source):
    rows = a.shape[0]
    source[:rows, :] = a[...]
    source[rows:, :] = b[...]
    pre = nn(source[...], w_up[...]) + bias[...]
    square = pre * pre
    bent = jnp.tanh(GELU * pre * (1.0 + CUBIC * square))
    half = 0.5 + 0.5 * bent
    value = (pre * half).astype(BF)
    act[...] = value
    rise = half + (0.5 * GELU) * pre * (1.0 - bent * bent) * (1.0 + 3.0 * CUBIC * square)
    slope[...] = rise.astype(BF)
    total = nn(value, w_down[...])
    keep[...] = total[:rows, :]
    send[...] = total[rows:, :].astype(BF)


def ffn(a, b, w_up, bias, w_down):
    rows, width = a.shape
    hidden = w_up.width
    outs = [
        ((2 * rows, hidden), BF),
        ((2 * rows, hidden), BF),
        ((rows, width), F32),
        ((rows, width), BF),
    ]
    scratch = [pltpu.VMEM((2 * rows, width), BF)]
    return kernel_call(ffn_kernel, "ffn", (a, b, w_up, bias, w_down), outs, scratch)


def ffn_back_kernel(a, b, slope, w_up, w_down, grad_pre, keep, send, sums, source):
    rows = a.shape[0]
    source[:rows, :] = a[...]
    source[rows:, :] = b[...]
    grad_act = nt(source[...], w_down[...])
    value = (grad_act * slope[...].astype(F32)).astype(BF)
    grad_pre[...] = value
    sums[...] = jnp.sum(value.astype(F32), axis=0, keepdims=True)
    total = nt(value, w_up[...])
    keep[...] = total[:rows, :]
    send[...] = total[rows:, :].astype(BF)


def ffn_back(a, b, slope, w_up, w_down):
    rows, width = a.shape
    hidden = w_up.width
    outs = [
        ((2 * rows, hidden), BF),
        ((rows, width), F32),
        ((rows, width), BF),
        ((1, hidden), F32),
    ]
    scratch = [pltpu.VMEM((2 * rows, width), BF)]
    return kernel_call(ffn_back_kernel, "ffn_back", (a, b, slope, w_up, w_down), outs, scratch)


def weight_grad_kernel(count, parts, scalars, *refs):
    x = scalars[1]
    lefts, rights = refs[: parts[0]], refs[parts[0] : parts[0] + parts[1]]
    same, *others, left, right, total = refs[parts[0] + parts[1] :]
    for sources, target in ((lefts, left), (rights, right)):
        start = 0
        for source in sources:
            target[start : start + source.shape[0], :] = source[...]
            start += source.shape[0]
    total[...] = tn(left[...], right[...]).astype(BF)
    rows = total.shape[0] // count
    each = count // 2 // len(others)
    for r in range(count):
        start = pl.multiple_of((r ^ x) * rows, rows)
        target = others[r // 2 // each] if r % 2 else same
        slot = r // 2 % each if r % 2 else r // 2
        target[slot * rows : (slot + 1) * rows, :] = total[pl.ds(start, rows), :]


def weight_grad(lefts, rights, place, cuts):
    count = lax.axis_size("fsdp")
    total = sum(item.shape[0] for item in lefts)
    tall, wide = lefts[0].shape[1], rights[0].shape[1]
    outs = [((tall // 2, wide), BF)] + [((tall // 2 // cuts, wide), BF)] * cuts
    scratch = [
        pltpu.VMEM((total, tall), BF),
        pltpu.VMEM((total, wide), BF),
        pltpu.VMEM((tall, wide), BF),
    ]
    inputs = (place, *lefts, *rights)
    body = functools.partial(weight_grad_kernel, count, (len(lefts), len(rights)))
    specs = [SMEM] + [VMEM] * (len(inputs) - 1)
    return list(kernel_call(body, "weight_grad", inputs, outs, scratch, specs))


def out_grad_kernel(count, place, left, right, keep, send, total):
    core, x = place[0] % 2, place[1]
    half = keep.shape[2]
    rows = total.shape[0] // count
    for target, number in ((keep, core), (send, 1 - core)):
        lanes = pl.ds(pl.multiple_of(number * half, half), half)
        total[...] = tn(left[...], right[:, lanes]).astype(BF)
        for r in range(count):
            start = pl.multiple_of((r ^ x) * rows, rows)
            target[r % 2, r // 2 * rows : (r // 2 + 1) * rows, :] = total[pl.ds(start, rows), :]


def out_grad(left, right, place):
    count = lax.axis_size("fsdp")
    tall, wide = left.shape[1], right.shape[1]
    outs = [((2, tall // 2, wide // 2), BF)] * 2
    scratch = [pltpu.VMEM((tall, wide // 2), BF)]
    body = functools.partial(out_grad_kernel, count)
    return kernel_call(
        body, "out_grad", (place, left, right), outs, scratch, [SMEM, VMEM, VMEM]
    )


def finish_kernel(layout, slots, aliased, place, *refs):
    run = place[0]
    groups = []
    for number in range(layout[-1]):
        groups.append(refs[4 * number : 4 * number + 4])
    refs = refs[4 * layout[-1] + aliased :]
    qkv, out, up, down = refs
    part, width = out.shape[1], out.shape[2]
    mine, half, size = width // 4, width // 2, up.shape[2] // 4
    piece = size // slots
    (q_group, q_start), (o_group, o_start), (u_group, u_start), (d_group, d_start) = layout[0]
    for j in range(4):
        owner = run ^ j
        for third in range(3):
            lanes = pl.ds(pl.multiple_of(third * width + owner * mine, mine), mine)
            start = q_start + third * mine
            qkv[0, :, lanes] = groups[q_group][j][:, start : start + mine].astype(F32)
        if piece % 128:
            lanes = pl.ds(pl.multiple_of(owner * size, size), size)
            up[0, :, lanes] = groups[u_group][j][:, u_start : u_start + size].astype(F32)
        else:
            for slot in range(slots):
                lanes = pl.ds(pl.multiple_of((4 * slot + owner) * piece, piece), piece)
                start = u_start + slot * piece
                up[0, :, lanes] = groups[u_group][j][:, start : start + piece].astype(F32)
        rows = pl.ds(pl.multiple_of(owner * part, part), part)
        down[0, rows, :] = groups[d_group][j][:, d_start : d_start + width].astype(F32)
    for j in range(2):
        lanes = pl.ds(pl.multiple_of((run ^ j) % 2 * half, half), half)
        columns = slice(o_start, o_start + half)
        first, second = groups[o_group][j][:, columns], groups[o_group][j + 2][:, columns]
        out[0, :, lanes] = first.astype(F32) + second.astype(F32)


def finish(layer, layers, groups, starts, place, before):
    slots = lax.axis_size("fsdp")
    part = groups[0][0].shape[0]
    width = part * slots
    shapes = [(part, 3 * width), (part, width), (part, 4 * width), (4 * part, width)]
    inputs = [place] + [item for group in groups for item in group]
    count = len(inputs)
    specs = [SMEM] + [VMEM] * (count - 1)
    aliases = {}
    if before is not None:
        inputs += before
        specs += [pl.BlockSpec(memory_space=pl.ANY)] * 4
        aliases = {count + i: i for i in range(4)}
    layout = (starts, len(groups))
    return pl.pallas_call(
        functools.partial(finish_kernel, layout, slots, len(aliases)),
        grid=(1,),
        in_specs=specs,
        out_specs=[pl.BlockSpec((1,) + shape, lambda i: (layer, 0, 0)) for shape in shapes],
        out_shape=[jax.ShapeDtypeStruct((layers,) + shape, F32) for shape in shapes],
        input_output_aliases=aliases,
        compiler_params=pltpu.CompilerParams(vmem_limit_bytes=48 << 20),
        cost_estimate=pl.CostEstimate(flops=0, bytes_accessed=0, transcendentals=0),
        name="finish",
    )(*inputs)


def out_back_kernel(
    scalars,
    keep,
    beside,
    across,
    middle,
    grad,
    table,
    w_own,
    w_other,
    grad_middle,
    branch,
    first,
    second,
    third,
    fourth,
    sums,
):
    run = scalars[0]
    core = run % 2
    total = keep[...] + beside[...].astype(F32) + across[...].astype(F32)
    value, grad_gain, grad_shift = norm_back(middle[...], row(table, GAIN_TWO), total)
    value = grad[...] + value
    grad_middle[...] = value
    low = value.astype(BF)
    branch[...] = low
    sums[...] = jnp.zeros_like(sums)
    sums[0:1, :] = grad_gain
    sums[1:2, :] = grad_shift
    sums[2:3, :] = jnp.sum(low.astype(F32), axis=0, keepdims=True)
    sums[3:4, :] = jnp.sum(grad[...].astype(BF).astype(F32), axis=0, keepdims=True)
    size = first.shape[1]
    half = w_own.shape[1]
    for j, target in enumerate((first, second, third, fourth)):
        rows = pl.ds(pl.multiple_of((run ^ j) * size, size), size)
        result = None
        for weight, place in ((w_own, core), (w_other, 1 - core)):
            lanes = pl.ds(pl.multiple_of(place * half, half), half)
            term = nt(branch[:, lanes], weight[rows, :])
            result = term if result is None else result + term
        target[...] = result.astype(BF)


def out_back(scalars, sums, middle, grad, table, w_outs):
    rows, width = middle.shape
    mine = width // 4
    outs = [
        ((rows, width), F32),
        ((rows, width), BF),
        ((rows, mine), BF),
        ((rows, mine), BF),
        ((rows, mine), BF),
        ((rows, mine), BF),
        ((8, width), F32),
    ]
    inputs = (scalars, *sums, middle, grad, table, *w_outs)
    return kernel_call(out_back_kernel, "out_back", inputs, outs, in_specs=[SMEM] + [VMEM] * 8)


def layer_begin_kernel(
    keep, beside, across, stream, grad_middle, table, grad, low, sums
):
    total = keep[...] + beside[...].astype(F32) + across[...].astype(F32)
    value, grad_gain, grad_shift = norm_back(stream[...], row(table, GAIN_ONE), total)
    value = grad_middle[...] + value
    grad[...] = value
    low[...] = value.astype(BF)
    sums[...] = jnp.zeros_like(sums)
    sums[0:1, :] = grad_gain
    sums[1:2, :] = grad_shift


def layer_begin(sums, stream, grad_middle, table):
    shape = stream.shape
    outs = [(shape, F32), (shape, BF), ((8, shape[1]), F32)]
    return kernel_call(
        layer_begin_kernel, "layer_begin", (*sums, stream, grad_middle, table), outs
    )


def halves(value, head):
    lane = lax.broadcasted_iota(jnp.int32, value.shape, 1)
    return jnp.where((lane >= HEAD_DIM) == (head == 1), value, jnp.zeros_like(value))


def masked_scores(keys, query, i, j, slope, offsets, length):
    scores = nt(keys, query)
    if i == j:
        scores = scores - slope * jnp.abs(offsets)
    else:
        scores = scores - (slope * offsets + slope * float((i - j) * BLOCK))
    if j == 0:
        return scores, None
    return scores, j * BLOCK + lax.broadcasted_iota(jnp.int32, scores.shape, 0) < length


def block(i):
    return slice(i * BLOCK, (i + 1) * BLOCK)


def distances(ref):
    shape = (BLOCK, BLOCK)
    offsets = lax.broadcasted_iota(jnp.int32, shape, 1) - lax.broadcasted_iota(jnp.int32, shape, 0)
    ref[...] = offsets.astype(F32)


def attend_kernel(
    scalars,
    slopes,
    a,
    b,
    c,
    d,
    w_qkv,
    bias,
    nat,
    att,
    own,
    near,
    far,
    farther,
    lse,
    low,
    scores,
    offsets,
):
    run, length = scalars[0], scalars[1]
    blocks = nat.shape[0] // BLOCK
    mine = nat.shape[1] // 3
    for j, rows in enumerate((a, b, c, d)):
        place = pl.ds(pl.multiple_of((run ^ j) * BLOCK, BLOCK), BLOCK)
        nat[place, :] = (nn(rows[...], w_qkv[...]) + bias[...]).astype(BF)
    distances(offsets)
    for i in range(blocks):
        for pair in range(mine // 128):
            lanes = slice(pair * 128, (pair + 1) * 128)
            out = jnp.zeros((128, BLOCK), F32)
            for head in range(2):
                slope = slopes[pair * 2 + head]
                query = halves(nat[block(i), lanes], head) * jnp.asarray(HEAD_DIM**-0.5, BF)
                top = None
                for j in range(i + 1):
                    keys = nat[block(j), mine + pair * 128 : mine + (pair + 1) * 128]
                    tile, seen = masked_scores(keys, query, i, j, slope, offsets[...], length)
                    if seen is not None:
                        tile = jnp.where(seen, tile, NEG)
                    scores[block(j), :] = tile
                    tile_top = jnp.max(tile, axis=0, keepdims=True)
                    top = tile_top if top is None else jnp.maximum(top, tile_top)
                total = jnp.zeros((1, BLOCK), F32)
                summed = jnp.zeros((128, BLOCK), F32)
                for j in range(i + 1):
                    weights = jnp.exp(scores[block(j), :] - top)
                    total = total + jnp.sum(weights, axis=0, keepdims=True)
                    values = nat[block(j), 2 * mine + pair * 128 : 2 * mine + (pair + 1) * 128]
                    summed = summed + tn(halves(values, head), weights.astype(BF))
                out = out + summed / total
                lse[pair * 2 + head : pair * 2 + head + 1, block(i)] = top + jnp.log(total)
            rows = jnp.transpose(out)
            att[block(i), lanes] = rows
            low[run ^ i, :, lanes] = rows.astype(BF)
    own[...] = low[0]
    near[...] = low[1]
    far[...] = low[2]
    farther[...] = low[3]


def attend_back_kernel(
    scalars,
    slopes,
    nat,
    own,
    beside,
    across,
    far,
    att,
    lse,
    w_qkv,
    out,
    near_keep,
    near_send,
    far_keep,
    far_send,
    sums,
    nat_grad,
    grad_q,
    grad_k,
    grad_v,
    offsets,
):
    run, length = scalars[0], scalars[1]
    blocks = nat.shape[0] // BLOCK
    mine = nat.shape[1] // 3
    for j, rows in enumerate((own[...], beside[...], across[...], far[...])):
        place = pl.ds(pl.multiple_of((run ^ j) * BLOCK, BLOCK), BLOCK)
        nat_grad[place, :] = rows
    distances(offsets)
    grad_k[...] = jnp.zeros_like(grad_k)
    grad_v[...] = jnp.zeros_like(grad_v)
    scale = jnp.asarray(HEAD_DIM**-0.5, BF)
    for pair in range(mine // 128):
        lanes = slice(pair * 128, (pair + 1) * 128)
        k_lanes = slice(mine + pair * 128, mine + (pair + 1) * 128)
        v_lanes = slice(2 * mine + pair * 128, 2 * mine + (pair + 1) * 128)
        for i in range(blocks):
            grad_rows = nat_grad[block(i), lanes]
            product = grad_rows.astype(F32) * att[block(i), lanes]
            ones = lax.broadcasted_iota(jnp.int32, (8, 128), 1) // HEAD_DIM
            ones = (ones == lax.broadcasted_iota(jnp.int32, (8, 128), 0)).astype(F32)
            delta = lax.dot_general(
                ones,
                product,
                (((1,), (1,)), ((), ())),
                precision=lax.Precision.HIGHEST,
                preferred_element_type=F32,
            )
            sum_q = jnp.zeros((128, BLOCK), F32)
            for head in range(2):
                number = pair * 2 + head
                slope = slopes[number]
                query = halves(nat[block(i), lanes], head) * scale
                grad_head = halves(grad_rows, head)
                row_lse = lse[number : number + 1, block(i)]
                row_delta = delta[head : head + 1, :]
                for j in range(i + 1):
                    keys = nat[block(j), k_lanes]
                    tile, seen = masked_scores(keys, query, i, j, slope, offsets[...], length)
                    probs = jnp.exp(tile - row_lse)
                    if seen is not None:
                        probs = jnp.where(seen, probs, 0.0)
                    grad_probs = nt(nat[block(j), v_lanes], grad_head)
                    grad_scores = (probs * (grad_probs - row_delta)).astype(BF)
                    grad_v[block(j), lanes] += nn(probs.astype(BF), grad_head)
                    grad_k[block(j), lanes] += nn(grad_scores, query)
                    sum_q = sum_q + tn(halves(keys, head), grad_scores)
            grad_q[block(i), lanes] = (jnp.transpose(sum_q) * HEAD_DIM**-0.5).astype(BF)
    sums[...] = jnp.zeros_like(sums)
    for j in range(4):
        place = pl.ds(pl.multiple_of((run ^ j) * BLOCK, BLOCK), BLOCK)
        out[block(j), :mine] = grad_q[place, :]
        out[block(j), mine : 2 * mine] = grad_k[place, :].astype(BF)
        out[block(j), 2 * mine :] = grad_v[place, :].astype(BF)
        rows = out[block(j), :]
        sums[0:1, :] += jnp.sum(rows.astype(F32), axis=0, keepdims=True)
        partial = nt(rows, w_qkv[...])
        if j == 0:
            near_keep[...] = partial
        elif j == 1:
            near_send[...] = partial.astype(BF)
        elif j == 2:
            far_keep[...] = partial
        else:
            far_send[...] = partial.astype(BF)


def attend(blocks, w_qkv, bias, scalars, slopes):
    rows, width = blocks[0].shape
    columns = w_qkv.width
    mine = columns // 3
    outs = [
        ((4 * rows, columns), BF),
        ((4 * rows, mine), F32),
        ((rows, mine), BF),
        ((rows, mine), BF),
        ((rows, mine), BF),
        ((rows, mine), BF),
        ((8, 4 * rows), F32),
    ]
    scratch = [
        pltpu.VMEM((4, rows, mine), BF),
        pltpu.VMEM((4 * rows, BLOCK), F32),
        pltpu.VMEM((BLOCK, BLOCK), F32),
    ]
    inputs = (scalars, slopes, *blocks, w_qkv, bias)
    specs = [SMEM, SMEM] + [VMEM] * 6
    return kernel_call(attend_kernel, "attend", inputs, outs, scratch, specs)


def attend_back(nat, parts, att, lse, w_qkv, scalars, slopes):
    total, columns = nat.shape
    rows, mine = total // 4, columns // 3
    width = w_qkv.rows * lax.axis_size("fsdp")
    outs = [
        ((total, columns), BF),
        ((rows, width), F32),
        ((rows, width), BF),
        ((rows, width), F32),
        ((rows, width), BF),
        ((8, columns), F32),
    ]
    scratch = [
        pltpu.VMEM((total, mine), BF),
        pltpu.VMEM((total, mine), BF),
        pltpu.VMEM((total, mine), F32),
        pltpu.VMEM((total, mine), F32),
        pltpu.VMEM((BLOCK, BLOCK), F32),
    ]
    inputs = (scalars, slopes, nat, *parts, att, lse, w_qkv)
    specs = [SMEM, SMEM] + [VMEM] * 8
    return kernel_call(attend_back_kernel, "attend_back", inputs, outs, scratch, specs)


def shards(
    tokens,
    lengths,
    cotangent,
    ln1_gain,
    ln1_bias,
    qkv_weight,
    query_bias,
    value_bias,
    out_weight,
    out_bias,
    ln2_gain,
    ln2_bias,
    up_weight,
    up_bias,
    down_weight,
    down_bias,
):
    fsdp = lax.axis_size("fsdp")
    run = lax.axis_index("seq")
    rows, width = tokens.shape[1:]
    hidden = up_weight.shape[2]
    heads = HEADS // 4
    mine = width // 4
    half = width // 2
    ffn_size = hidden // 4
    part = width // fsdp
    piece = hidden // fsdp // 4
    me = lax.axis_index("fsdp")
    scalars = jnp.stack([run.astype(jnp.int32), lengths[0]])
    place = jnp.stack([run, me % 2]).astype(jnp.int32)
    slopes = lax.dynamic_slice_in_dim(head_slopes(), run * heads, heads)

    def quarter(value, axis):
        size = value.shape[axis] // 4
        return lax.dynamic_slice_in_dim(value, run * size, size, axis)

    def core_half(value, axis):
        return lax.dynamic_slice_in_dim(value, (run % 2) * half, half, axis)

    def qkv_of(layer):
        return quarter(qkv_weight[layer].reshape(part, 3, width), 2).reshape(part, 3 * mine)

    def out_of(layer):
        return core_half(out_weight[layer], 1)

    def up_of(layer):
        return quarter(up_weight[layer].reshape(part, fsdp, -1), 2).reshape(part, ffn_size)

    def down_of(layer):
        return quarter(down_weight[layer], 0)

    def seq_blocks(own):
        across = y_swap(own)
        return [own, core_swap(own), across, core_swap(across)]

    def summed(near, far):
        far = far_sum(far)
        return near[0], core_swap(near[1]), y_swap(far)

    def far_sum(far):
        return (far[0] + core_swap(far[1]).astype(F32)).astype(BF)

    vectors = (ln1_gain, ln1_bias, query_bias, value_bias, out_bias, ln2_gain, ln2_bias, down_bias)
    small = jnp.concatenate([jnp.stack(vectors, 1).reshape(LAYERS, -1), up_bias], axis=1)
    columns = 3 * mine
    extra = small.size // columns
    small = jnp.pad(small.reshape(extra, columns), ((0, -extra % 16), (0, 0)))
    stride = part + small.shape[0]
    own = pack(["qkv", "small"], [qkv_weight, small], 0, place, stride, columns)
    token_blocks = seq_blocks(tokens[0])
    even = [own] + [hop(own, "fsdp", 2 * k) for k in range(1, fsdp // 2 - 1)]
    even.append(hop(tied(own, even[1]), "fsdp", fsdp - 2))
    first = jnp.concatenate(even)
    first = (first, x_swap(first))
    cot_blocks = seq_blocks(cotangent[0])
    token_blocks, cot_blocks, first = meet(token_blocks, cot_blocks, first)
    arrays = dict(qkv=qkv_weight, out=out_weight, up=up_weight, down=down_weight)
    sizes = dict(qkv=columns, out=half, up=ffn_size, down=width)

    def bundle(layer, names):
        if part % 128:
            parts = dict(qkv=qkv_of, out=out_of, up=up_of, down=down_of)
            return jnp.concatenate([parts[name](layer) for name in names], axis=1)
        total = sum(sizes[name] for name in names)
        return pack(names, [arrays[name] for name in names], layer, place, part, total)

    packs = [
        bundle(0, ["out", "up"]),
        bundle(0, ["down"]),
        bundle(1, ["qkv", "out"]),
        bundle(1, ["up", "down"]),
    ]
    keys = jnp.stack([me, me % 2]).astype(jnp.int32)
    early_one, late_one, early_two, late_two = (gather_z(item) for item in packs)

    def matrix(halves, column, size, key=1):
        return Slots(halves, column, size, part, keys, key)

    def out_matrices(halves, column):
        own = assemble(halves, column, half, part, me % 2)
        return own, core_swap(own)

    small = [item.reshape(fsdp // 2, stride, columns)[:, part : part + extra] for item in first]
    small = jnp.stack(small, 1).reshape(fsdp, LAYERS, -1)
    small = jnp.take(small, me ^ jnp.arange(fsdp), axis=0).astype(F32)
    tables, biases = [], []
    for layer in range(LAYERS):
        table = small[:, layer, : 8 * part].reshape(fsdp, 8, part)
        table = jnp.transpose(table, (1, 0, 2)).reshape(8, width)
        bias_q, bias_v = quarter(table[BIAS_Q], 0), quarter(table[BIAS_V], 0)
        bias_qkv = jnp.concatenate([bias_q, jnp.zeros_like(bias_q), bias_v])
        bias_up = quarter(small[:, layer, 8 * part :], 1)
        tables.append(table)
        biases.append((bias_qkv.reshape(1, -1), bias_up.reshape(1, -1)))

    stream = tokens[0].astype(F32)
    token_blocks, tables, biases = meet(token_blocks, tables, biases)
    h1 = first_norm(token_blocks, tables[0])
    w_qkv = matrix(first, 0, columns, 0)
    out_one, up_one = early_one[:, :half], early_one[:, half:]
    moved_out, moved = x_swap(out_one), x_swap(up_one)
    saved, weights = [], []
    for layer in range(LAYERS):
        top = layer + 1 == LAYERS
        bias_qkv, bias_up = biases[layer]
        packed, attended, *low, lse = attend(h1, w_qkv, bias_qkv, scalars, slopes)
        if top:
            w_outs = out_matrices(early_two, columns)
        else:
            low, moved_out = meet(low, moved_out)
            w_outs = out_matrices((out_one, moved_out), 0)
        far = y_swap(low[3])
        across = y_swap(low[2])
        if not top:
            across, far, moved, late_one = meet(across, far, moved, late_one)
            moved_late = x_swap(late_one)
        parts = [low[0], core_swap(low[1]), across, core_swap(far)]
        middle, normed, att_own = out_step(scalars, parts, w_outs, stream, tables[layer])
        h2 = seq_blocks(normed)
        if top:
            middle, moved = meet(middle, moved)
            late_two = (late_two, moved)
            w_up, w_down = matrix(late_two, 0, ffn_size), matrix(late_two, ffn_size, width)
            near = ffn(h2[0], h2[1], w_up, bias_up, w_down)
            near_back = ffn_back(cot_blocks[0], cot_blocks[1], near[1], w_up, w_down)
            h2[2], near, near_back = meet(h2[2], near, near_back)
            h2[3] = core_swap(h2[2])
        else:
            h2[2], moved_late, early_two = meet(h2[2], moved_late, early_two)
            h2[3] = core_swap(h2[2])
            w_up = matrix((up_one, moved), 0, ffn_size)
            w_down = matrix((late_one, moved_late), 0, width)
            moved = x_swap(early_two)
            near = ffn(h2[0], h2[1], w_up, bias_up, w_down)
        far = ffn(h2[2], h2[3], w_up, bias_up, w_down)
        saved.append((stream, h1, packed, attended, lse, att_own, middle, h2, near[:2], far[:2]))
        weights.append((w_qkv, w_outs, w_up, w_down))
        if top:
            last_sums = near[2:], far[2:]
        else:
            sums, moved, late_two = meet(summed(near[2:], far[2:]), moved, late_two)
            early_two = (early_two, moved)
            w_qkv = matrix(early_two, 0, columns)
            moved = x_swap(late_two)
            stream, normed = layer_end(middle, sums, tables[layer], tables[layer + 1])
            h1 = seq_blocks(normed)

    grad = cotangent[0].astype(F32)
    g_down = cot_blocks
    vectors = [None] * LAYERS
    upper, lower = [], []
    for layer in reversed(range(LAYERS)):
        top = layer + 1 == LAYERS
        totals = upper if top else lower
        w_qkv, w_outs, w_up, w_down = weights[layer]
        stream, h1, packed, attended, lse, att_own, middle, h2, act_near, act_far = saved[layer]
        if top:
            near = near_back
        else:
            near = ffn_back(g_down[0], g_down[1], act_near[1], w_up, w_down)
            g_down[2], near, late, reduced = meet(g_down[2], near, late, reduced)
            g_down[3] = core_swap(g_down[2])
            moved_late = x_swap(late[1])
        far = ffn_back(g_down[2], g_down[3], act_far[1], w_up, w_down)
        far_low = far_sum(far[1:3])
        acts, h2, far_low = meet([act_near[0], act_far[0]], h2, far_low)
        sent_down = weight_grad(acts, g_down, place, 1)
        sent_up = weight_grad(h2, [near[0], far[0]], place, 1)
        moved_down, moved_up = x_swap(sent_down[1]), x_swap(sent_up[1])
        sums = near[1], core_swap(near[2]), y_swap(far_low)
        sums, sent_down[0], sent_up[0] = meet(sums, sent_down[0], sent_up[0])
        grad_middle, g_branch, *g_att, lines_two = out_back(
            scalars, sums, middle, grad, tables[layer], w_outs
        )
        g_att = [
            g_att[0],
            core_swap(g_att[1]),
            y_swap(g_att[2]),
            y_swap(core_swap(g_att[3])),
        ]
        if not top:
            g_att, moved_late = meet(g_att, moved_late)
            reduced = added(late[0], moved_late)
            g_att, reduced, upper[:2] = meet(g_att, reduced, upper[:2])
            upper.append(scatter_z(reduced))
            upper_far = [y_swap(item) for item in upper[:2]]
        if top:
            g_att, last_sums = meet(g_att, last_sums)
        g_packed, *parts, packed_sum = attend_back(
            packed, g_att, attended, lse, w_qkv, scalars, slopes
        )
        if top:
            last_sums = summed(*last_sums)
            parts, moved_down, last_sums = meet(parts, moved_down, last_sums)
            result = layer_end(saved[layer][6], last_sums, tables[layer], None)[1]
        else:
            parts, moved_down, upper_far = meet(parts, moved_down, upper_far)
        far_low = far_sum(parts[2:])
        h1, sent_down[0], far_low = meet(h1, sent_down[0], far_low)
        if not layer:
            att_own, g_branch, far_low = meet(att_own, g_branch, far_low)
            keep, send = out_grad(att_own, g_branch, place)
        sent_qkv = weight_grad(h1, [g_packed], place, 1)
        sums = parts[0], core_swap(parts[1]), y_swap(far_low)
        reduced = added(sent_down[0], moved_down)
        totals.append(scatter_z(reduced))
        sums, moved_up, reduced, sent_qkv[0] = meet(sums, moved_up, reduced, sent_qkv[0])
        if not top:
            reduced = added(sent_up[0], moved_up)
            totals.append(scatter_z(reduced))
            sums, upper[2] = meet(sums, upper[2])
        up_sum = near[3] + far[3]
        grad, normed, lines_one = layer_begin(sums, stream, grad_middle, tables[layer])
        if layer:
            normed, sent_up[0], att_own, g_branch = meet(normed, sent_up[0], att_own, g_branch)
            g_down = seq_blocks(normed)
            keep, send = out_grad(att_own, g_branch, place)
            reduced = added(sent_up[0], moved_up)
            upper.append(scatter_z(reduced))
        else:
            grad, totals[0] = meet(grad, totals[0])
        sent_out = added_pair(keep, core_swap(send))
        late = [jnp.concatenate(pair, axis=1) for pair in zip(sent_qkv, sent_out)]
        if not layer:
            last, *totals = meet(added(late[0], x_swap(late[1])), *totals)
            lower = totals + [scatter_z(last)]

        vectors[layer] = (lines_two, lines_two, packed_sum, lines_one, up_sum)

    def spread(value, axis=0):
        shape = list(value.shape)
        size = shape[axis]
        shape[axis] = 4 * size
        return lax.dynamic_update_slice_in_dim(jnp.zeros(shape, F32), value, run * size, axis)

    small_sums = []
    vectors, upper[2], grad = meet(vectors, upper[2], grad)
    for _, lines_two, packed_sum, lines_one, up_sum in vectors:
        members = [
            lines_one[0],
            lines_one[1],
            spread(packed_sum[0, :mine]),
            spread(packed_sum[0, 2 * mine :]),
            lines_two[2],
            lines_two[0],
            lines_two[1],
            lines_two[3],
        ]
        small_sums.append(
            jnp.concatenate(
                [item.reshape(fsdp, part) for item in members]
                + [spread(up_sum.reshape(fsdp, piece), 1)],
                axis=1,
            )
        )

    own = zip(upper[:2], upper_far)
    upper[:2] = [(item, core_swap(item), far, core_swap(far)) for item, far in own]
    upper[2] = four(upper[2])
    starts = ((2, 0), (2, columns), (1, 0), (0, 0))
    matrices = finish(1, LAYERS, upper, starts, place, None)
    vector = sum_small(jnp.stack(small_sums, axis=1))
    early = [four(item) for item in lower[:2]]
    last, early, matrices, vector, result = meet(lower[2], early, matrices, vector, result)
    lower = [*early, four(last)]
    matrices = finish(0, LAYERS, lower, starts, place, matrices)
    grad_qkv_w, grad_out_w, grad_up_w, grad_down_w = matrices
    if piece % 128:
        grad_up_w = grad_up_w.reshape(LAYERS, part, 4, fsdp, piece)
        grad_up_w = jnp.swapaxes(grad_up_w, 2, 3).reshape(LAYERS, part, hidden)
    lines = [vector[:, i * part : (i + 1) * part] for i in range(8)]
    gain_one, shift_one, bias_q, bias_v, bias_o, gain_two, shift_two, bias_down = lines
    return (
        result[None],
        grad[None],
        gain_one,
        shift_one,
        grad_qkv_w,
        bias_q,
        bias_v,
        grad_out_w,
        bias_o,
        gain_two,
        shift_two,
        grad_up_w,
        vector[:, 8 * part :],
        grad_down_w,
        bias_down,
    )


def solution(mesh):
    vector = P(None, "fsdp")
    matrix = P(None, "fsdp", None)
    data = P("fsdp", "seq", None)
    weight_specs = (
        vector,
        vector,
        matrix,
        vector,
        vector,
        matrix,
        vector,
        vector,
        vector,
        matrix,
        vector,
        matrix,
        vector,
    )
    in_specs = (data, P("fsdp"), data) + weight_specs
    out_specs = (data, data) + weight_specs
    return jax.shard_map(shards, mesh=mesh, in_specs=in_specs, out_specs=out_specs, check_vma=False)
```

```python
import functools

import jax
import jax.numpy as jnp
from jax import lax
from jax.experimental import pallas as pl
from jax.experimental.pallas import tpu as pltpu
from jax.sharding import PartitionSpec as P

HEADS = 16
HEAD_DIM = 64
LAYERS = 2
BLOCK = 256
EPS = 1e-05
NEG = -1e30
BF = jnp.bfloat16
F32 = jnp.float32
GELU = 0.7978845608028654
CUBIC = 0.044715
VMEM = pl.BlockSpec(memory_space=pltpu.VMEM)
SMEM = pl.BlockSpec(memory_space=pltpu.SMEM)


def head_slopes():
    return jnp.exp2(-8.0 * (jnp.arange(HEADS, dtype=F32) + 1.0) / HEADS)


def hop(value, axis, mask):
    size = lax.axis_size(axis)
    return lax.ppermute(value, axis, [(i, i ^ mask) for i in range(size)])


def core_swap(value):
    return hop(value, "seq", 1)


def y_swap(value):
    return hop(value, "seq", 2)


def sum_small(full):
    size = lax.axis_size("fsdp")
    me = lax.axis_index("fsdp")
    full = full + y_swap(full)
    full = full + core_swap(full)
    slots = jnp.take(full, me ^ jnp.arange(size), axis=0)
    slots = slots.reshape((size // 2, 2) + full.shape[1:])
    slots = slots[:, 0] + hop(slots[:, 1], "fsdp", 1)
    total = slots[0]
    for k in range(1, size // 2):
        total = total + hop(slots[k], "fsdp", 2 * k)
    return total


def assemble_kernel(column, stride, key_ref, same, other, out, held, sems):
    key = key_ref[0]
    pairs, rows, width = held.shape[0] // 2, held.shape[1], held.shape[2]
    loads, stores = [], []
    for r in range(2 * pairs):
        place = pl.ds(r // 2 * stride, rows)
        source = (other if r % 2 else same).at[place, pl.ds(column, width)]
        loads.append(pltpu.make_async_copy(source, held.at[r], sems.at[r, 0]))
        start = pl.multiple_of((r ^ key) * rows, rows)
        target = out.at[pl.ds(start, rows), :]
        stores.append(pltpu.make_async_copy(held.at[r], target, sems.at[r, 1]))
    for load in loads:
        load.start()
    for load, store in zip(loads, stores):
        load.wait()
        store.start()
    for store in stores:
        store.wait()


def assemble(halves, column, width, rows, key):
    slots = lax.axis_size("fsdp")
    stride = 2 * halves[0].shape[0] // slots
    key = key.astype(jnp.int32).reshape(1)
    hbm = pl.BlockSpec(memory_space=pl.ANY)
    return pl.pallas_call(
        functools.partial(assemble_kernel, column, stride),
        grid_spec=pltpu.PrefetchScalarGridSpec(
            num_scalar_prefetch=1,
            grid=(),
            in_specs=[hbm] * 2,
            out_specs=hbm,
            scratch_shapes=[
                pltpu.VMEM((slots, rows, width), BF),
                pltpu.SemaphoreType.DMA((slots, 2)),
            ],
        ),
        out_shape=jax.ShapeDtypeStruct((slots * rows, width), BF),
        compiler_params=pltpu.CompilerParams(vmem_limit_bytes=32 << 20),
        cost_estimate=pl.CostEstimate(flops=0, bytes_accessed=0, transcendentals=0),
        name="assemble",
    )(key, *halves)


def tied(value, after):
    return lax.optimization_barrier((value, after))[0]


def meet(*values):
    return lax.optimization_barrier(values)


def pack_kernel(names, layer, place, *refs):
    sources, (out, sems) = dict(zip(names, refs)), refs[len(names) :]
    run = place[0]
    copies = []
    column = 0

    def add(source, size, rows=None):
        rows = source.shape[0] if rows is None else rows
        target = out.at[pl.ds(0, rows), pl.ds(column, size)]
        copies.append(pltpu.make_async_copy(source, target, sems.at[len(copies)]))
        return column + size

    for name in names:
        source = sources[name]
        if name == "small":
            rows = source.shape[0]
            target = out.at[pl.ds(out.shape[0] - rows, rows), :]
            copies.append(pltpu.make_async_copy(source, target, sems.at[len(copies)]))
            continue
        source = source.at[layer]
        part, width = source.shape
        if name == "qkv":
            for third in range(3):
                start = pl.multiple_of((4 * third + run) * (width // 12), width // 12)
                column = add(source.at[:, pl.ds(start, width // 12)], width // 12)
        elif name == "out":
            start = pl.multiple_of(run % 2 * (width // 2), width // 2)
            column = add(source.at[:, pl.ds(start, width // 2)], width // 2)
        elif name == "up":
            piece = part
            for slot in range(width // (4 * piece)):
                start = pl.multiple_of((4 * slot + run) * piece, piece)
                column = add(source.at[:, pl.ds(start, piece)], piece)
        else:
            start = pl.multiple_of(run * (part // 4), part // 4)
            column = add(source.at[pl.ds(start, part // 4), :], width)
    for copy in copies:
        copy.start()
    for copy in copies:
        copy.wait()


def pack(names, arrays, layer, place, rows, columns):
    count = sum({"qkv": 3, "up": arrays[0].shape[-1]}.get(name, 1) for name in names)
    hbm = pl.BlockSpec(memory_space=pl.ANY)
    return pl.pallas_call(
        functools.partial(pack_kernel, names, layer),
        in_specs=[SMEM] + [hbm] * len(arrays),
        out_specs=VMEM,
        out_shape=jax.ShapeDtypeStruct((rows, columns), BF),
        scratch_shapes=[pltpu.SemaphoreType.DMA((min(count, 64),))],
        compiler_params=pltpu.CompilerParams(vmem_limit_bytes=32 << 20),
        cost_estimate=pl.CostEstimate(flops=0, bytes_accessed=0, transcendentals=0),
        name="pack",
    )(place, *arrays)


def z_groups():
    size = lax.axis_size("fsdp")
    return [[x + 2 * k for k in range(size // 2)] for x in range(2)]


def gather_z(own):
    return lax.all_gather(own, "fsdp", axis=0, tiled=True, axis_index_groups=z_groups())


def x_swap(value):
    return hop(value, "fsdp", 1)


def scatter_z(same):
    return lax.psum_scatter(
        same, "fsdp", scatter_dimension=0, tiled=True, axis_index_groups=z_groups()
    )


def four(total):
    across = y_swap(total)
    return total, core_swap(total), across, core_swap(across)


class Slots:
    def __init__(self, halves, column, width, rows, keys, key):
        self.halves, self.column, self.width, self.rows = halves, column, width, rows
        self.keys, self.key = keys, key

    def copies(self, keys, same, other, buffer):
        count = buffer.shape[0] // self.rows
        stride = 2 * same.shape[0] // count
        for r in range(count):
            source = other if r % 2 else same
            source = source.at[pl.ds(r // 2 * stride, self.rows), pl.ds(self.column, self.width)]
            start = pl.multiple_of((r ^ keys[self.key]) * self.rows, self.rows)
            yield source, buffer.at[pl.ds(start, self.rows), :]


def staged(body, plan, refs):
    refs = list(refs)
    keys = refs.pop(0) if any(isinstance(item, Slots) for item in plan) else None
    taken = [refs.pop(0) for item in plan for _ in range(1 + isinstance(item, Slots))]
    sems = refs.pop()
    places = [i for i, item in enumerate(plan) if item is not None]
    buffers = refs[len(refs) - len(places) :]
    refs = refs[: len(refs) - len(places)]
    inputs, copies = [], []
    for item in plan:
        if item is None:
            inputs.append(taken.pop(0))
            continue
        buffer = buffers.pop(0)
        inputs.append(buffer)
        if item is VMEM:
            moves = [(taken.pop(0), buffer)]
        else:
            moves = item.copies(keys, taken.pop(0), taken.pop(0), buffer)
        for source, target in moves:
            copies.append(pltpu.make_async_copy(source, target, sems.at[len(copies)]))
    for copy in copies:
        copy.start()
    for copy in copies:
        copy.wait()
    body(*inputs, *refs)


def kernel_call(body, name, inputs, outputs, scratch=(), in_specs=None, cost=0):
    plan, arrays, specs, buffers, keys = [], [], [], [], None
    count = 1
    hbm = pl.BlockSpec(memory_space=pl.ANY)
    for item, spec in zip(inputs, in_specs or [VMEM] * len(inputs)):
        if isinstance(item, Slots):
            shape = (lax.axis_size("fsdp") * item.rows, item.width)
            plan.append(item)
            arrays += item.halves
            specs += [hbm, hbm]
            buffers.append(pltpu.VMEM(shape, BF))
            keys = item.keys
            count += lax.axis_size("fsdp")
            continue
        arrays.append(item)
        plan.append(VMEM if spec is VMEM else None)
        specs.append(hbm if spec is VMEM else SMEM)
        if spec is VMEM:
            buffers.append(pltpu.VMEM(item.shape, item.dtype))
            count += 1
    if keys is not None:
        arrays, specs = [keys] + arrays, [SMEM] + specs
    return pl.pallas_call(
        lambda *refs: staged(body, plan, refs),
        in_specs=specs,
        out_specs=[VMEM] * len(outputs),
        out_shape=[jax.ShapeDtypeStruct(shape, kind) for shape, kind in outputs],
        scratch_shapes=[*scratch, *buffers, pltpu.SemaphoreType.DMA((count,))],
        compiler_params=pltpu.CompilerParams(vmem_limit_bytes=48 << 20),
        cost_estimate=pl.CostEstimate(flops=0, bytes_accessed=cost, transcendentals=0),
        name=name,
    )(*arrays)


def pair_kernel(keep, received, same, other):
    for i, target in enumerate((same, other)):
        target[...] = (keep[i].astype(F32) + received[i].astype(F32)).astype(BF)


def added_pair(keep, received):
    outs = [(keep.shape[1:], BF)] * 2
    return kernel_call(pair_kernel, "added_pair", (keep, received), outs)


def add_kernel(same, *refs):
    out = refs[-1]
    start = 0
    for item in refs[:-1]:
        rows = slice(start, start + item.shape[0])
        out[rows, :] = (same[rows, :].astype(F32) + item[...].astype(F32)).astype(BF)
        start += item.shape[0]


def added(same, *received):
    return kernel_call(add_kernel, "added", (same, *received), [(same.shape, BF)])[0]


def nn(left, right):
    return jnp.dot(left, right, preferred_element_type=F32)


def nt(left, right):
    return lax.dot_general(left, right, (((1,), (1,)), ((), ())), preferred_element_type=F32)


def tn(left, right):
    return lax.dot_general(left, right, (((0,), (0,)), ((), ())), preferred_element_type=F32)


def normalized(value):
    center = value - jnp.mean(value, axis=-1, keepdims=True)
    scale = lax.rsqrt(jnp.mean(center * center, axis=-1, keepdims=True) + EPS)
    return center * scale, scale


def norm_back(value, gain, grad):
    hat, scale = normalized(value)
    inner = grad * gain
    mean = jnp.mean(inner, axis=-1, keepdims=True)
    along = jnp.mean(inner * hat, axis=-1, keepdims=True)
    grad_gain = jnp.sum(grad * hat, axis=0, keepdims=True)
    return scale * (inner - mean - hat * along), grad_gain, jnp.sum(grad, axis=0, keepdims=True)


GAIN_ONE, SHIFT_ONE, BIAS_Q, BIAS_V, BIAS_OUT, GAIN_TWO, SHIFT_TWO, BIAS_DOWN = range(8)


def row(table, index):
    return table[index : index + 1, :]


def first_norm_kernel(a, b, c, d, table, *outs):
    for value, out in zip((a, b, c, d), outs):
        hat, _ = normalized(value[...].astype(F32))
        out[...] = (hat * row(table, GAIN_ONE) + row(table, SHIFT_ONE)).astype(BF)


def first_norm(blocks, table):
    outs = [(item.shape, BF) for item in blocks]
    return kernel_call(first_norm_kernel, "first_norm", (*blocks, table), outs)


def layer_end_kernel(middle, keep, beside, across, table, after, stream, normed):
    total = keep[...] + beside[...].astype(F32) + across[...].astype(F32)
    value = middle[...] + (total + row(table, BIAS_DOWN))
    stream[...] = value
    if after is None:
        normed[...] = value.astype(BF)
    else:
        hat, _ = normalized(value)
        normed[...] = (hat * row(after, GAIN_ONE) + row(after, SHIFT_ONE)).astype(BF)


def last_end_kernel(middle, keep, beside, across, table, stream, low):
    layer_end_kernel(middle, keep, beside, across, table, None, stream, low)


def layer_end(middle, sums, table, after):
    outs = [(middle.shape, F32), (middle.shape, BF)]
    if after is None:
        return kernel_call(last_end_kernel, "last_end", (middle, *sums, table), outs)
    return kernel_call(layer_end_kernel, "layer_end", (middle, *sums, table, after), outs)


def out_kernel(
    scalars, own, beside, across, far, w_own, w_other, stream, table, middle, normed, attended
):
    run = scalars[0]
    core = run % 2
    parts = [own[...], beside[...], across[...], far[...]]
    size = parts[0].shape[1]
    starts = [pl.multiple_of((run ^ j) * size, size) for j in range(4)]
    for part, start in zip(parts, starts):
        attended[:, pl.ds(start, size)] = part
    half = w_own.shape[1]
    for weight, place in ((w_own, core), (w_other, 1 - core)):
        total = None
        for part, start in zip(parts, starts):
            term = nn(part, weight[pl.ds(start, size), :])
            total = term if total is None else total + term
        lanes = pl.ds(pl.multiple_of(place * half, half), half)
        bias = table[BIAS_OUT : BIAS_OUT + 1, lanes]
        middle[:, lanes] = stream[:, lanes] + (total + bias)
    hat, _ = normalized(middle[...])
    normed[...] = (hat * row(table, GAIN_TWO) + row(table, SHIFT_TWO)).astype(BF)


def out_step(scalars, parts, w_outs, stream, table):
    outs = [(stream.shape, F32), (stream.shape, BF), (stream.shape, BF)]
    inputs = (scalars, *parts, *w_outs, stream, table)
    return kernel_call(out_kernel, "out_step", inputs, outs, in_specs=[SMEM] + [VMEM] * 8)


def ffn_kernel(a, b, w_up, bias, w_down, act, slope, keep, send, source):
    rows = a.shape[0]
    source[:rows, :] = a[...]
    source[rows:, :] = b[...]
    pre = nn(source[...], w_up[...]) + bias[...]
    square = pre * pre
    bent = jnp.tanh(GELU * pre * (1.0 + CUBIC * square))
    half = 0.5 + 0.5 * bent
    value = (pre * half).astype(BF)
    act[...] = value
    rise = half + (0.5 * GELU) * pre * (1.0 - bent * bent) * (1.0 + 3.0 * CUBIC * square)
    slope[...] = rise.astype(BF)
    total = nn(value, w_down[...])
    keep[...] = total[:rows, :]
    send[...] = total[rows:, :].astype(BF)


def ffn(a, b, w_up, bias, w_down):
    rows, width = a.shape
    hidden = w_up.width
    outs = [
        ((2 * rows, hidden), BF),
        ((2 * rows, hidden), BF),
        ((rows, width), F32),
        ((rows, width), BF),
    ]
    scratch = [pltpu.VMEM((2 * rows, width), BF)]
    return kernel_call(ffn_kernel, "ffn", (a, b, w_up, bias, w_down), outs, scratch)


def ffn_back_kernel(a, b, slope, w_up, w_down, grad_pre, keep, send, sums, source):
    rows = a.shape[0]
    source[:rows, :] = a[...]
    source[rows:, :] = b[...]
    grad_act = nt(source[...], w_down[...])
    value = (grad_act * slope[...].astype(F32)).astype(BF)
    grad_pre[...] = value
    sums[...] = jnp.sum(value.astype(F32), axis=0, keepdims=True)
    total = nt(value, w_up[...])
    keep[...] = total[:rows, :]
    send[...] = total[rows:, :].astype(BF)


def ffn_back(a, b, slope, w_up, w_down):
    rows, width = a.shape
    hidden = w_up.width
    outs = [
        ((2 * rows, hidden), BF),
        ((rows, width), F32),
        ((rows, width), BF),
        ((1, hidden), F32),
    ]
    scratch = [pltpu.VMEM((2 * rows, width), BF)]
    return kernel_call(ffn_back_kernel, "ffn_back", (a, b, slope, w_up, w_down), outs, scratch)


def weight_grad_kernel(count, parts, scalars, *refs):
    x = scalars[1]
    lefts, rights = refs[: parts[0]], refs[parts[0] : parts[0] + parts[1]]
    *outs, left, right, total = refs[parts[0] + parts[1] :]
    for sources, target in ((lefts, left), (rights, right)):
        start = 0
        for source in sources:
            target[start : start + source.shape[0], :] = source[...]
            start += source.shape[0]
    total[...] = tn(left[...], right[...]).astype(BF)
    rows = total.shape[0] // count
    first = 0
    for same, other in zip(outs[::2], outs[1::2]):
        columns = slice(first, first + same.shape[1])
        first += same.shape[1]
        for r in range(count):
            start = pl.multiple_of((r ^ x) * rows, rows)
            target = other if r % 2 else same
            target[r // 2 * rows : (r // 2 + 1) * rows, :] = total[pl.ds(start, rows), columns]


def weight_grad(lefts, rights, place, cuts=()):
    count = lax.axis_size("fsdp")
    total = sum(item.shape[0] for item in lefts)
    tall, wide = lefts[0].shape[1], rights[0].shape[1]
    outs = [((tall // 2, size), BF) for size in cuts or (wide,) for _ in range(2)]
    scratch = [
        pltpu.VMEM((total, tall), BF),
        pltpu.VMEM((total, wide), BF),
        pltpu.VMEM((tall, wide), BF),
    ]
    inputs = (place, *lefts, *rights)
    body = functools.partial(weight_grad_kernel, count, (len(lefts), len(rights)))
    specs = [SMEM] + [VMEM] * (len(inputs) - 1)
    return list(kernel_call(body, "weight_grad", inputs, outs, scratch, specs))


def out_grad_kernel(count, place, left, right, keep, send, total):
    core, x = place[0] % 2, place[1]
    half = keep.shape[2]
    rows = total.shape[0] // count
    for target, number in ((keep, core), (send, 1 - core)):
        lanes = pl.ds(pl.multiple_of(number * half, half), half)
        total[...] = tn(left[...], right[:, lanes]).astype(BF)
        for r in range(count):
            start = pl.multiple_of((r ^ x) * rows, rows)
            target[r % 2, r // 2 * rows : (r // 2 + 1) * rows, :] = total[pl.ds(start, rows), :]


def out_grad(left, right, place):
    count = lax.axis_size("fsdp")
    tall, wide = left.shape[1], right.shape[1]
    outs = [((2, tall // 2, wide // 2), BF)] * 2
    scratch = [pltpu.VMEM((tall, wide // 2), BF)]
    body = functools.partial(out_grad_kernel, count)
    return kernel_call(
        body, "out_grad", (place, left, right), outs, scratch, [SMEM, VMEM, VMEM]
    )


def finish_kernel(layout, slots, aliased, place, *refs):
    run = place[0]
    groups = []
    for number in range(layout[-1]):
        groups.append(refs[4 * number : 4 * number + 4])
    refs = refs[4 * layout[-1] + aliased :]
    names = layout[1]
    outs = dict(zip(names, refs))
    part = groups[0][0].shape[0]
    width = part * slots
    mine, half, size = width // 4, width // 2, width
    piece = size // slots
    (q_group, q_start), (o_group, o_start), (u_group, u_start), (d_group, d_start) = layout[0]
    qkv, out, up, down = (outs.get(name) for name in ("qkv", "out", "up", "down"))
    for j in range(4):
        owner = run ^ j
        for third in range(3 if qkv is not None else 0):
            lanes = pl.ds(pl.multiple_of(third * width + owner * mine, mine), mine)
            start = q_start + third * mine
            qkv[0, :, lanes] = groups[q_group][j][:, start : start + mine].astype(F32)
        if up is None:
            continue
        if piece % 128:
            lanes = pl.ds(pl.multiple_of(owner * size, size), size)
            up[0, :, lanes] = groups[u_group][j][:, u_start : u_start + size].astype(F32)
        else:
            for slot in range(slots):
                lanes = pl.ds(pl.multiple_of((4 * slot + owner) * piece, piece), piece)
                start = u_start + slot * piece
                up[0, :, lanes] = groups[u_group][j][:, start : start + piece].astype(F32)
        rows = pl.ds(pl.multiple_of(owner * part, part), part)
        down[0, rows, :] = groups[d_group][j][:, d_start : d_start + width].astype(F32)
    for j in range(2 if out is not None else 0):
        lanes = pl.ds(pl.multiple_of((run ^ j) % 2 * half, half), half)
        columns = slice(o_start, o_start + half)
        first, second = groups[o_group][j][:, columns], groups[o_group][j + 2][:, columns]
        out[0, :, lanes] = first.astype(F32) + second.astype(F32)


def finish(layer, layers, groups, starts, place, before, names):
    slots = lax.axis_size("fsdp")
    part = groups[0][0].shape[0]
    width = part * slots
    shapes = dict(
        qkv=(part, 3 * width), out=(part, width), up=(part, 4 * width), down=(4 * part, width)
    )
    shapes = [shapes[name] for name in names]
    inputs = [place] + [item for group in groups for item in group]
    count = len(inputs)
    specs = [SMEM] + [VMEM] * (count - 1)
    aliases = {}
    if before is not None:
        inputs += before
        specs += [pl.BlockSpec(memory_space=pl.ANY)] * len(names)
        aliases = {count + i: i for i in range(len(names))}
    layout = (starts, names, len(groups))
    return pl.pallas_call(
        functools.partial(finish_kernel, layout, slots, len(aliases)),
        grid=(1,),
        in_specs=specs,
        out_specs=[pl.BlockSpec((1,) + shape, lambda i: (layer, 0, 0)) for shape in shapes],
        out_shape=[jax.ShapeDtypeStruct((layers,) + shape, F32) for shape in shapes],
        input_output_aliases=aliases,
        compiler_params=pltpu.CompilerParams(vmem_limit_bytes=48 << 20),
        cost_estimate=pl.CostEstimate(flops=0, bytes_accessed=0, transcendentals=0),
        name="finish",
    )(*inputs)


def out_back_kernel(
    scalars,
    keep,
    beside,
    across,
    middle,
    grad,
    table,
    w_own,
    w_other,
    grad_middle,
    branch,
    first,
    second,
    third,
    fourth,
    sums,
):
    run = scalars[0]
    core = run % 2
    total = keep[...] + beside[...].astype(F32) + across[...].astype(F32)
    value, grad_gain, grad_shift = norm_back(middle[...], row(table, GAIN_TWO), total)
    value = grad[...] + value
    grad_middle[...] = value
    low = value.astype(BF)
    branch[...] = low
    sums[...] = jnp.zeros_like(sums)
    sums[0:1, :] = grad_gain
    sums[1:2, :] = grad_shift
    sums[2:3, :] = jnp.sum(low.astype(F32), axis=0, keepdims=True)
    sums[3:4, :] = jnp.sum(grad[...].astype(BF).astype(F32), axis=0, keepdims=True)
    size = first.shape[1]
    half = w_own.shape[1]
    for j, target in enumerate((first, second, third, fourth)):
        rows = pl.ds(pl.multiple_of((run ^ j) * size, size), size)
        result = None
        for weight, place in ((w_own, core), (w_other, 1 - core)):
            lanes = pl.ds(pl.multiple_of(place * half, half), half)
            term = nt(branch[:, lanes], weight[rows, :])
            result = term if result is None else result + term
        target[...] = result.astype(BF)


def out_back(scalars, sums, middle, grad, table, w_outs):
    rows, width = middle.shape
    mine = width // 4
    outs = [
        ((rows, width), F32),
        ((rows, width), BF),
        ((rows, mine), BF),
        ((rows, mine), BF),
        ((rows, mine), BF),
        ((rows, mine), BF),
        ((8, width), F32),
    ]
    inputs = (scalars, *sums, middle, grad, table, *w_outs)
    return kernel_call(out_back_kernel, "out_back", inputs, outs, in_specs=[SMEM] + [VMEM] * 8)


def layer_begin_kernel(
    keep, beside, across, stream, grad_middle, table, grad, low, sums
):
    total = keep[...] + beside[...].astype(F32) + across[...].astype(F32)
    value, grad_gain, grad_shift = norm_back(stream[...], row(table, GAIN_ONE), total)
    value = grad_middle[...] + value
    grad[...] = value
    low[...] = value.astype(BF)
    sums[...] = jnp.zeros_like(sums)
    sums[0:1, :] = grad_gain
    sums[1:2, :] = grad_shift


def layer_begin(sums, stream, grad_middle, table):
    shape = stream.shape
    outs = [(shape, F32), (shape, BF), ((8, shape[1]), F32)]
    return kernel_call(
        layer_begin_kernel, "layer_begin", (*sums, stream, grad_middle, table), outs
    )


def halves(value, head):
    lane = lax.broadcasted_iota(jnp.int32, value.shape, 1)
    return jnp.where((lane >= HEAD_DIM) == (head == 1), value, jnp.zeros_like(value))


def masked_scores(keys, query, i, j, slope, offsets, length):
    scores = nt(keys, query)
    if i == j:
        scores = scores - slope * jnp.abs(offsets)
    else:
        scores = scores - (slope * offsets + slope * float((i - j) * BLOCK))
    if j == 0:
        return scores, None
    return scores, j * BLOCK + lax.broadcasted_iota(jnp.int32, scores.shape, 0) < length


def block(i):
    return slice(i * BLOCK, (i + 1) * BLOCK)


def distances(ref):
    shape = (BLOCK, BLOCK)
    offsets = lax.broadcasted_iota(jnp.int32, shape, 1) - lax.broadcasted_iota(jnp.int32, shape, 0)
    ref[...] = offsets.astype(F32)


def attend_kernel(
    scalars,
    slopes,
    a,
    b,
    c,
    d,
    w_qkv,
    bias,
    nat,
    att,
    own,
    near,
    far,
    farther,
    lse,
    low,
    scores,
    offsets,
):
    run, length = scalars[0], scalars[1]
    blocks = nat.shape[0] // BLOCK
    mine = nat.shape[1] // 3
    for j, rows in enumerate((a, b, c, d)):
        place = pl.ds(pl.multiple_of((run ^ j) * BLOCK, BLOCK), BLOCK)
        nat[place, :] = (nn(rows[...], w_qkv[...]) + bias[...]).astype(BF)
    distances(offsets)
    for i in range(blocks):
        for pair in range(mine // 128):
            lanes = slice(pair * 128, (pair + 1) * 128)
            out = jnp.zeros((128, BLOCK), F32)
            for head in range(2):
                slope = slopes[pair * 2 + head]
                query = halves(nat[block(i), lanes], head) * jnp.asarray(HEAD_DIM**-0.5, BF)
                top = None
                for j in range(i + 1):
                    keys = nat[block(j), mine + pair * 128 : mine + (pair + 1) * 128]
                    tile, seen = masked_scores(keys, query, i, j, slope, offsets[...], length)
                    if seen is not None:
                        tile = jnp.where(seen, tile, NEG)
                    scores[block(j), :] = tile
                    tile_top = jnp.max(tile, axis=0, keepdims=True)
                    top = tile_top if top is None else jnp.maximum(top, tile_top)
                total = jnp.zeros((1, BLOCK), F32)
                summed = jnp.zeros((128, BLOCK), F32)
                for j in range(i + 1):
                    weights = jnp.exp(scores[block(j), :] - top)
                    total = total + jnp.sum(weights, axis=0, keepdims=True)
                    values = nat[block(j), 2 * mine + pair * 128 : 2 * mine + (pair + 1) * 128]
                    summed = summed + tn(halves(values, head), weights.astype(BF))
                out = out + summed / total
                lse[pair * 2 + head : pair * 2 + head + 1, block(i)] = top + jnp.log(total)
            rows = jnp.transpose(out)
            att[block(i), lanes] = rows
            low[run ^ i, :, lanes] = rows.astype(BF)
    own[...] = low[0]
    near[...] = low[1]
    far[...] = low[2]
    farther[...] = low[3]


def attend_back_kernel(
    scalars,
    slopes,
    nat,
    own,
    beside,
    across,
    far,
    att,
    lse,
    w_qkv,
    out,
    near_keep,
    near_send,
    far_keep,
    far_send,
    sums,
    nat_grad,
    grad_q,
    grad_k,
    grad_v,
    offsets,
):
    run, length = scalars[0], scalars[1]
    blocks = nat.shape[0] // BLOCK
    mine = nat.shape[1] // 3
    for j, rows in enumerate((own[...], beside[...], across[...], far[...])):
        place = pl.ds(pl.multiple_of((run ^ j) * BLOCK, BLOCK), BLOCK)
        nat_grad[place, :] = rows
    distances(offsets)
    grad_k[...] = jnp.zeros_like(grad_k)
    grad_v[...] = jnp.zeros_like(grad_v)
    scale = jnp.asarray(HEAD_DIM**-0.5, BF)
    for pair in range(mine // 128):
        lanes = slice(pair * 128, (pair + 1) * 128)
        k_lanes = slice(mine + pair * 128, mine + (pair + 1) * 128)
        v_lanes = slice(2 * mine + pair * 128, 2 * mine + (pair + 1) * 128)
        for i in range(blocks):
            grad_rows = nat_grad[block(i), lanes]
            product = grad_rows.astype(F32) * att[block(i), lanes]
            ones = lax.broadcasted_iota(jnp.int32, (8, 128), 1) // HEAD_DIM
            ones = (ones == lax.broadcasted_iota(jnp.int32, (8, 128), 0)).astype(F32)
            delta = lax.dot_general(
                ones,
                product,
                (((1,), (1,)), ((), ())),
                precision=lax.Precision.HIGHEST,
                preferred_element_type=F32,
            )
            sum_q = jnp.zeros((128, BLOCK), F32)
            for head in range(2):
                number = pair * 2 + head
                slope = slopes[number]
                query = halves(nat[block(i), lanes], head) * scale
                grad_head = halves(grad_rows, head)
                row_lse = lse[number : number + 1, block(i)]
                row_delta = delta[head : head + 1, :]
                for j in range(i + 1):
                    keys = nat[block(j), k_lanes]
                    tile, seen = masked_scores(keys, query, i, j, slope, offsets[...], length)
                    probs = jnp.exp(tile - row_lse)
                    if seen is not None:
                        probs = jnp.where(seen, probs, 0.0)
                    grad_probs = nt(nat[block(j), v_lanes], grad_head)
                    grad_scores = (probs * (grad_probs - row_delta)).astype(BF)
                    grad_v[block(j), lanes] += nn(probs.astype(BF), grad_head)
                    grad_k[block(j), lanes] += nn(grad_scores, query)
                    sum_q = sum_q + tn(halves(keys, head), grad_scores)
            grad_q[block(i), lanes] = (jnp.transpose(sum_q) * HEAD_DIM**-0.5).astype(BF)
    sums[...] = jnp.zeros_like(sums)
    for j in range(4):
        place = pl.ds(pl.multiple_of((run ^ j) * BLOCK, BLOCK), BLOCK)
        out[block(j), :mine] = grad_q[place, :]
        out[block(j), mine : 2 * mine] = grad_k[place, :].astype(BF)
        out[block(j), 2 * mine :] = grad_v[place, :].astype(BF)
        rows = out[block(j), :]
        sums[0:1, :] += jnp.sum(rows.astype(F32), axis=0, keepdims=True)
        partial = nt(rows, w_qkv[...])
        if j == 0:
            near_keep[...] = partial
        elif j == 1:
            near_send[...] = partial.astype(BF)
        elif j == 2:
            far_keep[...] = partial
        else:
            far_send[...] = partial.astype(BF)


def attend(blocks, w_qkv, bias, scalars, slopes):
    rows, width = blocks[0].shape
    columns = w_qkv.width
    mine = columns // 3
    outs = [
        ((4 * rows, columns), BF),
        ((4 * rows, mine), F32),
        ((rows, mine), BF),
        ((rows, mine), BF),
        ((rows, mine), BF),
        ((rows, mine), BF),
        ((8, 4 * rows), F32),
    ]
    scratch = [
        pltpu.VMEM((4, rows, mine), BF),
        pltpu.VMEM((4 * rows, BLOCK), F32),
        pltpu.VMEM((BLOCK, BLOCK), F32),
    ]
    inputs = (scalars, slopes, *blocks, w_qkv, bias)
    specs = [SMEM, SMEM] + [VMEM] * 6
    return kernel_call(attend_kernel, "attend", inputs, outs, scratch, specs)


def attend_back(nat, parts, att, lse, w_qkv, scalars, slopes):
    total, columns = nat.shape
    rows, mine = total // 4, columns // 3
    width = w_qkv.rows * lax.axis_size("fsdp")
    outs = [
        ((total, columns), BF),
        ((rows, width), F32),
        ((rows, width), BF),
        ((rows, width), F32),
        ((rows, width), BF),
        ((8, columns), F32),
    ]
    scratch = [
        pltpu.VMEM((total, mine), BF),
        pltpu.VMEM((total, mine), BF),
        pltpu.VMEM((total, mine), F32),
        pltpu.VMEM((total, mine), F32),
        pltpu.VMEM((BLOCK, BLOCK), F32),
    ]
    inputs = (scalars, slopes, nat, *parts, att, lse, w_qkv)
    specs = [SMEM, SMEM] + [VMEM] * 8
    return kernel_call(attend_back_kernel, "attend_back", inputs, outs, scratch, specs)


def shards(
    tokens,
    lengths,
    cotangent,
    ln1_gain,
    ln1_bias,
    qkv_weight,
    query_bias,
    value_bias,
    out_weight,
    out_bias,
    ln2_gain,
    ln2_bias,
    up_weight,
    up_bias,
    down_weight,
    down_bias,
):
    fsdp = lax.axis_size("fsdp")
    run = lax.axis_index("seq")
    rows, width = tokens.shape[1:]
    hidden = up_weight.shape[2]
    heads = HEADS // 4
    mine = width // 4
    half = width // 2
    ffn_size = hidden // 4
    part = width // fsdp
    piece = hidden // fsdp // 4
    me = lax.axis_index("fsdp")
    scalars = jnp.stack([run.astype(jnp.int32), lengths[0]])
    place = jnp.stack([run, me % 2]).astype(jnp.int32)
    slopes = lax.dynamic_slice_in_dim(head_slopes(), run * heads, heads)

    def quarter(value, axis):
        size = value.shape[axis] // 4
        return lax.dynamic_slice_in_dim(value, run * size, size, axis)

    def core_half(value, axis):
        return lax.dynamic_slice_in_dim(value, (run % 2) * half, half, axis)

    def qkv_of(layer):
        return quarter(qkv_weight[layer].reshape(part, 3, width), 2).reshape(part, 3 * mine)

    def out_of(layer):
        return core_half(out_weight[layer], 1)

    def up_of(layer):
        return quarter(up_weight[layer].reshape(part, fsdp, -1), 2).reshape(part, ffn_size)

    def down_of(layer):
        return quarter(down_weight[layer], 0)

    def seq_blocks(own):
        across = y_swap(own)
        return [own, core_swap(own), across, core_swap(across)]

    def summed(near, far):
        far = far_sum(far)
        return near[0], core_swap(near[1]), y_swap(far)

    def far_sum(far):
        return (far[0] + core_swap(far[1]).astype(F32)).astype(BF)

    vectors = (ln1_gain, ln1_bias, query_bias, value_bias, out_bias, ln2_gain, ln2_bias, down_bias)
    small = jnp.concatenate([jnp.stack(vectors, 1).reshape(LAYERS, -1), up_bias], axis=1)
    columns = 3 * mine
    extra = small.size // columns
    small = jnp.pad(small.reshape(extra, columns), ((0, -extra % 16), (0, 0)))
    stride = part + small.shape[0]
    own = pack(["qkv", "small"], [qkv_weight, small], 0, place, stride, columns)
    token_blocks = seq_blocks(tokens[0])
    even = [own] + [hop(own, "fsdp", 2 * k) for k in range(1, fsdp // 2 - 1)]
    even.append(hop(tied(own, even[1]), "fsdp", fsdp - 2))
    first = jnp.concatenate(even)
    first = (first, x_swap(first))
    cot_blocks = seq_blocks(cotangent[0])
    token_blocks, cot_blocks, first = meet(token_blocks, cot_blocks, first)
    arrays = dict(qkv=qkv_weight, out=out_weight, up=up_weight, down=down_weight)
    sizes = dict(qkv=columns, out=half, up=ffn_size, down=width)

    def bundle(layer, names):
        if part % 128:
            parts = dict(qkv=qkv_of, out=out_of, up=up_of, down=down_of)
            return jnp.concatenate([parts[name](layer) for name in names], axis=1)
        total = sum(sizes[name] for name in names)
        return pack(names, [arrays[name] for name in names], layer, place, part, total)

    packs = [
        bundle(0, ["out", "up"]),
        bundle(0, ["down"]),
        bundle(1, ["qkv", "out"]),
        bundle(1, ["up"]),
        bundle(1, ["down"]),
    ]
    keys = jnp.stack([me, me % 2]).astype(jnp.int32)
    early_one, late_one, early_two, up_two, down_two = (gather_z(item) for item in packs)

    def matrix(halves, column, size, key=1):
        return Slots(halves, column, size, part, keys, key)

    def out_matrices(halves, column):
        own = assemble(halves, column, half, part, me % 2)
        return own, core_swap(own)

    small = [item.reshape(fsdp // 2, stride, columns)[:, part : part + extra] for item in first]
    small = jnp.stack(small, 1).reshape(fsdp, LAYERS, -1)
    small = jnp.take(small, me ^ jnp.arange(fsdp), axis=0).astype(F32)
    tables, biases = [], []
    for layer in range(LAYERS):
        table = small[:, layer, : 8 * part].reshape(fsdp, 8, part)
        table = jnp.transpose(table, (1, 0, 2)).reshape(8, width)
        bias_q, bias_v = quarter(table[BIAS_Q], 0), quarter(table[BIAS_V], 0)
        bias_qkv = jnp.concatenate([bias_q, jnp.zeros_like(bias_q), bias_v])
        bias_up = quarter(small[:, layer, 8 * part :], 1)
        tables.append(table)
        biases.append((bias_qkv.reshape(1, -1), bias_up.reshape(1, -1)))

    stream = tokens[0].astype(F32)
    token_blocks, tables, biases = meet(token_blocks, tables, biases)
    h1 = first_norm(token_blocks, tables[0])
    w_qkv = matrix(first, 0, columns, 0)
    out_one, up_one = early_one[:, :half], early_one[:, half:]
    moved_out, moved = x_swap(out_one), x_swap(up_one)
    saved, weights = [], []
    for layer in range(LAYERS):
        top = layer + 1 == LAYERS
        bias_qkv, bias_up = biases[layer]
        packed, attended, *low, lse = attend(h1, w_qkv, bias_qkv, scalars, slopes)
        if top:
            w_outs = out_matrices(early_two, columns)
        else:
            low, moved_out = meet(low, moved_out)
            w_outs = out_matrices((out_one, moved_out), 0)
        far = y_swap(low[3])
        across = y_swap(low[2])
        if not top:
            across, far, moved, late_one = meet(across, far, moved, late_one)
            moved_late = x_swap(late_one)
        parts = [low[0], core_swap(low[1]), across, core_swap(far)]
        middle, normed, att_own = out_step(scalars, parts, w_outs, stream, tables[layer])
        h2 = seq_blocks(normed)
        if top:
            middle, moved_late = meet(middle, moved_late)
            w_up = matrix((up_two, moved_up), 0, ffn_size)
            w_down = matrix((down_two, moved_late), 0, width)
            near = ffn(h2[0], h2[1], w_up, bias_up, w_down)
            near_back = ffn_back(cot_blocks[0], cot_blocks[1], near[1], w_up, w_down)
            h2[2], near, near_back = meet(h2[2], near, near_back)
            h2[3] = core_swap(h2[2])
        else:
            h2[2], moved_late, early_two = meet(h2[2], moved_late, early_two)
            h2[3] = core_swap(h2[2])
            w_up = matrix((up_one, moved), 0, ffn_size)
            w_down = matrix((late_one, moved_late), 0, width)
            moved = x_swap(early_two)
            near = ffn(h2[0], h2[1], w_up, bias_up, w_down)
        far = ffn(h2[2], h2[3], w_up, bias_up, w_down)
        saved.append((stream, h1, packed, attended, lse, att_own, middle, h2, near[:2], far[:2]))
        weights.append((w_qkv, w_outs, w_up, w_down))
        if top:
            last_sums = near[2:], far[2:]
        else:
            sums, moved, up_two = meet(summed(near[2:], far[2:]), moved, up_two)
            early_two = (early_two, moved)
            w_qkv = matrix(early_two, 0, columns)
            moved_up = x_swap(up_two)
            stream, normed = layer_end(middle, sums, tables[layer], tables[layer + 1])
            h1 = seq_blocks(normed)
            h1[2], moved_up, down_two = meet(h1[2], moved_up, down_two)
            h1[3] = core_swap(h1[2])
            moved_late = x_swap(down_two)

    grad = cotangent[0].astype(F32)
    g_down = cot_blocks
    vectors = [None] * LAYERS
    upper, lower = [], []
    for layer in reversed(range(LAYERS)):
        top = layer + 1 == LAYERS
        totals = upper if top else lower
        w_qkv, w_outs, w_up, w_down = weights[layer]
        stream, h1, packed, attended, lse, att_own, middle, h2, act_near, act_far = saved[layer]
        if top:
            near = near_back
        else:
            near = ffn_back(g_down[0], g_down[1], act_near[1], w_up, w_down)
            g_down[2], near, late, moved_above = meet(g_down[2], near, late, moved_above)
            g_down[3] = core_swap(g_down[2])
            moved_late = x_swap(late[1])
        far = ffn_back(g_down[2], g_down[3], act_far[1], w_up, w_down)
        far_low = far_sum(far[1:3])
        acts, h2, far_low = meet([act_near[0], act_far[0]], h2, far_low)
        if not top:
            far_low, up_above = meet(far_low, up_above)
            reduced = added(up_above, moved_above)
            upper.append(scatter_z(reduced))
        sums = near[1], core_swap(near[2]), y_swap(far_low)
        if top:
            size = width * 3 // 4
            sent_down = weight_grad(acts, g_down, place, (size, width - size))
            size = ffn_size * 3 // 8
            sent_up = weight_grad(h2, [near[0], far[0]], place, (size, ffn_size - size))
            pair = zip(sent_down[2:], sent_up[:2])
            sent_both = [jnp.concatenate(item, axis=1) for item in pair]
            sent_down, sent_up = sent_down[:2], sent_up[2:]
            moved_both = x_swap(sent_both[1])
            sums, sent_both[0] = meet(sums, sent_both[0])
        else:
            sent_down = weight_grad(acts, g_down, place)
            sent_up = weight_grad(h2, [near[0], far[0]], place)
        moved_down, moved_up = x_swap(sent_down[1]), x_swap(sent_up[1])
        sums, sent_down[0], sent_up[0] = meet(sums, sent_down[0], sent_up[0])
        grad_middle, g_branch, *g_att, lines_two = out_back(
            scalars, sums, middle, grad, tables[layer], w_outs
        )
        g_att = [
            g_att[0],
            core_swap(g_att[1]),
            y_swap(g_att[2]),
            y_swap(core_swap(g_att[3])),
        ]
        if not top:
            g_att, moved_late = meet(g_att, moved_late)
            reduced = added(late[0], moved_late)
            g_att, reduced, upper[:3] = meet(g_att, reduced, upper[:3])
            upper.append(scatter_z(reduced))
        if top:
            g_att, last_sums = meet(g_att, last_sums)
        g_packed, *parts, packed_sum = attend_back(
            packed, g_att, attended, lse, w_qkv, scalars, slopes
        )
        if top:
            last_sums = summed(*last_sums)
            parts, moved_down, last_sums = meet(parts, moved_down, last_sums)
            result = layer_end(saved[layer][6], last_sums, tables[layer], None)[1]
        else:
            parts, moved_down = meet(parts, moved_down)
        far_low = far_sum(parts[2:])
        h1, sent_down[0], far_low = meet(h1, sent_down[0], far_low)
        if not layer:
            att_own, g_branch, far_low = meet(att_own, g_branch, far_low)
            keep, send = out_grad(att_own, g_branch, place)
        sent_qkv = weight_grad(h1, [g_packed], place)
        sums = parts[0], core_swap(parts[1]), y_swap(far_low)
        reduced = added(sent_down[0], moved_down)
        totals.append(scatter_z(reduced))
        sums, reduced, sent_qkv[0] = meet(sums, reduced, sent_qkv[0])
        if top:
            sums, moved_both = meet(sums, moved_both)
        else:
            sums, moved_up = meet(sums, moved_up)
            reduced = added(sent_up[0], moved_up)
            totals.append(scatter_z(reduced))
            sent_out = added_pair(keep, core_swap(send))
            late = [jnp.concatenate(pair, axis=1) for pair in zip(sent_qkv, sent_out)]
            sums, upper[3], late[0] = meet(sums, upper[3], late[0])
            one, two, three, last_piece = upper
            size = width // 4
            upper = [
                jnp.concatenate([one, two[:, :size]], axis=1),
                jnp.concatenate([two[:, size:], three], axis=1),
                last_piece,
            ]
        up_sum = near[3] + far[3]
        grad, normed, lines_one = layer_begin(sums, stream, grad_middle, tables[layer])
        if layer:
            normed, sent_both[0], sent_up[0], att_own, g_branch = meet(
                normed, sent_both[0], sent_up[0], att_own, g_branch
            )
            upper.append(scatter_z(added(sent_both[0], moved_both)))
            g_down = seq_blocks(normed)
            up_above, moved_above = sent_up[0], moved_up
            keep, send = out_grad(att_own, g_branch, place)
        else:
            grad, totals[0] = meet(grad, totals[0])
        if layer:
            sent_out = added_pair(keep, core_swap(send))
            late = [jnp.concatenate(pair, axis=1) for pair in zip(sent_qkv, sent_out)]
        else:
            upper = [four(item) for item in upper]
            totals[0] = four(totals[0])
            last, upper, totals = meet(added(late[0], x_swap(late[1])), upper, totals)
            lower = totals + [scatter_z(last)]

        vectors[layer] = (lines_two, lines_two, packed_sum, lines_one, up_sum)

    def spread(value, axis=0):
        shape = list(value.shape)
        size = shape[axis]
        shape[axis] = 4 * size
        return lax.dynamic_update_slice_in_dim(jnp.zeros(shape, F32), value, run * size, axis)

    small_sums = []
    vectors, grad = meet(vectors, grad)
    for _, lines_two, packed_sum, lines_one, up_sum in vectors:
        members = [
            lines_one[0],
            lines_one[1],
            spread(packed_sum[0, :mine]),
            spread(packed_sum[0, 2 * mine :]),
            lines_two[2],
            lines_two[0],
            lines_two[1],
            lines_two[3],
        ]
        small_sums.append(
            jnp.concatenate(
                [item.reshape(fsdp, part) for item in members]
                + [spread(up_sum.reshape(fsdp, piece), 1)],
                axis=1,
            )
        )

    starts = ((2, 0), (2, columns), (1, 0), (0, 0))
    names = ("qkv", "out", "up", "down")
    matrices = finish(1, LAYERS, upper, starts, place, None, names)
    vector = sum_small(jnp.stack(small_sums, axis=1))
    middle, vector, result = meet(four(lower[1]), vector, result)
    groups = [lower[0], middle]
    ffn_grads = finish(0, LAYERS, groups, starts, place, list(matrices[2:]), names[2:])
    last, ffn_grads, matrices, vector = meet(lower[2], ffn_grads, matrices[:2], vector)
    starts = ((0, 0), (0, columns), (0, 0), (0, 0))
    matrices = finish(0, LAYERS, [four(last)], starts, place, list(matrices), names[:2])
    grad_qkv_w, grad_out_w = matrices
    grad_up_w, grad_down_w = ffn_grads
    if piece % 128:
        grad_up_w = grad_up_w.reshape(LAYERS, part, 4, fsdp, piece)
        grad_up_w = jnp.swapaxes(grad_up_w, 2, 3).reshape(LAYERS, part, hidden)
    lines = [vector[:, i * part : (i + 1) * part] for i in range(8)]
    gain_one, shift_one, bias_q, bias_v, bias_o, gain_two, shift_two, bias_down = lines
    return (
        result[None],
        grad[None],
        gain_one,
        shift_one,
        grad_qkv_w,
        bias_q,
        bias_v,
        grad_out_w,
        bias_o,
        gain_two,
        shift_two,
        grad_up_w,
        vector[:, 8 * part :],
        grad_down_w,
        bias_down,
    )


def solution(mesh):
    vector = P(None, "fsdp")
    matrix = P(None, "fsdp", None)
    data = P("fsdp", "seq", None)
    weight_specs = (
        vector,
        vector,
        matrix,
        vector,
        vector,
        matrix,
        vector,
        vector,
        vector,
        matrix,
        vector,
        matrix,
        vector,
    )
    in_specs = (data, P("fsdp"), data) + weight_specs
    out_specs = (data, data) + weight_specs
    return jax.shard_map(shards, mesh=mesh, in_specs=in_specs, out_specs=out_specs, check_vma=False)
```

```python
import functools

import jax
import jax.numpy as jnp
from jax import lax
from jax.experimental import pallas as pl
from jax.experimental.pallas import tpu as pltpu
from jax.sharding import PartitionSpec as P

HEADS = 16
HEAD_DIM = 64
LAYERS = 2
BLOCK = 256
EPS = 1e-05
NEG = -1e30
BF = jnp.bfloat16
F32 = jnp.float32
GELU = 0.7978845608028654
CUBIC = 0.044715
VMEM = pl.BlockSpec(memory_space=pltpu.VMEM)
SMEM = pl.BlockSpec(memory_space=pltpu.SMEM)


def head_slopes():
    return jnp.exp2(-8.0 * (jnp.arange(HEADS, dtype=F32) + 1.0) / HEADS)


def hop(value, axis, mask):
    size = lax.axis_size(axis)
    return lax.ppermute(value, axis, [(i, i ^ mask) for i in range(size)])


def core_swap(value):
    return hop(value, "seq", 1)


def y_swap(value):
    return hop(value, "seq", 2)


def sum_small(full):
    size = lax.axis_size("fsdp")
    me = lax.axis_index("fsdp")
    full = full + y_swap(full)
    full = full + core_swap(full)
    slots = jnp.take(full, me ^ jnp.arange(size), axis=0)
    slots = slots.reshape((size // 2, 2) + full.shape[1:])
    slots = slots[:, 0] + hop(slots[:, 1], "fsdp", 1)
    total = slots[0]
    for k in range(1, size // 2):
        total = total + hop(slots[k], "fsdp", 2 * k)
    return total


def assemble_kernel(column, stride, key_ref, same, other, out, held, sems):
    key = key_ref[0]
    pairs, rows, width = held.shape[0] // 2, held.shape[1], held.shape[2]
    loads, stores = [], []
    for r in range(2 * pairs):
        place = pl.ds(r // 2 * stride, rows)
        source = (other if r % 2 else same).at[place, pl.ds(column, width)]
        loads.append(pltpu.make_async_copy(source, held.at[r], sems.at[r, 0]))
        start = pl.multiple_of((r ^ key) * rows, rows)
        target = out.at[pl.ds(start, rows), :]
        stores.append(pltpu.make_async_copy(held.at[r], target, sems.at[r, 1]))
    for load in loads:
        load.start()
    for load, store in zip(loads, stores):
        load.wait()
        store.start()
    for store in stores:
        store.wait()


def assemble(halves, column, width, rows, key):
    slots = lax.axis_size("fsdp")
    stride = 2 * halves[0].shape[0] // slots
    key = key.astype(jnp.int32).reshape(1)
    hbm = pl.BlockSpec(memory_space=pl.ANY)
    return pl.pallas_call(
        functools.partial(assemble_kernel, column, stride),
        grid_spec=pltpu.PrefetchScalarGridSpec(
            num_scalar_prefetch=1,
            grid=(),
            in_specs=[hbm] * 2,
            out_specs=hbm,
            scratch_shapes=[
                pltpu.VMEM((slots, rows, width), BF),
                pltpu.SemaphoreType.DMA((slots, 2)),
            ],
        ),
        out_shape=jax.ShapeDtypeStruct((slots * rows, width), BF),
        compiler_params=pltpu.CompilerParams(vmem_limit_bytes=32 << 20),
        cost_estimate=pl.CostEstimate(flops=0, bytes_accessed=0, transcendentals=0),
        name="assemble",
    )(key, *halves)


def tied(value, after):
    return lax.optimization_barrier((value, after))[0]


def meet(*values):
    return lax.optimization_barrier(values)


def pack_kernel(names, layer, place, *refs):
    sources, (out, sems) = dict(zip(names, refs)), refs[len(names) :]
    run = place[0]
    copies = []
    column = 0

    def add(source, size, rows=None):
        rows = source.shape[0] if rows is None else rows
        target = out.at[pl.ds(0, rows), pl.ds(column, size)]
        copies.append(pltpu.make_async_copy(source, target, sems.at[len(copies)]))
        return column + size

    for name in names:
        source = sources[name]
        if name == "small":
            rows = source.shape[0]
            target = out.at[pl.ds(out.shape[0] - rows, rows), :]
            copies.append(pltpu.make_async_copy(source, target, sems.at[len(copies)]))
            continue
        source = source.at[layer]
        part, width = source.shape
        if name == "qkv":
            for third in range(3):
                start = pl.multiple_of((4 * third + run) * (width // 12), width // 12)
                column = add(source.at[:, pl.ds(start, width // 12)], width // 12)
        elif name == "out":
            start = pl.multiple_of(run % 2 * (width // 2), width // 2)
            column = add(source.at[:, pl.ds(start, width // 2)], width // 2)
        elif name == "up":
            piece = part
            for slot in range(width // (4 * piece)):
                start = pl.multiple_of((4 * slot + run) * piece, piece)
                column = add(source.at[:, pl.ds(start, piece)], piece)
        else:
            start = pl.multiple_of(run * (part // 4), part // 4)
            column = add(source.at[pl.ds(start, part // 4), :], width)
    for copy in copies:
        copy.start()
    for copy in copies:
        copy.wait()


def pack(names, arrays, layer, place, rows, columns):
    count = sum({"qkv": 3, "up": arrays[0].shape[-1]}.get(name, 1) for name in names)
    hbm = pl.BlockSpec(memory_space=pl.ANY)
    return pl.pallas_call(
        functools.partial(pack_kernel, names, layer),
        in_specs=[SMEM] + [hbm] * len(arrays),
        out_specs=VMEM,
        out_shape=jax.ShapeDtypeStruct((rows, columns), BF),
        scratch_shapes=[pltpu.SemaphoreType.DMA((min(count, 64),))],
        compiler_params=pltpu.CompilerParams(vmem_limit_bytes=32 << 20),
        cost_estimate=pl.CostEstimate(flops=0, bytes_accessed=0, transcendentals=0),
        name="pack",
    )(place, *arrays)


def z_groups():
    size = lax.axis_size("fsdp")
    return [[x + 2 * k for k in range(size // 2)] for x in range(2)]


def gather_z(own):
    return lax.all_gather(own, "fsdp", axis=0, tiled=True, axis_index_groups=z_groups())


def x_swap(value):
    return hop(value, "fsdp", 1)


def scatter_z(same):
    return lax.psum_scatter(
        same, "fsdp", scatter_dimension=0, tiled=True, axis_index_groups=z_groups()
    )


def four(total):
    across = y_swap(total)
    return total, core_swap(total), across, core_swap(across)


class Slots:
    def __init__(self, halves, column, width, rows, keys, key):
        self.halves, self.column, self.width, self.rows = halves, column, width, rows
        self.keys, self.key = keys, key

    def copies(self, keys, same, other, buffer):
        count = buffer.shape[0] // self.rows
        stride = 2 * same.shape[0] // count
        for r in range(count):
            source = other if r % 2 else same
            source = source.at[pl.ds(r // 2 * stride, self.rows), pl.ds(self.column, self.width)]
            start = pl.multiple_of((r ^ keys[self.key]) * self.rows, self.rows)
            yield source, buffer.at[pl.ds(start, self.rows), :]


def staged(body, plan, stored, refs):
    refs = list(refs)
    keys = refs.pop(0) if any(isinstance(item, Slots) for item in plan) else None
    taken = [refs.pop(0) for item in plan for _ in range(1 + isinstance(item, Slots))]
    sems = refs.pop()
    results = [refs.pop() for _ in stored][::-1]
    places = [i for i, item in enumerate(plan) if item is not None]
    buffers = refs[len(refs) - len(places) :]
    refs = refs[: len(refs) - len(places)]
    inputs, copies = [], []
    for item in plan:
        if item is None:
            inputs.append(taken.pop(0))
            continue
        buffer = buffers.pop(0)
        inputs.append(buffer)
        if item is VMEM:
            moves = [(taken.pop(0), buffer)]
        else:
            moves = item.copies(keys, taken.pop(0), taken.pop(0), buffer)
        for source, target in moves:
            copies.append(pltpu.make_async_copy(source, target, sems.at[len(copies)]))
    for copy in copies:
        copy.start()
    for copy in copies:
        copy.wait()
    first = len(copies)
    stores = {}
    for number, (i, result) in enumerate(zip(stored, results)):
        stores[i] = pltpu.make_async_copy(result, refs[i], sems.at[first + number])
        refs[i] = result
    waiting = list(stored)
    steps = body(*inputs, *refs)
    for i in steps if stored and steps is not None else ():
        stores[i].start()
        waiting.remove(i)
    for i in waiting:
        stores[i].start()
    for store in stores.values():
        store.wait()


def kernel_call(body, name, inputs, outputs, scratch=(), in_specs=None, cost=0, stored=()):
    plan, arrays, specs, buffers, keys = [], [], [], [], None
    count = 1
    hbm = pl.BlockSpec(memory_space=pl.ANY)
    for item, spec in zip(inputs, in_specs or [VMEM] * len(inputs)):
        if isinstance(item, Slots):
            shape = (lax.axis_size("fsdp") * item.rows, item.width)
            plan.append(item)
            arrays += item.halves
            specs += [hbm, hbm]
            buffers.append(pltpu.VMEM(shape, BF))
            keys = item.keys
            count += lax.axis_size("fsdp")
            continue
        arrays.append(item)
        plan.append(VMEM if spec is VMEM else None)
        specs.append(hbm if spec is VMEM else SMEM)
        if spec is VMEM:
            buffers.append(pltpu.VMEM(item.shape, item.dtype))
            count += 1
    if keys is not None:
        arrays, specs = [keys] + arrays, [SMEM] + specs
    buffers += [pltpu.VMEM(*outputs[i]) for i in stored]
    there = pl.BlockSpec(memory_space=pltpu.HBM)
    return pl.pallas_call(
        lambda *refs: staged(body, plan, stored, refs),
        in_specs=specs,
        out_specs=[there if i in stored else VMEM for i in range(len(outputs))],
        out_shape=[jax.ShapeDtypeStruct(shape, kind) for shape, kind in outputs],
        scratch_shapes=[*scratch, *buffers, pltpu.SemaphoreType.DMA((count + len(stored),))],
        compiler_params=pltpu.CompilerParams(vmem_limit_bytes=48 << 20),
        cost_estimate=pl.CostEstimate(flops=0, bytes_accessed=cost, transcendentals=0),
        name=name,
    )(*arrays)


def pair_kernel(keep, received, same, other):
    for i, target in enumerate((same, other)):
        target[...] = (keep[i].astype(F32) + received[i].astype(F32)).astype(BF)


def added_pair(keep, received):
    outs = [(keep.shape[1:], BF)] * 2
    return kernel_call(pair_kernel, "added_pair", (keep, received), outs)


def add_kernel(same, *refs):
    out = refs[-1]
    start = 0
    for item in refs[:-1]:
        rows = slice(start, start + item.shape[0])
        out[rows, :] = (same[rows, :].astype(F32) + item[...].astype(F32)).astype(BF)
        start += item.shape[0]


def added(same, *received):
    return kernel_call(add_kernel, "added", (same, *received), [(same.shape, BF)])[0]


def nn(left, right):
    return jnp.dot(left, right, preferred_element_type=F32)


def nt(left, right):
    return lax.dot_general(left, right, (((1,), (1,)), ((), ())), preferred_element_type=F32)


def tn(left, right):
    return lax.dot_general(left, right, (((0,), (0,)), ((), ())), preferred_element_type=F32)


def normalized(value):
    center = value - jnp.mean(value, axis=-1, keepdims=True)
    scale = lax.rsqrt(jnp.mean(center * center, axis=-1, keepdims=True) + EPS)
    return center * scale, scale


def norm_back(value, gain, grad):
    hat, scale = normalized(value)
    inner = grad * gain
    mean = jnp.mean(inner, axis=-1, keepdims=True)
    along = jnp.mean(inner * hat, axis=-1, keepdims=True)
    grad_gain = jnp.sum(grad * hat, axis=0, keepdims=True)
    return scale * (inner - mean - hat * along), grad_gain, jnp.sum(grad, axis=0, keepdims=True)


GAIN_ONE, SHIFT_ONE, BIAS_Q, BIAS_V, BIAS_OUT, GAIN_TWO, SHIFT_TWO, BIAS_DOWN = range(8)


def row(table, index):
    return table[index : index + 1, :]


def first_norm_kernel(a, b, c, d, table, *outs):
    for value, out in zip((a, b, c, d), outs):
        hat, _ = normalized(value[...].astype(F32))
        out[...] = (hat * row(table, GAIN_ONE) + row(table, SHIFT_ONE)).astype(BF)


def first_norm(blocks, table):
    outs = [(item.shape, BF) for item in blocks]
    return kernel_call(first_norm_kernel, "first_norm", (*blocks, table), outs)


def layer_end_kernel(middle, keep, beside, across, table, after, stream, normed):
    total = keep[...] + beside[...].astype(F32) + across[...].astype(F32)
    value = middle[...] + (total + row(table, BIAS_DOWN))
    stream[...] = value
    if after is None:
        normed[...] = value.astype(BF)
    else:
        hat, _ = normalized(value)
        normed[...] = (hat * row(after, GAIN_ONE) + row(after, SHIFT_ONE)).astype(BF)


def last_end_kernel(middle, keep, beside, across, table, stream, low):
    layer_end_kernel(middle, keep, beside, across, table, None, stream, low)


def layer_end(middle, sums, table, after):
    outs = [(middle.shape, F32), (middle.shape, BF)]
    if after is None:
        return kernel_call(last_end_kernel, "last_end", (middle, *sums, table), outs)
    inputs = (middle, *sums, table, after)
    return kernel_call(layer_end_kernel, "layer_end", inputs, outs, stored=(0,))


def out_kernel(
    scalars, own, beside, across, far, w_own, w_other, stream, table, middle, normed, attended
):
    run = scalars[0]
    core = run % 2
    parts = [own[...], beside[...], across[...], far[...]]
    size = parts[0].shape[1]
    starts = [pl.multiple_of((run ^ j) * size, size) for j in range(4)]
    for part, start in zip(parts, starts):
        attended[:, pl.ds(start, size)] = part
    yield 2
    half = w_own.shape[1]
    for weight, place in ((w_own, core), (w_other, 1 - core)):
        total = None
        for part, start in zip(parts, starts):
            term = nn(part, weight[pl.ds(start, size), :])
            total = term if total is None else total + term
        lanes = pl.ds(pl.multiple_of(place * half, half), half)
        bias = table[BIAS_OUT : BIAS_OUT + 1, lanes]
        middle[:, lanes] = stream[:, lanes] + (total + bias)
    yield 0
    hat, _ = normalized(middle[...])
    normed[...] = (hat * row(table, GAIN_TWO) + row(table, SHIFT_TWO)).astype(BF)


def out_step(scalars, parts, w_outs, stream, table):
    outs = [(stream.shape, F32), (stream.shape, BF), (stream.shape, BF)]
    inputs = (scalars, *parts, *w_outs, stream, table)
    specs = [SMEM] + [VMEM] * 8
    return kernel_call(out_kernel, "out_step", inputs, outs, in_specs=specs, stored=(0, 2))


def ffn_kernel(a, b, w_up, bias, w_down, act, slope, keep, send, source):
    rows = a.shape[0]
    source[:rows, :] = a[...]
    source[rows:, :] = b[...]
    pre = nn(source[...], w_up[...]) + bias[...]
    square = pre * pre
    bent = jnp.tanh(GELU * pre * (1.0 + CUBIC * square))
    half = 0.5 + 0.5 * bent
    value = (pre * half).astype(BF)
    act[...] = value
    yield 0
    rise = half + (0.5 * GELU) * pre * (1.0 - bent * bent) * (1.0 + 3.0 * CUBIC * square)
    slope[...] = rise.astype(BF)
    yield 1
    total = nn(value, w_down[...])
    keep[...] = total[:rows, :]
    send[...] = total[rows:, :].astype(BF)


def ffn(a, b, w_up, bias, w_down):
    rows, width = a.shape
    hidden = w_up.width
    outs = [
        ((2 * rows, hidden), BF),
        ((2 * rows, hidden), BF),
        ((rows, width), F32),
        ((rows, width), BF),
    ]
    scratch = [pltpu.VMEM((2 * rows, width), BF)]
    inputs = (a, b, w_up, bias, w_down)
    return kernel_call(ffn_kernel, "ffn", inputs, outs, scratch, stored=(0, 1))


def ffn_back_kernel(a, b, slope, w_up, w_down, grad_pre, keep, send, sums, source):
    rows = a.shape[0]
    source[:rows, :] = a[...]
    source[rows:, :] = b[...]
    grad_act = nt(source[...], w_down[...])
    value = (grad_act * slope[...].astype(F32)).astype(BF)
    grad_pre[...] = value
    sums[...] = jnp.sum(value.astype(F32), axis=0, keepdims=True)
    total = nt(value, w_up[...])
    keep[...] = total[:rows, :]
    send[...] = total[rows:, :].astype(BF)


def ffn_back(a, b, slope, w_up, w_down):
    rows, width = a.shape
    hidden = w_up.width
    outs = [
        ((2 * rows, hidden), BF),
        ((rows, width), F32),
        ((rows, width), BF),
        ((1, hidden), F32),
    ]
    scratch = [pltpu.VMEM((2 * rows, width), BF)]
    return kernel_call(ffn_back_kernel, "ffn_back", (a, b, slope, w_up, w_down), outs, scratch)


def weight_grad_kernel(count, parts, scalars, *refs):
    x = scalars[1]
    lefts, rights = refs[: parts[0]], refs[parts[0] : parts[0] + parts[1]]
    *outs, left, right, total = refs[parts[0] + parts[1] :]
    for sources, target in ((lefts, left), (rights, right)):
        start = 0
        for source in sources:
            target[start : start + source.shape[0], :] = source[...]
            start += source.shape[0]
    total[...] = tn(left[...], right[...]).astype(BF)
    rows = total.shape[0] // count
    first = 0
    for same, other in zip(outs[::2], outs[1::2]):
        columns = slice(first, first + same.shape[1])
        first += same.shape[1]
        for r in range(count):
            start = pl.multiple_of((r ^ x) * rows, rows)
            target = other if r % 2 else same
            target[r // 2 * rows : (r // 2 + 1) * rows, :] = total[pl.ds(start, rows), columns]


def weight_grad(lefts, rights, place, cuts=()):
    count = lax.axis_size("fsdp")
    total = sum(item.shape[0] for item in lefts)
    tall, wide = lefts[0].shape[1], rights[0].shape[1]
    outs = [((tall // 2, size), BF) for size in cuts or (wide,) for _ in range(2)]
    scratch = [
        pltpu.VMEM((total, tall), BF),
        pltpu.VMEM((total, wide), BF),
        pltpu.VMEM((tall, wide), BF),
    ]
    inputs = (place, *lefts, *rights)
    body = functools.partial(weight_grad_kernel, count, (len(lefts), len(rights)))
    specs = [SMEM] + [VMEM] * (len(inputs) - 1)
    return list(kernel_call(body, "weight_grad", inputs, outs, scratch, specs))


def out_grad_kernel(count, place, left, right, keep, send, total):
    core, x = place[0] % 2, place[1]
    half = keep.shape[2]
    rows = total.shape[0] // count
    for target, number in ((keep, core), (send, 1 - core)):
        lanes = pl.ds(pl.multiple_of(number * half, half), half)
        total[...] = tn(left[...], right[:, lanes]).astype(BF)
        for r in range(count):
            start = pl.multiple_of((r ^ x) * rows, rows)
            target[r % 2, r // 2 * rows : (r // 2 + 1) * rows, :] = total[pl.ds(start, rows), :]


def out_grad(left, right, place):
    count = lax.axis_size("fsdp")
    tall, wide = left.shape[1], right.shape[1]
    outs = [((2, tall // 2, wide // 2), BF)] * 2
    scratch = [pltpu.VMEM((tall, wide // 2), BF)]
    body = functools.partial(out_grad_kernel, count)
    return kernel_call(
        body, "out_grad", (place, left, right), outs, scratch, [SMEM, VMEM, VMEM]
    )


def finish_kernel(layout, slots, aliased, place, *refs):
    run = place[0]
    groups = []
    for number in range(layout[-1]):
        groups.append(refs[4 * number : 4 * number + 4])
    refs = refs[4 * layout[-1] + aliased :]
    names = layout[1]
    outs = dict(zip(names, refs))
    part = groups[0][0].shape[0]
    width = part * slots
    mine, half, size = width // 4, width // 2, width
    piece = size // slots
    (q_group, q_start), (o_group, o_start), (u_group, u_start), (d_group, d_start) = layout[0]
    qkv, out, up, down = (outs.get(name) for name in ("qkv", "out", "up", "down"))
    for j in range(4):
        owner = run ^ j
        for third in range(3 if qkv is not None else 0):
            lanes = pl.ds(pl.multiple_of(third * width + owner * mine, mine), mine)
            start = q_start + third * mine
            qkv[0, :, lanes] = groups[q_group][j][:, start : start + mine].astype(F32)
        if up is None:
            continue
        if piece % 128:
            lanes = pl.ds(pl.multiple_of(owner * size, size), size)
            up[0, :, lanes] = groups[u_group][j][:, u_start : u_start + size].astype(F32)
        else:
            for slot in range(slots):
                lanes = pl.ds(pl.multiple_of((4 * slot + owner) * piece, piece), piece)
                start = u_start + slot * piece
                up[0, :, lanes] = groups[u_group][j][:, start : start + piece].astype(F32)
        rows = pl.ds(pl.multiple_of(owner * part, part), part)
        down[0, rows, :] = groups[d_group][j][:, d_start : d_start + width].astype(F32)
    for j in range(2 if out is not None else 0):
        lanes = pl.ds(pl.multiple_of((run ^ j) % 2 * half, half), half)
        columns = slice(o_start, o_start + half)
        first, second = groups[o_group][j][:, columns], groups[o_group][j + 2][:, columns]
        out[0, :, lanes] = first.astype(F32) + second.astype(F32)


def finish(layer, layers, groups, starts, place, before, names):
    slots = lax.axis_size("fsdp")
    part = groups[0][0].shape[0]
    width = part * slots
    shapes = dict(
        qkv=(part, 3 * width), out=(part, width), up=(part, 4 * width), down=(4 * part, width)
    )
    shapes = [shapes[name] for name in names]
    inputs = [place] + [item for group in groups for item in group]
    count = len(inputs)
    specs = [SMEM] + [VMEM] * (count - 1)
    aliases = {}
    if before is not None:
        inputs += before
        specs += [pl.BlockSpec(memory_space=pl.ANY)] * len(names)
        aliases = {count + i: i for i in range(len(names))}
    layout = (starts, names, len(groups))
    return pl.pallas_call(
        functools.partial(finish_kernel, layout, slots, len(aliases)),
        grid=(1,),
        in_specs=specs,
        out_specs=[pl.BlockSpec((1,) + shape, lambda i: (layer, 0, 0)) for shape in shapes],
        out_shape=[jax.ShapeDtypeStruct((layers,) + shape, F32) for shape in shapes],
        input_output_aliases=aliases,
        compiler_params=pltpu.CompilerParams(vmem_limit_bytes=48 << 20),
        cost_estimate=pl.CostEstimate(flops=0, bytes_accessed=0, transcendentals=0),
        name="finish",
    )(*inputs)


def out_back_kernel(
    scalars,
    keep,
    beside,
    across,
    middle,
    grad,
    table,
    w_own,
    w_other,
    grad_middle,
    branch,
    first,
    second,
    third,
    fourth,
    sums,
):
    run = scalars[0]
    core = run % 2
    total = keep[...] + beside[...].astype(F32) + across[...].astype(F32)
    value, grad_gain, grad_shift = norm_back(middle[...], row(table, GAIN_TWO), total)
    value = grad[...] + value
    grad_middle[...] = value
    low = value.astype(BF)
    branch[...] = low
    sums[...] = jnp.zeros_like(sums)
    sums[0:1, :] = grad_gain
    sums[1:2, :] = grad_shift
    sums[2:3, :] = jnp.sum(low.astype(F32), axis=0, keepdims=True)
    sums[3:4, :] = jnp.sum(grad[...].astype(BF).astype(F32), axis=0, keepdims=True)
    size = first.shape[1]
    half = w_own.shape[1]
    for j, target in enumerate((first, second, third, fourth)):
        rows = pl.ds(pl.multiple_of((run ^ j) * size, size), size)
        result = None
        for weight, place in ((w_own, core), (w_other, 1 - core)):
            lanes = pl.ds(pl.multiple_of(place * half, half), half)
            term = nt(branch[:, lanes], weight[rows, :])
            result = term if result is None else result + term
        target[...] = result.astype(BF)


def out_back(scalars, sums, middle, grad, table, w_outs):
    rows, width = middle.shape
    mine = width // 4
    outs = [
        ((rows, width), F32),
        ((rows, width), BF),
        ((rows, mine), BF),
        ((rows, mine), BF),
        ((rows, mine), BF),
        ((rows, mine), BF),
        ((8, width), F32),
    ]
    inputs = (scalars, *sums, middle, grad, table, *w_outs)
    return kernel_call(out_back_kernel, "out_back", inputs, outs, in_specs=[SMEM] + [VMEM] * 8)


def layer_begin_kernel(
    keep, beside, across, stream, grad_middle, table, grad, low, sums
):
    total = keep[...] + beside[...].astype(F32) + across[...].astype(F32)
    value, grad_gain, grad_shift = norm_back(stream[...], row(table, GAIN_ONE), total)
    value = grad_middle[...] + value
    grad[...] = value
    low[...] = value.astype(BF)
    sums[...] = jnp.zeros_like(sums)
    sums[0:1, :] = grad_gain
    sums[1:2, :] = grad_shift


def layer_begin(sums, stream, grad_middle, table):
    shape = stream.shape
    outs = [(shape, F32), (shape, BF), ((8, shape[1]), F32)]
    return kernel_call(
        layer_begin_kernel, "layer_begin", (*sums, stream, grad_middle, table), outs
    )


def halves(value, head):
    lane = lax.broadcasted_iota(jnp.int32, value.shape, 1)
    return jnp.where((lane >= HEAD_DIM) == (head == 1), value, jnp.zeros_like(value))


def masked_scores(keys, query, i, j, slope, offsets, length):
    scores = nt(keys, query)
    if i == j:
        scores = scores - slope * jnp.abs(offsets)
    else:
        scores = scores - (slope * offsets + slope * float((i - j) * BLOCK))
    if j == 0:
        return scores, None
    return scores, j * BLOCK + lax.broadcasted_iota(jnp.int32, scores.shape, 0) < length


def block(i):
    return slice(i * BLOCK, (i + 1) * BLOCK)


def distances(ref):
    shape = (BLOCK, BLOCK)
    offsets = lax.broadcasted_iota(jnp.int32, shape, 1) - lax.broadcasted_iota(jnp.int32, shape, 0)
    ref[...] = offsets.astype(F32)


def attend_kernel(
    scalars,
    slopes,
    a,
    b,
    c,
    d,
    w_qkv,
    bias,
    nat,
    att,
    own,
    near,
    far,
    farther,
    lse,
    low,
    scores,
    offsets,
):
    run, length = scalars[0], scalars[1]
    blocks = nat.shape[0] // BLOCK
    mine = nat.shape[1] // 3
    for j, rows in enumerate((a, b, c, d)):
        place = pl.ds(pl.multiple_of((run ^ j) * BLOCK, BLOCK), BLOCK)
        nat[place, :] = (nn(rows[...], w_qkv[...]) + bias[...]).astype(BF)
    yield 0
    distances(offsets)
    for i in range(blocks):
        for pair in range(mine // 128):
            lanes = slice(pair * 128, (pair + 1) * 128)
            out = jnp.zeros((128, BLOCK), F32)
            for head in range(2):
                slope = slopes[pair * 2 + head]
                query = halves(nat[block(i), lanes], head) * jnp.asarray(HEAD_DIM**-0.5, BF)
                top = None
                for j in range(i + 1):
                    keys = nat[block(j), mine + pair * 128 : mine + (pair + 1) * 128]
                    tile, seen = masked_scores(keys, query, i, j, slope, offsets[...], length)
                    if seen is not None:
                        tile = jnp.where(seen, tile, NEG)
                    scores[block(j), :] = tile
                    tile_top = jnp.max(tile, axis=0, keepdims=True)
                    top = tile_top if top is None else jnp.maximum(top, tile_top)
                total = jnp.zeros((1, BLOCK), F32)
                summed = jnp.zeros((128, BLOCK), F32)
                for j in range(i + 1):
                    weights = jnp.exp(scores[block(j), :] - top)
                    total = total + jnp.sum(weights, axis=0, keepdims=True)
                    values = nat[block(j), 2 * mine + pair * 128 : 2 * mine + (pair + 1) * 128]
                    summed = summed + tn(halves(values, head), weights.astype(BF))
                out = out + summed / total
                lse[pair * 2 + head : pair * 2 + head + 1, block(i)] = top + jnp.log(total)
            rows = jnp.transpose(out)
            att[block(i), lanes] = rows
            low[run ^ i, :, lanes] = rows.astype(BF)
    own[...] = low[0]
    near[...] = low[1]
    far[...] = low[2]
    farther[...] = low[3]


def attend_back_kernel(
    scalars,
    slopes,
    nat,
    own,
    beside,
    across,
    far,
    att,
    lse,
    w_qkv,
    out,
    near_keep,
    near_send,
    far_keep,
    far_send,
    sums,
    nat_grad,
    grad_q,
    grad_k,
    grad_v,
    offsets,
):
    run, length = scalars[0], scalars[1]
    blocks = nat.shape[0] // BLOCK
    mine = nat.shape[1] // 3
    for j, rows in enumerate((own[...], beside[...], across[...], far[...])):
        place = pl.ds(pl.multiple_of((run ^ j) * BLOCK, BLOCK), BLOCK)
        nat_grad[place, :] = rows
    distances(offsets)
    grad_k[...] = jnp.zeros_like(grad_k)
    grad_v[...] = jnp.zeros_like(grad_v)
    scale = jnp.asarray(HEAD_DIM**-0.5, BF)
    for pair in range(mine // 128):
        lanes = slice(pair * 128, (pair + 1) * 128)
        k_lanes = slice(mine + pair * 128, mine + (pair + 1) * 128)
        v_lanes = slice(2 * mine + pair * 128, 2 * mine + (pair + 1) * 128)
        for i in range(blocks):
            grad_rows = nat_grad[block(i), lanes]
            product = grad_rows.astype(F32) * att[block(i), lanes]
            ones = lax.broadcasted_iota(jnp.int32, (8, 128), 1) // HEAD_DIM
            ones = (ones == lax.broadcasted_iota(jnp.int32, (8, 128), 0)).astype(F32)
            delta = lax.dot_general(
                ones,
                product,
                (((1,), (1,)), ((), ())),
                precision=lax.Precision.HIGHEST,
                preferred_element_type=F32,
            )
            sum_q = jnp.zeros((128, BLOCK), F32)
            for head in range(2):
                number = pair * 2 + head
                slope = slopes[number]
                query = halves(nat[block(i), lanes], head) * scale
                grad_head = halves(grad_rows, head)
                row_lse = lse[number : number + 1, block(i)]
                row_delta = delta[head : head + 1, :]
                for j in range(i + 1):
                    keys = nat[block(j), k_lanes]
                    tile, seen = masked_scores(keys, query, i, j, slope, offsets[...], length)
                    probs = jnp.exp(tile - row_lse)
                    if seen is not None:
                        probs = jnp.where(seen, probs, 0.0)
                    grad_probs = nt(nat[block(j), v_lanes], grad_head)
                    grad_scores = (probs * (grad_probs - row_delta)).astype(BF)
                    grad_v[block(j), lanes] += nn(probs.astype(BF), grad_head)
                    grad_k[block(j), lanes] += nn(grad_scores, query)
                    sum_q = sum_q + tn(halves(keys, head), grad_scores)
            grad_q[block(i), lanes] = (jnp.transpose(sum_q) * HEAD_DIM**-0.5).astype(BF)
    sums[...] = jnp.zeros_like(sums)
    for j in range(4):
        place = pl.ds(pl.multiple_of((run ^ j) * BLOCK, BLOCK), BLOCK)
        out[block(j), :mine] = grad_q[place, :]
        out[block(j), mine : 2 * mine] = grad_k[place, :].astype(BF)
        out[block(j), 2 * mine :] = grad_v[place, :].astype(BF)
        rows = out[block(j), :]
        sums[0:1, :] += jnp.sum(rows.astype(F32), axis=0, keepdims=True)
        partial = nt(rows, w_qkv[...])
        if j == 0:
            near_keep[...] = partial
        elif j == 1:
            near_send[...] = partial.astype(BF)
        elif j == 2:
            far_keep[...] = partial
        else:
            far_send[...] = partial.astype(BF)


def attend(blocks, w_qkv, bias, scalars, slopes):
    rows, width = blocks[0].shape
    columns = w_qkv.width
    mine = columns // 3
    outs = [
        ((4 * rows, columns), BF),
        ((4 * rows, mine), F32),
        ((rows, mine), BF),
        ((rows, mine), BF),
        ((rows, mine), BF),
        ((rows, mine), BF),
        ((8, 4 * rows), F32),
    ]
    scratch = [
        pltpu.VMEM((4, rows, mine), BF),
        pltpu.VMEM((4 * rows, BLOCK), F32),
        pltpu.VMEM((BLOCK, BLOCK), F32),
    ]
    inputs = (scalars, slopes, *blocks, w_qkv, bias)
    specs = [SMEM, SMEM] + [VMEM] * 6
    return kernel_call(attend_kernel, "attend", inputs, outs, scratch, specs, stored=(0, 1))


def attend_back(nat, parts, att, lse, w_qkv, scalars, slopes):
    total, columns = nat.shape
    rows, mine = total // 4, columns // 3
    width = w_qkv.rows * lax.axis_size("fsdp")
    outs = [
        ((total, columns), BF),
        ((rows, width), F32),
        ((rows, width), BF),
        ((rows, width), F32),
        ((rows, width), BF),
        ((8, columns), F32),
    ]
    scratch = [
        pltpu.VMEM((total, mine), BF),
        pltpu.VMEM((total, mine), BF),
        pltpu.VMEM((total, mine), F32),
        pltpu.VMEM((total, mine), F32),
        pltpu.VMEM((BLOCK, BLOCK), F32),
    ]
    inputs = (scalars, slopes, nat, *parts, att, lse, w_qkv)
    specs = [SMEM, SMEM] + [VMEM] * 8
    return kernel_call(attend_back_kernel, "attend_back", inputs, outs, scratch, specs)


def shards(
    tokens,
    lengths,
    cotangent,
    ln1_gain,
    ln1_bias,
    qkv_weight,
    query_bias,
    value_bias,
    out_weight,
    out_bias,
    ln2_gain,
    ln2_bias,
    up_weight,
    up_bias,
    down_weight,
    down_bias,
):
    fsdp = lax.axis_size("fsdp")
    run = lax.axis_index("seq")
    rows, width = tokens.shape[1:]
    hidden = up_weight.shape[2]
    heads = HEADS // 4
    mine = width // 4
    half = width // 2
    ffn_size = hidden // 4
    part = width // fsdp
    piece = hidden // fsdp // 4
    me = lax.axis_index("fsdp")
    scalars = jnp.stack([run.astype(jnp.int32), lengths[0]])
    place = jnp.stack([run, me % 2]).astype(jnp.int32)
    slopes = lax.dynamic_slice_in_dim(head_slopes(), run * heads, heads)

    def quarter(value, axis):
        size = value.shape[axis] // 4
        return lax.dynamic_slice_in_dim(value, run * size, size, axis)

    def core_half(value, axis):
        return lax.dynamic_slice_in_dim(value, (run % 2) * half, half, axis)

    def qkv_of(layer):
        return quarter(qkv_weight[layer].reshape(part, 3, width), 2).reshape(part, 3 * mine)

    def out_of(layer):
        return core_half(out_weight[layer], 1)

    def up_of(layer):
        return quarter(up_weight[layer].reshape(part, fsdp, -1), 2).reshape(part, ffn_size)

    def down_of(layer):
        return quarter(down_weight[layer], 0)

    def seq_blocks(own):
        across = y_swap(own)
        return [own, core_swap(own), across, core_swap(across)]

    def summed(near, far):
        far = far_sum(far)
        return near[0], core_swap(near[1]), y_swap(far)

    def far_sum(far):
        return (far[0] + core_swap(far[1]).astype(F32)).astype(BF)

    vectors = (ln1_gain, ln1_bias, query_bias, value_bias, out_bias, ln2_gain, ln2_bias, down_bias)
    small = jnp.concatenate([jnp.stack(vectors, 1).reshape(LAYERS, -1), up_bias], axis=1)
    columns = 3 * mine
    extra = small.size // columns
    small = jnp.pad(small.reshape(extra, columns), ((0, -extra % 16), (0, 0)))
    stride = part + small.shape[0]
    own = pack(["qkv", "small"], [qkv_weight, small], 0, place, stride, columns)
    token_blocks = seq_blocks(tokens[0])
    even = [own] + [hop(own, "fsdp", 2 * k) for k in range(1, fsdp // 2 - 1)]
    even.append(hop(tied(own, even[1]), "fsdp", fsdp - 2))
    first = jnp.concatenate(even)
    first = (first, x_swap(first))
    cot_blocks = seq_blocks(cotangent[0])
    token_blocks, cot_blocks, first = meet(token_blocks, cot_blocks, first)
    arrays = dict(qkv=qkv_weight, out=out_weight, up=up_weight, down=down_weight)
    sizes = dict(qkv=columns, out=half, up=ffn_size, down=width)

    def bundle(layer, names):
        if part % 128:
            parts = dict(qkv=qkv_of, out=out_of, up=up_of, down=down_of)
            return jnp.concatenate([parts[name](layer) for name in names], axis=1)
        total = sum(sizes[name] for name in names)
        return pack(names, [arrays[name] for name in names], layer, place, part, total)

    packs = [
        bundle(0, ["out", "up"]),
        bundle(0, ["down"]),
        bundle(1, ["qkv", "out"]),
        bundle(1, ["up"]),
        bundle(1, ["down"]),
    ]
    keys = jnp.stack([me, me % 2]).astype(jnp.int32)
    early_one, late_one, early_two, up_two, down_two = (gather_z(item) for item in packs)

    def matrix(halves, column, size, key=1):
        return Slots(halves, column, size, part, keys, key)

    def out_matrices(halves, column):
        own = assemble(halves, column, half, part, me % 2)
        return own, core_swap(own)

    small = [item.reshape(fsdp // 2, stride, columns)[:, part : part + extra] for item in first]
    small = jnp.stack(small, 1).reshape(fsdp, LAYERS, -1)
    small = jnp.take(small, me ^ jnp.arange(fsdp), axis=0).astype(F32)
    tables, biases = [], []
    for layer in range(LAYERS):
        table = small[:, layer, : 8 * part].reshape(fsdp, 8, part)
        table = jnp.transpose(table, (1, 0, 2)).reshape(8, width)
        bias_q, bias_v = quarter(table[BIAS_Q], 0), quarter(table[BIAS_V], 0)
        bias_qkv = jnp.concatenate([bias_q, jnp.zeros_like(bias_q), bias_v])
        bias_up = quarter(small[:, layer, 8 * part :], 1)
        tables.append(table)
        biases.append((bias_qkv.reshape(1, -1), bias_up.reshape(1, -1)))

    stream = tokens[0].astype(F32)
    token_blocks, tables, biases = meet(token_blocks, tables, biases)
    h1 = first_norm(token_blocks, tables[0])
    w_qkv = matrix(first, 0, columns, 0)
    out_one, up_one = early_one[:, :half], early_one[:, half:]
    moved_out, moved = x_swap(out_one), x_swap(up_one)
    saved, weights = [], []
    for layer in range(LAYERS):
        top = layer + 1 == LAYERS
        bias_qkv, bias_up = biases[layer]
        packed, attended, *low, lse = attend(h1, w_qkv, bias_qkv, scalars, slopes)
        if top:
            w_outs = out_matrices(early_two, columns)
        else:
            low, moved_out = meet(low, moved_out)
            w_outs = out_matrices((out_one, moved_out), 0)
        far = y_swap(low[3])
        across = y_swap(low[2])
        if not top:
            across, far, moved, late_one = meet(across, far, moved, late_one)
            moved_late = x_swap(late_one)
        parts = [low[0], core_swap(low[1]), across, core_swap(far)]
        middle, normed, att_own = out_step(scalars, parts, w_outs, stream, tables[layer])
        h2 = seq_blocks(normed)
        if top:
            middle, moved_late = meet(middle, moved_late)
            w_up = matrix((up_two, moved_up), 0, ffn_size)
            w_down = matrix((down_two, moved_late), 0, width)
            near = ffn(h2[0], h2[1], w_up, bias_up, w_down)
            near_back = ffn_back(cot_blocks[0], cot_blocks[1], near[1], w_up, w_down)
            h2[2], near, near_back = meet(h2[2], near, near_back)
            h2[3] = core_swap(h2[2])
        else:
            h2[2], moved_late, early_two = meet(h2[2], moved_late, early_two)
            h2[3] = core_swap(h2[2])
            w_up = matrix((up_one, moved), 0, ffn_size)
            w_down = matrix((late_one, moved_late), 0, width)
            moved = x_swap(early_two)
            near = ffn(h2[0], h2[1], w_up, bias_up, w_down)
        far = ffn(h2[2], h2[3], w_up, bias_up, w_down)
        saved.append((stream, h1, packed, attended, lse, att_own, middle, h2, near[:2], far[:2]))
        weights.append((w_qkv, w_outs, w_up, w_down))
        if top:
            last_sums = near[2:], far[2:]
        else:
            sums, moved, up_two = meet(summed(near[2:], far[2:]), moved, up_two)
            early_two = (early_two, moved)
            w_qkv = matrix(early_two, 0, columns)
            moved_up = x_swap(up_two)
            stream, normed = layer_end(middle, sums, tables[layer], tables[layer + 1])
            h1 = seq_blocks(normed)
            h1[2], moved_up, down_two = meet(h1[2], moved_up, down_two)
            h1[3] = core_swap(h1[2])
            moved_late = x_swap(down_two)

    grad = cotangent[0].astype(F32)
    g_down = cot_blocks
    vectors = [None] * LAYERS
    upper, lower = [], []
    for layer in reversed(range(LAYERS)):
        top = layer + 1 == LAYERS
        totals = upper if top else lower
        w_qkv, w_outs, w_up, w_down = weights[layer]
        stream, h1, packed, attended, lse, att_own, middle, h2, act_near, act_far = saved[layer]
        if top:
            near = near_back
        else:
            near = ffn_back(g_down[0], g_down[1], act_near[1], w_up, w_down)
            g_down[2], near, late, moved_above = meet(g_down[2], near, late, moved_above)
            g_down[3] = core_swap(g_down[2])
            moved_late = x_swap(late[1])
        far = ffn_back(g_down[2], g_down[3], act_far[1], w_up, w_down)
        far_low = far_sum(far[1:3])
        acts, h2, far_low = meet([act_near[0], act_far[0]], h2, far_low)
        if not top:
            far_low, up_above = meet(far_low, up_above)
            reduced = added(up_above, moved_above)
            upper.append(scatter_z(reduced))
        sums = near[1], core_swap(near[2]), y_swap(far_low)
        if top:
            size = width * 3 // 4
            sent_down = weight_grad(acts, g_down, place, (size, width - size))
            size = ffn_size * 3 // 8
            sent_up = weight_grad(h2, [near[0], far[0]], place, (size, ffn_size - size))
            pair = zip(sent_down[2:], sent_up[:2])
            sent_both = [jnp.concatenate(item, axis=1) for item in pair]
            sent_down, sent_up = sent_down[:2], sent_up[2:]
            moved_both = x_swap(sent_both[1])
            sums, sent_both[0] = meet(sums, sent_both[0])
        else:
            sent_down = weight_grad(acts, g_down, place)
            sent_up = weight_grad(h2, [near[0], far[0]], place)
        moved_down, moved_up = x_swap(sent_down[1]), x_swap(sent_up[1])
        sums, sent_down[0], sent_up[0] = meet(sums, sent_down[0], sent_up[0])
        grad_middle, g_branch, *g_att, lines_two = out_back(
            scalars, sums, middle, grad, tables[layer], w_outs
        )
        g_att = [
            g_att[0],
            core_swap(g_att[1]),
            y_swap(g_att[2]),
            y_swap(core_swap(g_att[3])),
        ]
        if not top:
            g_att, moved_late = meet(g_att, moved_late)
            reduced = added(late[0], moved_late)
            g_att, reduced, upper[:2] = meet(g_att, reduced, upper[:2])
            upper.append(scatter_z(reduced))
        if top:
            g_att, last_sums = meet(g_att, last_sums)
        keep, send = out_grad(att_own, g_branch, place)
        send = core_swap(send)
        g_packed, *parts, packed_sum = attend_back(
            packed, g_att, attended, lse, w_qkv, scalars, slopes
        )
        if top:
            last_sums = summed(*last_sums)
            parts, moved_down, last_sums, send = meet(parts, moved_down, last_sums, send)
            result = layer_end(saved[layer][6], last_sums, tables[layer], None)[1]
        else:
            parts, moved_down, send = meet(parts, moved_down, send)
        far_low = far_sum(parts[2:])
        h1, sent_down[0], far_low = meet(h1, sent_down[0], far_low)
        sent_qkv = weight_grad(h1, [g_packed], place)
        sums = parts[0], core_swap(parts[1]), y_swap(far_low)
        reduced = added(sent_down[0], moved_down)
        totals.append(scatter_z(reduced))
        sums, reduced, sent_qkv[0] = meet(sums, reduced, sent_qkv[0])
        if top:
            sums, moved_both = meet(sums, moved_both)
        else:
            sums, moved_up = meet(sums, moved_up)
            reduced = added(sent_up[0], moved_up)
            totals.append(scatter_z(reduced))
            sent_out = added_pair(keep, send)
            late = [jnp.concatenate(pair, axis=1) for pair in zip(sent_qkv, sent_out)]
            sums, upper[2:], late[0] = meet(sums, upper[2:], late[0])
            one, two, three, last_piece = upper
            size = width // 4
            upper = [
                jnp.concatenate([one, two[:, :size]], axis=1),
                jnp.concatenate([two[:, size:], three], axis=1),
                last_piece,
            ]
        up_sum = near[3] + far[3]
        grad, normed, lines_one = layer_begin(sums, stream, grad_middle, tables[layer])
        if layer:
            normed, sent_both[0], sent_up[0], keep = meet(
                normed, sent_both[0], sent_up[0], keep
            )
            upper.append(scatter_z(added(sent_both[0], moved_both)))
            g_down = seq_blocks(normed)
            up_above, moved_above = sent_up[0], moved_up
        else:
            grad, totals[0] = meet(grad, totals[0])
        if layer:
            sent_out = added_pair(keep, send)
            late = [jnp.concatenate(pair, axis=1) for pair in zip(sent_qkv, sent_out)]
        else:
            upper = [four(item) for item in upper]
            totals[0] = four(totals[0])
            last, upper, totals = meet(added(late[0], x_swap(late[1])), upper, totals)
            lower = totals + [scatter_z(last)]

        vectors[layer] = (lines_two, lines_two, packed_sum, lines_one, up_sum)

    def spread(value, axis=0):
        shape = list(value.shape)
        size = shape[axis]
        shape[axis] = 4 * size
        return lax.dynamic_update_slice_in_dim(jnp.zeros(shape, F32), value, run * size, axis)

    small_sums = []
    vectors, grad = meet(vectors, grad)
    for _, lines_two, packed_sum, lines_one, up_sum in vectors:
        members = [
            lines_one[0],
            lines_one[1],
            spread(packed_sum[0, :mine]),
            spread(packed_sum[0, 2 * mine :]),
            lines_two[2],
            lines_two[0],
            lines_two[1],
            lines_two[3],
        ]
        small_sums.append(
            jnp.concatenate(
                [item.reshape(fsdp, part) for item in members]
                + [spread(up_sum.reshape(fsdp, piece), 1)],
                axis=1,
            )
        )

    starts = ((2, 0), (2, columns), (1, 0), (0, 0))
    names = ("qkv", "out", "up", "down")
    matrices = finish(1, LAYERS, upper, starts, place, None, names)
    vector = sum_small(jnp.stack(small_sums, axis=1))
    middle, vector, result = meet(four(lower[1]), vector, result)
    groups = [lower[0], middle]
    ffn_grads = finish(0, LAYERS, groups, starts, place, list(matrices[2:]), names[2:])
    last, ffn_grads, matrices, vector = meet(lower[2], ffn_grads, matrices[:2], vector)
    starts = ((0, 0), (0, columns), (0, 0), (0, 0))
    matrices = finish(0, LAYERS, [four(last)], starts, place, list(matrices), names[:2])
    grad_qkv_w, grad_out_w = matrices
    grad_up_w, grad_down_w = ffn_grads
    if piece % 128:
        grad_up_w = grad_up_w.reshape(LAYERS, part, 4, fsdp, piece)
        grad_up_w = jnp.swapaxes(grad_up_w, 2, 3).reshape(LAYERS, part, hidden)
    lines = [vector[:, i * part : (i + 1) * part] for i in range(8)]
    gain_one, shift_one, bias_q, bias_v, bias_o, gain_two, shift_two, bias_down = lines
    return (
        result[None],
        grad[None],
        gain_one,
        shift_one,
        grad_qkv_w,
        bias_q,
        bias_v,
        grad_out_w,
        bias_o,
        gain_two,
        shift_two,
        grad_up_w,
        vector[:, 8 * part :],
        grad_down_w,
        bias_down,
    )


def solution(mesh):
    vector = P(None, "fsdp")
    matrix = P(None, "fsdp", None)
    data = P("fsdp", "seq", None)
    weight_specs = (
        vector,
        vector,
        matrix,
        vector,
        vector,
        matrix,
        vector,
        vector,
        vector,
        matrix,
        vector,
        matrix,
        vector,
    )
    in_specs = (data, P("fsdp"), data) + weight_specs
    out_specs = (data, data) + weight_specs
    return jax.shard_map(shards, mesh=mesh, in_specs=in_specs, out_specs=out_specs, check_vma=False)
```

```python
import functools

import jax
import jax.numpy as jnp
from jax import lax
from jax.experimental import pallas as pl
from jax.experimental.pallas import tpu as pltpu
from jax.sharding import PartitionSpec as P

HEADS = 16
HEAD_DIM = 64
LAYERS = 2
BLOCK = 256
EPS = 1e-05
NEG = -1e30
BF = jnp.bfloat16
F32 = jnp.float32
GELU = 0.7978845608028654
CUBIC = 0.044715
GRANT = [24]
VMEM = pl.BlockSpec(memory_space=pltpu.VMEM)
SMEM = pl.BlockSpec(memory_space=pltpu.SMEM)


def head_slopes():
    return jnp.exp2(-8.0 * (jnp.arange(HEADS, dtype=F32) + 1.0) / HEADS)


def hop(value, axis, mask):
    size = lax.axis_size(axis)
    return lax.ppermute(value, axis, [(i, i ^ mask) for i in range(size)])


def core_swap(value):
    return hop(value, "seq", 1)


def y_swap(value):
    return hop(value, "seq", 2)


def sum_small(full):
    size = lax.axis_size("fsdp")
    me = lax.axis_index("fsdp")
    full = full + y_swap(full)
    full = full + core_swap(full)
    slots = jnp.take(full, me ^ jnp.arange(size), axis=0)
    slots = slots.reshape((size // 2, 2) + full.shape[1:])
    slots = slots[:, 0] + hop(slots[:, 1], "fsdp", 1)
    total = slots[0]
    for k in range(1, size // 2):
        total = total + hop(slots[k], "fsdp", 2 * k)
    return total


def assemble_kernel(column, stride, key_ref, same, other, out, held, sems):
    key = key_ref[0]
    pairs, rows, width = held.shape[0] // 2, held.shape[1], held.shape[2]
    loads, stores = [], []
    for r in range(2 * pairs):
        place = pl.ds(r // 2 * stride, rows)
        source = (other if r % 2 else same).at[place, pl.ds(column, width)]
        loads.append(pltpu.make_async_copy(source, held.at[r], sems.at[r, 0]))
        start = pl.multiple_of((r ^ key) * rows, rows)
        target = out.at[pl.ds(start, rows), :]
        stores.append(pltpu.make_async_copy(held.at[r], target, sems.at[r, 1]))
    for load in loads:
        load.start()
    for load, store in zip(loads, stores):
        load.wait()
        store.start()
    for store in stores:
        store.wait()


def assemble(halves, column, width, rows, key):
    slots = lax.axis_size("fsdp")
    stride = 2 * halves[0].shape[0] // slots
    key = key.astype(jnp.int32).reshape(1)
    hbm = pl.BlockSpec(memory_space=pl.ANY)
    return pl.pallas_call(
        functools.partial(assemble_kernel, column, stride),
        grid_spec=pltpu.PrefetchScalarGridSpec(
            num_scalar_prefetch=1,
            grid=(),
            in_specs=[hbm] * 2,
            out_specs=hbm,
            scratch_shapes=[
                pltpu.VMEM((slots, rows, width), BF),
                pltpu.SemaphoreType.DMA((slots, 2)),
            ],
        ),
        out_shape=jax.ShapeDtypeStruct((slots * rows, width), BF),
        compiler_params=pltpu.CompilerParams(vmem_limit_bytes=12 << 20),
        cost_estimate=pl.CostEstimate(flops=0, bytes_accessed=0, transcendentals=0),
        name="assemble",
    )(key, *halves)


def tied(value, after):
    return lax.optimization_barrier((value, after))[0]


def meet(*values):
    return lax.optimization_barrier(values)


def pack_kernel(names, layer, place, *refs):
    sources, (out, sems) = dict(zip(names, refs)), refs[len(names) :]
    run = place[0]
    copies = []
    column = 0

    def add(source, size, rows=None):
        rows = source.shape[0] if rows is None else rows
        target = out.at[pl.ds(0, rows), pl.ds(column, size)]
        copies.append(pltpu.make_async_copy(source, target, sems.at[len(copies)]))
        return column + size

    for name in names:
        source = sources[name]
        if name == "small":
            rows = source.shape[0]
            target = out.at[pl.ds(out.shape[0] - rows, rows), :]
            copies.append(pltpu.make_async_copy(source, target, sems.at[len(copies)]))
            continue
        source = source.at[layer]
        part, width = source.shape
        if name == "qkv":
            for third in range(3):
                start = pl.multiple_of((4 * third + run) * (width // 12), width // 12)
                column = add(source.at[:, pl.ds(start, width // 12)], width // 12)
        elif name == "out":
            start = pl.multiple_of(run % 2 * (width // 2), width // 2)
            column = add(source.at[:, pl.ds(start, width // 2)], width // 2)
        elif name == "up":
            piece = part
            for slot in range(width // (4 * piece)):
                start = pl.multiple_of((4 * slot + run) * piece, piece)
                column = add(source.at[:, pl.ds(start, piece)], piece)
        else:
            start = pl.multiple_of(run * (part // 4), part // 4)
            column = add(source.at[pl.ds(start, part // 4), :], width)
    for copy in copies:
        copy.start()
    for copy in copies:
        copy.wait()


def pack(names, arrays, layer, place, rows, columns):
    count = sum({"qkv": 3, "up": arrays[0].shape[-1]}.get(name, 1) for name in names)
    hbm = pl.BlockSpec(memory_space=pl.ANY)
    return pl.pallas_call(
        functools.partial(pack_kernel, names, layer),
        in_specs=[SMEM] + [hbm] * len(arrays),
        out_specs=VMEM,
        out_shape=jax.ShapeDtypeStruct((rows, columns), BF),
        scratch_shapes=[pltpu.SemaphoreType.DMA((min(count, 64),))],
        compiler_params=pltpu.CompilerParams(vmem_limit_bytes=12 << 20),
        cost_estimate=pl.CostEstimate(flops=0, bytes_accessed=0, transcendentals=0),
        name="pack",
    )(place, *arrays)


def z_groups():
    size = lax.axis_size("fsdp")
    return [[x + 2 * k for k in range(size // 2)] for x in range(2)]


def gather_z(own):
    return lax.all_gather(own, "fsdp", axis=0, tiled=True, axis_index_groups=z_groups())


def x_swap(value):
    return hop(value, "fsdp", 1)


def scatter_z(same):
    return lax.psum_scatter(
        same, "fsdp", scatter_dimension=0, tiled=True, axis_index_groups=z_groups()
    )


def four(total):
    across = y_swap(total)
    return total, core_swap(total), across, core_swap(across)


class Slots:
    def __init__(self, halves, column, width, rows, keys, key):
        self.halves, self.column, self.width, self.rows = halves, column, width, rows
        self.keys, self.key = keys, key

    def copies(self, keys, same, other, buffer):
        count = buffer.shape[0] // self.rows
        stride = 2 * same.shape[0] // count
        for r in range(count):
            source = other if r % 2 else same
            source = source.at[pl.ds(r // 2 * stride, self.rows), pl.ds(self.column, self.width)]
            start = pl.multiple_of((r ^ keys[self.key]) * self.rows, self.rows)
            yield source, buffer.at[pl.ds(start, self.rows), :]


def staged(body, plan, stored, refs):
    refs = list(refs)
    keys = refs.pop(0) if any(isinstance(item, Slots) for item in plan) else None
    taken = [refs.pop(0) for item in plan for _ in range(1 + isinstance(item, Slots))]
    sems = refs.pop()
    results = [refs.pop() for _ in stored][::-1]
    places = [i for i, item in enumerate(plan) if item is not None]
    buffers = refs[len(refs) - len(places) :]
    refs = refs[: len(refs) - len(places)]
    inputs, copies = [], []
    for item in plan:
        if item is None:
            inputs.append(taken.pop(0))
            continue
        buffer = buffers.pop(0)
        inputs.append(buffer)
        if item is VMEM:
            moves = [(taken.pop(0), buffer)]
        else:
            moves = item.copies(keys, taken.pop(0), taken.pop(0), buffer)
        for source, target in moves:
            copies.append(pltpu.make_async_copy(source, target, sems.at[len(copies)]))
    for copy in copies:
        copy.start()
    for copy in copies:
        copy.wait()
    first = len(copies)
    stores = {}
    for number, (i, result) in enumerate(zip(stored, results)):
        stores[i] = pltpu.make_async_copy(result, refs[i], sems.at[first + number])
        refs[i] = result
    waiting = list(stored)
    steps = body(*inputs, *refs)
    for i in steps if stored and steps is not None else ():
        stores[i].start()
        waiting.remove(i)
    for i in waiting:
        stores[i].start()
    for store in stores.values():
        store.wait()


def kernel_call(body, name, inputs, outputs, scratch=(), in_specs=None, cost=0, stored=()):
    plan, arrays, specs, buffers, keys = [], [], [], [], None
    count = 1
    hbm = pl.BlockSpec(memory_space=pl.ANY)
    for item, spec in zip(inputs, in_specs or [VMEM] * len(inputs)):
        if isinstance(item, Slots):
            shape = (lax.axis_size("fsdp") * item.rows, item.width)
            plan.append(item)
            arrays += item.halves
            specs += [hbm, hbm]
            buffers.append(pltpu.VMEM(shape, BF))
            keys = item.keys
            count += lax.axis_size("fsdp")
            continue
        arrays.append(item)
        plan.append(VMEM if spec is VMEM else None)
        specs.append(hbm if spec is VMEM else SMEM)
        if spec is VMEM:
            buffers.append(pltpu.VMEM(item.shape, item.dtype))
            count += 1
    if keys is not None:
        arrays, specs = [keys] + arrays, [SMEM] + specs
    buffers += [pltpu.VMEM(*outputs[i]) for i in stored]
    there = pl.BlockSpec(memory_space=pltpu.HBM)
    return pl.pallas_call(
        lambda *refs: staged(body, plan, stored, refs),
        in_specs=specs,
        out_specs=[there if i in stored else VMEM for i in range(len(outputs))],
        out_shape=[jax.ShapeDtypeStruct(shape, kind) for shape, kind in outputs],
        scratch_shapes=[*scratch, *buffers, pltpu.SemaphoreType.DMA((count + len(stored),))],
        compiler_params=pltpu.CompilerParams(vmem_limit_bytes=GRANT[0] << 20),
        cost_estimate=pl.CostEstimate(flops=0, bytes_accessed=cost, transcendentals=0),
        name=name,
    )(*arrays)


def pair_kernel(keep, received, same, other):
    for i, target in enumerate((same, other)):
        target[...] = (keep[i].astype(F32) + received[i].astype(F32)).astype(BF)


def added_pair(keep, received):
    outs = [(keep.shape[1:], BF)] * 2
    return kernel_call(pair_kernel, "added_pair", (keep, received), outs)


def add_kernel(same, *refs):
    out = refs[-1]
    start = 0
    for item in refs[:-1]:
        rows = slice(start, start + item.shape[0])
        out[rows, :] = (same[rows, :].astype(F32) + item[...].astype(F32)).astype(BF)
        start += item.shape[0]


def added(same, *received):
    return kernel_call(add_kernel, "added", (same, *received), [(same.shape, BF)])[0]


def nn(left, right):
    return jnp.dot(left, right, preferred_element_type=F32)


def nt(left, right):
    return lax.dot_general(left, right, (((1,), (1,)), ((), ())), preferred_element_type=F32)


def tn(left, right):
    return lax.dot_general(left, right, (((0,), (0,)), ((), ())), preferred_element_type=F32)


def normalized(value):
    center = value - jnp.mean(value, axis=-1, keepdims=True)
    scale = lax.rsqrt(jnp.mean(center * center, axis=-1, keepdims=True) + EPS)
    return center * scale, scale


def norm_back(value, gain, grad):
    hat, scale = normalized(value)
    inner = grad * gain
    mean = jnp.mean(inner, axis=-1, keepdims=True)
    along = jnp.mean(inner * hat, axis=-1, keepdims=True)
    grad_gain = jnp.sum(grad * hat, axis=0, keepdims=True)
    return scale * (inner - mean - hat * along), grad_gain, jnp.sum(grad, axis=0, keepdims=True)


GAIN_ONE, SHIFT_ONE, BIAS_Q, BIAS_V, BIAS_OUT, GAIN_TWO, SHIFT_TWO, BIAS_DOWN = range(8)


def row(table, index):
    return table[index : index + 1, :]


def first_norm_kernel(a, b, c, d, table, *outs):
    for value, out in zip((a, b, c, d), outs):
        hat, _ = normalized(value[...].astype(F32))
        out[...] = (hat * row(table, GAIN_ONE) + row(table, SHIFT_ONE)).astype(BF)


def first_norm(blocks, table):
    outs = [(item.shape, BF) for item in blocks]
    return kernel_call(first_norm_kernel, "first_norm", (*blocks, table), outs)


def layer_end_kernel(middle, keep, beside, across, table, after, stream, normed):
    total = keep[...] + beside[...].astype(F32) + across[...].astype(F32)
    value = middle[...] + (total + row(table, BIAS_DOWN))
    stream[...] = value
    if after is None:
        normed[...] = value.astype(BF)
    else:
        hat, _ = normalized(value)
        normed[...] = (hat * row(after, GAIN_ONE) + row(after, SHIFT_ONE)).astype(BF)


def last_end_kernel(middle, keep, beside, across, table, stream, low):
    layer_end_kernel(middle, keep, beside, across, table, None, stream, low)


def layer_end(middle, sums, table, after):
    outs = [(middle.shape, F32), (middle.shape, BF)]
    if after is None:
        return kernel_call(last_end_kernel, "last_end", (middle, *sums, table), outs)
    inputs = (middle, *sums, table, after)
    return kernel_call(layer_end_kernel, "layer_end", inputs, outs, stored=(0,))


def out_kernel(
    scalars, own, beside, across, far, w_own, w_other, stream, table, middle, normed, attended
):
    run = scalars[0]
    core = run % 2
    parts = [own[...], beside[...], across[...], far[...]]
    size = parts[0].shape[1]
    starts = [pl.multiple_of((run ^ j) * size, size) for j in range(4)]
    for part, start in zip(parts, starts):
        attended[:, pl.ds(start, size)] = part
    yield 2
    half = w_own.shape[1]
    for weight, place in ((w_own, core), (w_other, 1 - core)):
        total = None
        for part, start in zip(parts, starts):
            term = nn(part, weight[pl.ds(start, size), :])
            total = term if total is None else total + term
        lanes = pl.ds(pl.multiple_of(place * half, half), half)
        bias = table[BIAS_OUT : BIAS_OUT + 1, lanes]
        middle[:, lanes] = stream[:, lanes] + (total + bias)
    yield 0
    hat, _ = normalized(middle[...])
    normed[...] = (hat * row(table, GAIN_TWO) + row(table, SHIFT_TWO)).astype(BF)


def out_step(scalars, parts, w_outs, stream, table):
    outs = [(stream.shape, F32), (stream.shape, BF), (stream.shape, BF)]
    inputs = (scalars, *parts, *w_outs, stream, table)
    specs = [SMEM] + [VMEM] * 8
    return kernel_call(out_kernel, "out_step", inputs, outs, in_specs=specs, stored=(0, 2))


def ffn_kernel(a, b, w_up, bias, w_down, act, slope, keep, send, source):
    rows = a.shape[0]
    source[:rows, :] = a[...]
    source[rows:, :] = b[...]
    pre = nn(source[...], w_up[...]) + bias[...]
    square = pre * pre
    bent = jnp.tanh(GELU * pre * (1.0 + CUBIC * square))
    half = 0.5 + 0.5 * bent
    value = (pre * half).astype(BF)
    act[...] = value
    yield 0
    rise = half + (0.5 * GELU) * pre * (1.0 - bent * bent) * (1.0 + 3.0 * CUBIC * square)
    slope[...] = rise.astype(BF)
    yield 1
    total = nn(value, w_down[...])
    keep[...] = total[:rows, :]
    send[...] = total[rows:, :].astype(BF)


def ffn(a, b, w_up, bias, w_down):
    rows, width = a.shape
    hidden = w_up.width
    outs = [
        ((2 * rows, hidden), BF),
        ((2 * rows, hidden), BF),
        ((rows, width), F32),
        ((rows, width), BF),
    ]
    scratch = [pltpu.VMEM((2 * rows, width), BF)]
    inputs = (a, b, w_up, bias, w_down)
    return kernel_call(ffn_kernel, "ffn", inputs, outs, scratch, stored=(0, 1))


def ffn_back_kernel(a, b, slope, w_up, w_down, grad_pre, keep, send, sums, source):
    rows = a.shape[0]
    source[:rows, :] = a[...]
    source[rows:, :] = b[...]
    grad_act = nt(source[...], w_down[...])
    value = (grad_act * slope[...].astype(F32)).astype(BF)
    grad_pre[...] = value
    sums[...] = jnp.sum(value.astype(F32), axis=0, keepdims=True)
    total = nt(value, w_up[...])
    keep[...] = total[:rows, :]
    send[...] = total[rows:, :].astype(BF)


def ffn_back(a, b, slope, w_up, w_down):
    rows, width = a.shape
    hidden = w_up.width
    outs = [
        ((2 * rows, hidden), BF),
        ((rows, width), F32),
        ((rows, width), BF),
        ((1, hidden), F32),
    ]
    scratch = [pltpu.VMEM((2 * rows, width), BF)]
    return kernel_call(ffn_back_kernel, "ffn_back", (a, b, slope, w_up, w_down), outs, scratch)


def weight_grad_kernel(count, parts, scalars, *refs):
    x = scalars[1]
    lefts, rights = refs[: parts[0]], refs[parts[0] : parts[0] + parts[1]]
    *outs, left, right, total = refs[parts[0] + parts[1] :]
    for sources, target in ((lefts, left), (rights, right)):
        start = 0
        for source in sources:
            target[start : start + source.shape[0], :] = source[...]
            start += source.shape[0]
    total[...] = tn(left[...], right[...]).astype(BF)
    rows = total.shape[0] // count
    first = 0
    for same, other in zip(outs[::2], outs[1::2]):
        columns = slice(first, first + same.shape[1])
        first += same.shape[1]
        for r in range(count):
            start = pl.multiple_of((r ^ x) * rows, rows)
            target = other if r % 2 else same
            target[r // 2 * rows : (r // 2 + 1) * rows, :] = total[pl.ds(start, rows), columns]


def weight_grad(lefts, rights, place, cuts=()):
    count = lax.axis_size("fsdp")
    total = sum(item.shape[0] for item in lefts)
    tall, wide = lefts[0].shape[1], rights[0].shape[1]
    outs = [((tall // 2, size), BF) for size in cuts or (wide,) for _ in range(2)]
    scratch = [
        pltpu.VMEM((total, tall), BF),
        pltpu.VMEM((total, wide), BF),
        pltpu.VMEM((tall, wide), BF),
    ]
    inputs = (place, *lefts, *rights)
    body = functools.partial(weight_grad_kernel, count, (len(lefts), len(rights)))
    specs = [SMEM] + [VMEM] * (len(inputs) - 1)
    return list(kernel_call(body, "weight_grad", inputs, outs, scratch, specs))


def out_grad_kernel(count, place, left, right, keep, send, total):
    core, x = place[0] % 2, place[1]
    half = keep.shape[2]
    rows = total.shape[0] // count
    for target, number in ((keep, core), (send, 1 - core)):
        lanes = pl.ds(pl.multiple_of(number * half, half), half)
        total[...] = tn(left[...], right[:, lanes]).astype(BF)
        for r in range(count):
            start = pl.multiple_of((r ^ x) * rows, rows)
            target[r % 2, r // 2 * rows : (r // 2 + 1) * rows, :] = total[pl.ds(start, rows), :]


def out_grad(left, right, place):
    count = lax.axis_size("fsdp")
    tall, wide = left.shape[1], right.shape[1]
    outs = [((2, tall // 2, wide // 2), BF)] * 2
    scratch = [pltpu.VMEM((tall, wide // 2), BF)]
    body = functools.partial(out_grad_kernel, count)
    return kernel_call(
        body, "out_grad", (place, left, right), outs, scratch, [SMEM, VMEM, VMEM]
    )


def finish_kernel(layout, slots, aliased, place, *refs):
    run = place[0]
    groups = []
    for number in range(layout[-1]):
        groups.append(refs[4 * number : 4 * number + 4])
    refs = refs[4 * layout[-1] + aliased :]
    names = layout[1]
    outs = dict(zip(names, refs))
    part = groups[0][0].shape[0]
    width = part * slots
    mine, half, size = width // 4, width // 2, width
    piece = size // slots
    (q_group, q_start), (o_group, o_start), (u_group, u_start), (d_group, d_start) = layout[0]
    qkv, out, up, down = (outs.get(name) for name in ("qkv", "out", "up", "down"))
    for j in range(4):
        owner = run ^ j
        for third in range(3 if qkv is not None else 0):
            lanes = pl.ds(pl.multiple_of(third * width + owner * mine, mine), mine)
            start = q_start + third * mine
            qkv[0, :, lanes] = groups[q_group][j][:, start : start + mine].astype(F32)
        if up is None:
            continue
        if piece % 128:
            lanes = pl.ds(pl.multiple_of(owner * size, size), size)
            up[0, :, lanes] = groups[u_group][j][:, u_start : u_start + size].astype(F32)
        else:
            for slot in range(slots):
                lanes = pl.ds(pl.multiple_of((4 * slot + owner) * piece, piece), piece)
                start = u_start + slot * piece
                up[0, :, lanes] = groups[u_group][j][:, start : start + piece].astype(F32)
        rows = pl.ds(pl.multiple_of(owner * part, part), part)
        down[0, rows, :] = groups[d_group][j][:, d_start : d_start + width].astype(F32)
    for j in range(2 if out is not None else 0):
        lanes = pl.ds(pl.multiple_of((run ^ j) % 2 * half, half), half)
        columns = slice(o_start, o_start + half)
        first, second = groups[o_group][j][:, columns], groups[o_group][j + 2][:, columns]
        out[0, :, lanes] = first.astype(F32) + second.astype(F32)


def finish(layer, layers, groups, starts, place, before, names):
    slots = lax.axis_size("fsdp")
    part = groups[0][0].shape[0]
    width = part * slots
    shapes = dict(
        qkv=(part, 3 * width), out=(part, width), up=(part, 4 * width), down=(4 * part, width)
    )
    shapes = [shapes[name] for name in names]
    inputs = [place] + [item for group in groups for item in group]
    count = len(inputs)
    specs = [SMEM] + [VMEM] * (count - 1)
    aliases = {}
    if before is not None:
        inputs += before
        specs += [pl.BlockSpec(memory_space=pl.ANY)] * len(names)
        aliases = {count + i: i for i in range(len(names))}
    layout = (starts, names, len(groups))
    return pl.pallas_call(
        functools.partial(finish_kernel, layout, slots, len(aliases)),
        grid=(1,),
        in_specs=specs,
        out_specs=[pl.BlockSpec((1,) + shape, lambda i: (layer, 0, 0)) for shape in shapes],
        out_shape=[jax.ShapeDtypeStruct((layers,) + shape, F32) for shape in shapes],
        input_output_aliases=aliases,
        compiler_params=pltpu.CompilerParams(vmem_limit_bytes=48 << 20),
        cost_estimate=pl.CostEstimate(flops=0, bytes_accessed=0, transcendentals=0),
        name="finish",
    )(*inputs)


def out_back_kernel(
    scalars,
    keep,
    beside,
    across,
    middle,
    grad,
    table,
    w_own,
    w_other,
    grad_middle,
    branch,
    first,
    second,
    third,
    fourth,
    sums,
):
    run = scalars[0]
    core = run % 2
    total = keep[...] + beside[...].astype(F32) + across[...].astype(F32)
    value, grad_gain, grad_shift = norm_back(middle[...], row(table, GAIN_TWO), total)
    value = grad[...] + value
    grad_middle[...] = value
    low = value.astype(BF)
    branch[...] = low
    sums[...] = jnp.zeros_like(sums)
    sums[0:1, :] = grad_gain
    sums[1:2, :] = grad_shift
    sums[2:3, :] = jnp.sum(low.astype(F32), axis=0, keepdims=True)
    sums[3:4, :] = jnp.sum(grad[...].astype(BF).astype(F32), axis=0, keepdims=True)
    size = first.shape[1]
    half = w_own.shape[1]
    for j, target in enumerate((first, second, third, fourth)):
        rows = pl.ds(pl.multiple_of((run ^ j) * size, size), size)
        result = None
        for weight, place in ((w_own, core), (w_other, 1 - core)):
            lanes = pl.ds(pl.multiple_of(place * half, half), half)
            term = nt(branch[:, lanes], weight[rows, :])
            result = term if result is None else result + term
        target[...] = result.astype(BF)


def out_back(scalars, sums, middle, grad, table, w_outs):
    rows, width = middle.shape
    mine = width // 4
    outs = [
        ((rows, width), F32),
        ((rows, width), BF),
        ((rows, mine), BF),
        ((rows, mine), BF),
        ((rows, mine), BF),
        ((rows, mine), BF),
        ((8, width), F32),
    ]
    inputs = (scalars, *sums, middle, grad, table, *w_outs)
    return kernel_call(out_back_kernel, "out_back", inputs, outs, in_specs=[SMEM] + [VMEM] * 8)


def layer_begin_kernel(
    keep, beside, across, stream, grad_middle, table, grad, low, sums
):
    total = keep[...] + beside[...].astype(F32) + across[...].astype(F32)
    value, grad_gain, grad_shift = norm_back(stream[...], row(table, GAIN_ONE), total)
    value = grad_middle[...] + value
    grad[...] = value
    low[...] = value.astype(BF)
    sums[...] = jnp.zeros_like(sums)
    sums[0:1, :] = grad_gain
    sums[1:2, :] = grad_shift


def layer_begin(sums, stream, grad_middle, table):
    shape = stream.shape
    outs = [(shape, F32), (shape, BF), ((8, shape[1]), F32)]
    return kernel_call(
        layer_begin_kernel, "layer_begin", (*sums, stream, grad_middle, table), outs
    )


def halves(value, head):
    lane = lax.broadcasted_iota(jnp.int32, value.shape, 1)
    return jnp.where((lane >= HEAD_DIM) == (head == 1), value, jnp.zeros_like(value))


def masked_scores(keys, query, i, j, slope, offsets, length):
    scores = nt(keys, query)
    if i == j:
        scores = scores - slope * jnp.abs(offsets)
    else:
        scores = scores - (slope * offsets + slope * float((i - j) * BLOCK))
    if j == 0:
        return scores, None
    return scores, j * BLOCK + lax.broadcasted_iota(jnp.int32, scores.shape, 0) < length


def block(i):
    return slice(i * BLOCK, (i + 1) * BLOCK)


def distances(ref):
    shape = (BLOCK, BLOCK)
    offsets = lax.broadcasted_iota(jnp.int32, shape, 1) - lax.broadcasted_iota(jnp.int32, shape, 0)
    ref[...] = offsets.astype(F32)


def attend_kernel(
    scalars,
    slopes,
    a,
    b,
    c,
    d,
    w_qkv,
    bias,
    nat,
    att,
    own,
    near,
    far,
    farther,
    lse,
    low,
    scores,
    offsets,
):
    run, length = scalars[0], scalars[1]
    blocks = nat.shape[0] // BLOCK
    mine = nat.shape[1] // 3
    for j, rows in enumerate((a, b, c, d)):
        place = pl.ds(pl.multiple_of((run ^ j) * BLOCK, BLOCK), BLOCK)
        nat[place, :] = (nn(rows[...], w_qkv[...]) + bias[...]).astype(BF)
    yield 0
    distances(offsets)
    for i in range(blocks):
        for pair in range(mine // 128):
            lanes = slice(pair * 128, (pair + 1) * 128)
            out = jnp.zeros((128, BLOCK), F32)
            for head in range(2):
                slope = slopes[pair * 2 + head]
                query = halves(nat[block(i), lanes], head) * jnp.asarray(HEAD_DIM**-0.5, BF)
                top = None
                for j in range(i + 1):
                    keys = nat[block(j), mine + pair * 128 : mine + (pair + 1) * 128]
                    tile, seen = masked_scores(keys, query, i, j, slope, offsets[...], length)
                    if seen is not None:
                        tile = jnp.where(seen, tile, NEG)
                    scores[block(j), :] = tile
                    tile_top = jnp.max(tile, axis=0, keepdims=True)
                    top = tile_top if top is None else jnp.maximum(top, tile_top)
                total = jnp.zeros((1, BLOCK), F32)
                summed = jnp.zeros((128, BLOCK), F32)
                for j in range(i + 1):
                    weights = jnp.exp(scores[block(j), :] - top)
                    total = total + jnp.sum(weights, axis=0, keepdims=True)
                    values = nat[block(j), 2 * mine + pair * 128 : 2 * mine + (pair + 1) * 128]
                    summed = summed + tn(halves(values, head), weights.astype(BF))
                out = out + summed / total
                lse[pair * 2 + head : pair * 2 + head + 1, block(i)] = top + jnp.log(total)
            rows = jnp.transpose(out)
            att[block(i), lanes] = rows
            low[run ^ i, :, lanes] = rows.astype(BF)
    own[...] = low[0]
    near[...] = low[1]
    far[...] = low[2]
    farther[...] = low[3]


def attend_back_kernel(
    scalars,
    slopes,
    nat,
    own,
    beside,
    across,
    far,
    att,
    lse,
    w_qkv,
    out,
    near_keep,
    near_send,
    far_keep,
    far_send,
    sums,
    nat_grad,
    grad_q,
    grad_k,
    grad_v,
    offsets,
):
    run, length = scalars[0], scalars[1]
    blocks = nat.shape[0] // BLOCK
    mine = nat.shape[1] // 3
    for j, rows in enumerate((own[...], beside[...], across[...], far[...])):
        place = pl.ds(pl.multiple_of((run ^ j) * BLOCK, BLOCK), BLOCK)
        nat_grad[place, :] = rows
    distances(offsets)
    grad_k[...] = jnp.zeros_like(grad_k)
    grad_v[...] = jnp.zeros_like(grad_v)
    scale = jnp.asarray(HEAD_DIM**-0.5, BF)
    for pair in range(mine // 128):
        lanes = slice(pair * 128, (pair + 1) * 128)
        k_lanes = slice(mine + pair * 128, mine + (pair + 1) * 128)
        v_lanes = slice(2 * mine + pair * 128, 2 * mine + (pair + 1) * 128)
        for i in range(blocks):
            grad_rows = nat_grad[block(i), lanes]
            product = grad_rows.astype(F32) * att[block(i), lanes]
            ones = lax.broadcasted_iota(jnp.int32, (8, 128), 1) // HEAD_DIM
            ones = (ones == lax.broadcasted_iota(jnp.int32, (8, 128), 0)).astype(F32)
            delta = lax.dot_general(
                ones,
                product,
                (((1,), (1,)), ((), ())),
                precision=lax.Precision.HIGHEST,
                preferred_element_type=F32,
            )
            sum_q = jnp.zeros((128, BLOCK), F32)
            for head in range(2):
                number = pair * 2 + head
                slope = slopes[number]
                query = halves(nat[block(i), lanes], head) * scale
                grad_head = halves(grad_rows, head)
                row_lse = lse[number : number + 1, block(i)]
                row_delta = delta[head : head + 1, :]
                for j in range(i + 1):
                    keys = nat[block(j), k_lanes]
                    tile, seen = masked_scores(keys, query, i, j, slope, offsets[...], length)
                    probs = jnp.exp(tile - row_lse)
                    if seen is not None:
                        probs = jnp.where(seen, probs, 0.0)
                    grad_probs = nt(nat[block(j), v_lanes], grad_head)
                    grad_scores = (probs * (grad_probs - row_delta)).astype(BF)
                    grad_v[block(j), lanes] += nn(probs.astype(BF), grad_head)
                    grad_k[block(j), lanes] += nn(grad_scores, query)
                    sum_q = sum_q + tn(halves(keys, head), grad_scores)
            grad_q[block(i), lanes] = (jnp.transpose(sum_q) * HEAD_DIM**-0.5).astype(BF)
    sums[...] = jnp.zeros_like(sums)
    for j in range(4):
        place = pl.ds(pl.multiple_of((run ^ j) * BLOCK, BLOCK), BLOCK)
        out[block(j), :mine] = grad_q[place, :]
        out[block(j), mine : 2 * mine] = grad_k[place, :].astype(BF)
        out[block(j), 2 * mine :] = grad_v[place, :].astype(BF)
        rows = out[block(j), :]
        sums[0:1, :] += jnp.sum(rows.astype(F32), axis=0, keepdims=True)
        partial = nt(rows, w_qkv[...])
        if j == 0:
            near_keep[...] = partial
        elif j == 1:
            near_send[...] = partial.astype(BF)
        elif j == 2:
            far_keep[...] = partial
        else:
            far_send[...] = partial.astype(BF)


def attend(blocks, w_qkv, bias, scalars, slopes):
    rows, width = blocks[0].shape
    columns = w_qkv.width
    mine = columns // 3
    outs = [
        ((4 * rows, columns), BF),
        ((4 * rows, mine), F32),
        ((rows, mine), BF),
        ((rows, mine), BF),
        ((rows, mine), BF),
        ((rows, mine), BF),
        ((8, 4 * rows), F32),
    ]
    scratch = [
        pltpu.VMEM((4, rows, mine), BF),
        pltpu.VMEM((4 * rows, BLOCK), F32),
        pltpu.VMEM((BLOCK, BLOCK), F32),
    ]
    inputs = (scalars, slopes, *blocks, w_qkv, bias)
    specs = [SMEM, SMEM] + [VMEM] * 6
    return kernel_call(attend_kernel, "attend", inputs, outs, scratch, specs, stored=(0, 1))


def attend_back(nat, parts, att, lse, w_qkv, scalars, slopes):
    total, columns = nat.shape
    rows, mine = total // 4, columns // 3
    width = w_qkv.rows * lax.axis_size("fsdp")
    outs = [
        ((total, columns), BF),
        ((rows, width), F32),
        ((rows, width), BF),
        ((rows, width), F32),
        ((rows, width), BF),
        ((8, columns), F32),
    ]
    scratch = [
        pltpu.VMEM((total, mine), BF),
        pltpu.VMEM((total, mine), BF),
        pltpu.VMEM((total, mine), F32),
        pltpu.VMEM((total, mine), F32),
        pltpu.VMEM((BLOCK, BLOCK), F32),
    ]
    inputs = (scalars, slopes, nat, *parts, att, lse, w_qkv)
    specs = [SMEM, SMEM] + [VMEM] * 8
    return kernel_call(attend_back_kernel, "attend_back", inputs, outs, scratch, specs)


def shards(
    tokens,
    lengths,
    cotangent,
    ln1_gain,
    ln1_bias,
    qkv_weight,
    query_bias,
    value_bias,
    out_weight,
    out_bias,
    ln2_gain,
    ln2_bias,
    up_weight,
    up_bias,
    down_weight,
    down_bias,
):
    GRANT[0] = 24
    fsdp = lax.axis_size("fsdp")
    run = lax.axis_index("seq")
    rows, width = tokens.shape[1:]
    hidden = up_weight.shape[2]
    heads = HEADS // 4
    mine = width // 4
    half = width // 2
    ffn_size = hidden // 4
    part = width // fsdp
    piece = hidden // fsdp // 4
    me = lax.axis_index("fsdp")
    scalars = jnp.stack([run.astype(jnp.int32), lengths[0]])
    place = jnp.stack([run, me % 2]).astype(jnp.int32)
    slopes = lax.dynamic_slice_in_dim(head_slopes(), run * heads, heads)

    def quarter(value, axis):
        size = value.shape[axis] // 4
        return lax.dynamic_slice_in_dim(value, run * size, size, axis)

    def core_half(value, axis):
        return lax.dynamic_slice_in_dim(value, (run % 2) * half, half, axis)

    def qkv_of(layer):
        return quarter(qkv_weight[layer].reshape(part, 3, width), 2).reshape(part, 3 * mine)

    def out_of(layer):
        return core_half(out_weight[layer], 1)

    def up_of(layer):
        return quarter(up_weight[layer].reshape(part, fsdp, -1), 2).reshape(part, ffn_size)

    def down_of(layer):
        return quarter(down_weight[layer], 0)

    def seq_blocks(own):
        across = y_swap(own)
        return [own, core_swap(own), across, core_swap(across)]

    def summed(near, far):
        far = far_sum(far)
        return near[0], core_swap(near[1]), y_swap(far)

    def far_sum(far):
        return (far[0] + core_swap(far[1]).astype(F32)).astype(BF)

    vectors = (ln1_gain, ln1_bias, query_bias, value_bias, out_bias, ln2_gain, ln2_bias, down_bias)
    small = jnp.concatenate([jnp.stack(vectors, 1).reshape(LAYERS, -1), up_bias], axis=1)
    columns = 3 * mine
    extra = small.size // columns
    small = jnp.pad(small.reshape(extra, columns), ((0, -extra % 16), (0, 0)))
    stride = part + small.shape[0]
    own = pack(["qkv", "small"], [qkv_weight, small], 0, place, stride, columns)
    token_blocks = seq_blocks(tokens[0])
    even = [own] + [hop(own, "fsdp", 2 * k) for k in range(1, fsdp // 2 - 1)]
    even.append(hop(tied(own, even[1]), "fsdp", fsdp - 2))
    first = jnp.concatenate(even)
    first = (first, x_swap(first))
    cot_blocks = seq_blocks(cotangent[0])
    token_blocks, cot_blocks, first = meet(token_blocks, cot_blocks, first)
    arrays = dict(qkv=qkv_weight, out=out_weight, up=up_weight, down=down_weight)
    sizes = dict(qkv=columns, out=half, up=ffn_size, down=width)

    def bundle(layer, names):
        if part % 128:
            parts = dict(qkv=qkv_of, out=out_of, up=up_of, down=down_of)
            return jnp.concatenate([parts[name](layer) for name in names], axis=1)
        total = sum(sizes[name] for name in names)
        return pack(names, [arrays[name] for name in names], layer, place, part, total)

    packs = [
        bundle(0, ["out", "up"]),
        bundle(0, ["down"]),
        bundle(1, ["qkv", "out"]),
        bundle(1, ["up"]),
        bundle(1, ["down"]),
    ]
    keys = jnp.stack([me, me % 2]).astype(jnp.int32)
    early_one, late_one, early_two, up_two, down_two = (gather_z(item) for item in packs)

    def matrix(halves, column, size, key=1):
        return Slots(halves, column, size, part, keys, key)

    def out_matrices(halves, column):
        own = assemble(halves, column, half, part, me % 2)
        return own, core_swap(own)

    small = [item.reshape(fsdp // 2, stride, columns)[:, part : part + extra] for item in first]
    small = jnp.stack(small, 1).reshape(fsdp, LAYERS, -1)
    small = jnp.take(small, me ^ jnp.arange(fsdp), axis=0).astype(F32)
    tables, biases = [], []
    for layer in range(LAYERS):
        table = small[:, layer, : 8 * part].reshape(fsdp, 8, part)
        table = jnp.transpose(table, (1, 0, 2)).reshape(8, width)
        bias_q, bias_v = quarter(table[BIAS_Q], 0), quarter(table[BIAS_V], 0)
        bias_qkv = jnp.concatenate([bias_q, jnp.zeros_like(bias_q), bias_v])
        bias_up = quarter(small[:, layer, 8 * part :], 1)
        tables.append(table)
        biases.append((bias_qkv.reshape(1, -1), bias_up.reshape(1, -1)))

    stream = tokens[0].astype(F32)
    token_blocks, tables, biases = meet(token_blocks, tables, biases)
    h1 = first_norm(token_blocks, tables[0])
    w_qkv = matrix(first, 0, columns, 0)
    out_one, up_one = early_one[:, :half], early_one[:, half:]
    moved_out, moved = x_swap(out_one), x_swap(up_one)
    saved, weights = [], []
    for layer in range(LAYERS):
        top = layer + 1 == LAYERS
        bias_qkv, bias_up = biases[layer]
        packed, attended, *low, lse = attend(h1, w_qkv, bias_qkv, scalars, slopes)
        if top:
            w_outs = out_matrices(early_two, columns)
        else:
            low, moved_out = meet(low, moved_out)
            w_outs = out_matrices((out_one, moved_out), 0)
        far = y_swap(low[3])
        across = y_swap(low[2])
        if not top:
            across, far, moved, late_one = meet(across, far, moved, late_one)
            moved_late = x_swap(late_one)
        parts = [low[0], core_swap(low[1]), across, core_swap(far)]
        middle, normed, att_own = out_step(scalars, parts, w_outs, stream, tables[layer])
        h2 = seq_blocks(normed)
        if top:
            middle, moved_late = meet(middle, moved_late)
            w_up = matrix((up_two, moved_up), 0, ffn_size)
            w_down = matrix((down_two, moved_late), 0, width)
            near = ffn(h2[0], h2[1], w_up, bias_up, w_down)
            near_back = ffn_back(cot_blocks[0], cot_blocks[1], near[1], w_up, w_down)
            h2[2], near, near_back = meet(h2[2], near, near_back)
            h2[3] = core_swap(h2[2])
        else:
            h2[2], moved_late, early_two = meet(h2[2], moved_late, early_two)
            h2[3] = core_swap(h2[2])
            w_up = matrix((up_one, moved), 0, ffn_size)
            w_down = matrix((late_one, moved_late), 0, width)
            moved = x_swap(early_two)
            near = ffn(h2[0], h2[1], w_up, bias_up, w_down)
        far = ffn(h2[2], h2[3], w_up, bias_up, w_down)
        saved.append((stream, h1, packed, attended, lse, att_own, middle, h2, near[:2], far[:2]))
        weights.append((w_qkv, w_outs, w_up, w_down))
        if top:
            last_sums = near[2:], far[2:]
        else:
            sums, moved, up_two = meet(summed(near[2:], far[2:]), moved, up_two)
            early_two = (early_two, moved)
            w_qkv = matrix(early_two, 0, columns)
            moved_up = x_swap(up_two)
            stream, normed = layer_end(middle, sums, tables[layer], tables[layer + 1])
            h1 = seq_blocks(normed)
            h1[2], moved_up, down_two = meet(h1[2], moved_up, down_two)
            h1[3] = core_swap(h1[2])
            moved_late = x_swap(down_two)

    grad = cotangent[0].astype(F32)
    g_down = cot_blocks
    vectors = [None] * LAYERS
    upper, lower = [], []
    for layer in reversed(range(LAYERS)):
        top = layer + 1 == LAYERS
        totals = upper if top else lower
        GRANT[0] = 24 if top else 48
        w_qkv, w_outs, w_up, w_down = weights[layer]
        stream, h1, packed, attended, lse, att_own, middle, h2, act_near, act_far = saved[layer]
        if top:
            near = near_back
        else:
            near = ffn_back(g_down[0], g_down[1], act_near[1], w_up, w_down)
            g_down[2], near, late, moved_above = meet(g_down[2], near, late, moved_above)
            g_down[3] = core_swap(g_down[2])
            moved_late = x_swap(late[1])
        far = ffn_back(g_down[2], g_down[3], act_far[1], w_up, w_down)
        far_low = far_sum(far[1:3])
        acts, h2, far_low = meet([act_near[0], act_far[0]], h2, far_low)
        if not top:
            far_low, up_above = meet(far_low, up_above)
            reduced = added(up_above, moved_above)
            upper.append(scatter_z(reduced))
        sums = near[1], core_swap(near[2]), y_swap(far_low)
        if top:
            size = width * 3 // 4
            sent_down = weight_grad(acts, g_down, place, (size, width - size))
            size = ffn_size * 3 // 8
            sent_up = weight_grad(h2, [near[0], far[0]], place, (size, ffn_size - size))
            pair = zip(sent_down[2:], sent_up[:2])
            sent_both = [jnp.concatenate(item, axis=1) for item in pair]
            sent_down, sent_up = sent_down[:2], sent_up[2:]
            moved_both = x_swap(sent_both[1])
            sums, sent_both[0] = meet(sums, sent_both[0])
        else:
            sent_down = weight_grad(acts, g_down, place)
            sent_up = weight_grad(h2, [near[0], far[0]], place)
        moved_down, moved_up = x_swap(sent_down[1]), x_swap(sent_up[1])
        sums, sent_down[0], sent_up[0] = meet(sums, sent_down[0], sent_up[0])
        grad_middle, g_branch, *g_att, lines_two = out_back(
            scalars, sums, middle, grad, tables[layer], w_outs
        )
        g_att = [
            g_att[0],
            core_swap(g_att[1]),
            y_swap(g_att[2]),
            y_swap(core_swap(g_att[3])),
        ]
        if not top:
            g_att, moved_late = meet(g_att, moved_late)
            reduced = added(late[0], moved_late)
            g_att, reduced, upper[:2] = meet(g_att, reduced, upper[:2])
            upper.append(scatter_z(reduced))
        if top:
            g_att, last_sums = meet(g_att, last_sums)
        keep, send = out_grad(att_own, g_branch, place)
        send = core_swap(send)
        g_packed, *parts, packed_sum = attend_back(
            packed, g_att, attended, lse, w_qkv, scalars, slopes
        )
        if top:
            last_sums = summed(*last_sums)
            parts, moved_down, last_sums, send = meet(parts, moved_down, last_sums, send)
            result = layer_end(saved[layer][6], last_sums, tables[layer], None)[1]
        else:
            parts, moved_down, send = meet(parts, moved_down, send)
        far_low = far_sum(parts[2:])
        h1, sent_down[0], far_low = meet(h1, sent_down[0], far_low)
        sent_qkv = weight_grad(h1, [g_packed], place)
        sums = parts[0], core_swap(parts[1]), y_swap(far_low)
        reduced = added(sent_down[0], moved_down)
        totals.append(scatter_z(reduced))
        sums, reduced, sent_qkv[0] = meet(sums, reduced, sent_qkv[0])
        if top:
            sums, moved_both = meet(sums, moved_both)
        else:
            sums, moved_up = meet(sums, moved_up)
            reduced = added(sent_up[0], moved_up)
            totals.append(scatter_z(reduced))
            sent_out = added_pair(keep, send)
            late = [jnp.concatenate(pair, axis=1) for pair in zip(sent_qkv, sent_out)]
            sums, upper[2:], late[0] = meet(sums, upper[2:], late[0])
            one, two, three, last_piece = upper
            size = width // 4
            upper = [
                jnp.concatenate([one, two[:, :size]], axis=1),
                jnp.concatenate([two[:, size:], three], axis=1),
                last_piece,
            ]
        up_sum = near[3] + far[3]
        grad, normed, lines_one = layer_begin(sums, stream, grad_middle, tables[layer])
        if layer:
            normed, sent_both[0], sent_up[0], keep = meet(
                normed, sent_both[0], sent_up[0], keep
            )
            upper.append(scatter_z(added(sent_both[0], moved_both)))
            g_down = seq_blocks(normed)
            up_above, moved_above = sent_up[0], moved_up
        else:
            grad, totals[0] = meet(grad, totals[0])
        if layer:
            sent_out = added_pair(keep, send)
            late = [jnp.concatenate(pair, axis=1) for pair in zip(sent_qkv, sent_out)]
        else:
            upper = [four(item) for item in upper]
            totals[0] = four(totals[0])
            last, upper, totals = meet(added(late[0], x_swap(late[1])), upper, totals)
            lower = totals + [scatter_z(last)]

        vectors[layer] = (lines_two, lines_two, packed_sum, lines_one, up_sum)

    def spread(value, axis=0):
        shape = list(value.shape)
        size = shape[axis]
        shape[axis] = 4 * size
        return lax.dynamic_update_slice_in_dim(jnp.zeros(shape, F32), value, run * size, axis)

    small_sums = []
    vectors, grad = meet(vectors, grad)
    for _, lines_two, packed_sum, lines_one, up_sum in vectors:
        members = [
            lines_one[0],
            lines_one[1],
            spread(packed_sum[0, :mine]),
            spread(packed_sum[0, 2 * mine :]),
            lines_two[2],
            lines_two[0],
            lines_two[1],
            lines_two[3],
        ]
        small_sums.append(
            jnp.concatenate(
                [item.reshape(fsdp, part) for item in members]
                + [spread(up_sum.reshape(fsdp, piece), 1)],
                axis=1,
            )
        )

    starts = ((2, 0), (2, columns), (1, 0), (0, 0))
    names = ("qkv", "out", "up", "down")
    matrices = finish(1, LAYERS, upper, starts, place, None, names)
    vector = sum_small(jnp.stack(small_sums, axis=1))
    middle, vector, result = meet(four(lower[1]), vector, result)
    groups = [lower[0], middle]
    ffn_grads = finish(0, LAYERS, groups, starts, place, list(matrices[2:]), names[2:])
    last, ffn_grads, matrices, vector = meet(lower[2], ffn_grads, matrices[:2], vector)
    starts = ((0, 0), (0, columns), (0, 0), (0, 0))
    matrices = finish(0, LAYERS, [four(last)], starts, place, list(matrices), names[:2])
    grad_qkv_w, grad_out_w = matrices
    grad_up_w, grad_down_w = ffn_grads
    if piece % 128:
        grad_up_w = grad_up_w.reshape(LAYERS, part, 4, fsdp, piece)
        grad_up_w = jnp.swapaxes(grad_up_w, 2, 3).reshape(LAYERS, part, hidden)
    lines = [vector[:, i * part : (i + 1) * part] for i in range(8)]
    gain_one, shift_one, bias_q, bias_v, bias_o, gain_two, shift_two, bias_down = lines
    return (
        result[None],
        grad[None],
        gain_one,
        shift_one,
        grad_qkv_w,
        bias_q,
        bias_v,
        grad_out_w,
        bias_o,
        gain_two,
        shift_two,
        grad_up_w,
        vector[:, 8 * part :],
        grad_down_w,
        bias_down,
    )


def solution(mesh):
    vector = P(None, "fsdp")
    matrix = P(None, "fsdp", None)
    data = P("fsdp", "seq", None)
    weight_specs = (
        vector,
        vector,
        matrix,
        vector,
        vector,
        matrix,
        vector,
        vector,
        vector,
        matrix,
        vector,
        matrix,
        vector,
    )
    in_specs = (data, P("fsdp"), data) + weight_specs
    out_specs = (data, data) + weight_specs
    return jax.shard_map(shards, mesh=mesh, in_specs=in_specs, out_specs=out_specs, check_vma=False)
```
